256 devices in a mesh: loop: 32 (over x, y, z_hi), team: 8 (over z_lo, core).
Axes of the slice: x: 4, y: 4, z: 8 (z_hi: 2, z_lo: 4; z = z_hi * 4 + z_lo), core: 2. Of those that a mesh axis runs over, the one named last changes fastest.
Arguments:
- features: bfloat16 [32768, 256], P(('loop', 'team')), may hold values from -6 to 6
- weight: bfloat16 [256, 256], replicated, may hold values from -0.375 to 0.375
- bias: float32 [256], replicated, may hold values from -1 to 1
- node_scale: float32 [32768], P(('loop', 'team')), may hold values from 0.1 to 1
- cotangent: bfloat16 [32768, 256], P(('loop', 'team')), may hold values from -6 to 6
- edge_slot: int32 [32, 8, 32, 96], P('loop', 'team'), may hold values from 0 to 4, as said below
- edge_row: int32 [32, 8, 32, 96], P('loop', 'team'), may hold values from 0 to 127
- edge_col: int32 [32, 8, 32, 96], P('loop', 'team'), may hold values from 0 to 127
- tile_row: int32 [32, 8, 32, 4], P('loop', 'team'), may hold values from 0 to 7
Outputs:
- output: bfloat16 [32768, 256], P(('loop', 'team'))
- feature_grad: bfloat16 [32768, 256], P(('loop', 'team'))
- weight_grad: float32 [256, 256], replicated
- bias_grad: float32 [256], replicated
The draws below stay inside these ranges and needn't reach their ends.
Inputs may be any that keep to these rules, and one draw needn't show every extreme that they name: `edge_slot`: unused edge slots hold 4 and come after the used ones of each column block; in every device's lists one column block has all 96 edge slots used and another only its first one. Repeated edges count with their multiplicity.
All inputs are finite; a program needn't handle non-finite values.
Results may differ from the reference program's by a relative error of at most 0.01.
Values may be sent and summed in bfloat16 or wider, within the bound.
No kernel may reach another device: no remote copies, remote signals or barrier semaphores. Data moves between devices by JAX's collectives and lax.ppermute only.
A program may use at most 64 MiB of HBM per device.

```python
import math
from functools import partial
import jax
import jax.numpy as jnp
from jax import lax

F = 256
TILE = 128
SLOTS = 4
EDGES_BLK = 96
LOOPS = 32
TEAMS = 8
BLOCK = 1024
NODES = 32768


def draw_edge_slot(key, part):
    key = jax.random.fold_in(key, 11)
    first_key, second_key, third_key = jax.random.split(key, 3)
    counts = jax.random.randint(first_key, (LOOPS, TEAMS, LOOPS), 1, EDGES_BLK + 1)
    filled = jax.random.randint(second_key, (LOOPS, TEAMS, 1), 0, LOOPS)
    column_ids = jnp.arange(LOOPS)[None, None, :]
    counts = jnp.where(column_ids == filled, EDGES_BLK, jnp.where(column_ids == (filled + 1) % LOOPS, 1, counts))
    slots = jax.random.randint(third_key, (LOOPS, TEAMS, LOOPS, EDGES_BLK), 0, SLOTS)
    position = jnp.arange(EDGES_BLK)[None, None, None, :]
    return jnp.where(position < counts[..., None], slots, SLOTS).astype(jnp.int32)


def plant(result, stream_key, low, largest):
    index_at = [jax.random.randint(jax.random.fold_in(stream_key, axis), (), 0, length) for axis, length in enumerate(result.shape)]
    widest = result.shape.index(max(result.shape))
    neighbour = index_at[:widest] + [(index_at[widest] + 1) % result.shape[widest]] + index_at[widest + 1:]
    return result.at[tuple(index_at)].set(low).at[tuple(neighbour)].set(largest)


def block_levels(stream_key, dims, cuts, low, top_value):
    level, own = 1.0, jax.random.fold_in(stream_key, 6)
    for axis_at, blocks in cuts:
        draws = jnp.exp(jax.random.uniform(jax.random.fold_in(own, axis_at), (blocks,), jnp.float32, low / len(cuts), top_value / len(cuts)))
        level = level * jnp.repeat(draws, dims[axis_at] // blocks).reshape([-1 if axis == axis_at else 1 for axis in range(len(dims))])
    return level


def bell_draw(own_key, extent, width, limit, cuts=(), kind=jnp.bfloat16):
    result = width * jax.random.normal(own_key, extent, jnp.float32)
    if cuts:
        result = result * block_levels(own_key, extent, cuts, -0.22, 0.18)
    return jnp.clip(result, -limit, limit).astype(kind)


def setup_inputs(seed: int = 0) -> dict:
    arg_keys = jax.random.split(jax.random.key(seed), 10)
    features = bell_draw(arg_keys[0], (NODES, F), 1.0, 6.0, ((0, 256),))
    weight = bell_draw(arg_keys[1], (F, F), F ** -0.5, 0.375)
    bias = jnp.clip(jax.random.uniform(arg_keys[2], (F,), jnp.float32, -1.0, 1.0), -1.0, 1.0)
    node_scale = jnp.clip(jnp.exp(math.log(1.0) - 2.3025851 * jax.random.uniform(arg_keys[3], (NODES,), jnp.float32) ** block_levels(arg_keys[3], (NODES,), ((0, 256),), -0.2, 0.2)), 0.1, 1.0)
    cotangent = bell_draw(arg_keys[4], (NODES, F), 1.0, 6.0, ((0, 256),))
    edge_slot = draw_edge_slot(jax.random.fold_in(arg_keys[9], 71), 0)
    edge_row = plant(jax.random.randint(arg_keys[6], (LOOPS, TEAMS, LOOPS, EDGES_BLK), 0, TILE), jax.random.fold_in(arg_keys[6], 1), 0, TILE - 1).astype(jnp.int32)
    edge_col = plant(jax.random.randint(arg_keys[7], (LOOPS, TEAMS, LOOPS, EDGES_BLK), 0, TILE), jax.random.fold_in(arg_keys[7], 1), 0, TILE - 1).astype(jnp.int32)
    tile_row = plant(jax.random.randint(arg_keys[8], (LOOPS, TEAMS, LOOPS, SLOTS), 0, TEAMS), jax.random.fold_in(arg_keys[8], 1), 0, TEAMS - 1).astype(jnp.int32)
    return dict(features=features, weight=weight, bias=bias, node_scale=node_scale, cotangent=cotangent, edge_slot=edge_slot, edge_row=edge_row, edge_col=edge_col, tile_row=tile_row)


def activation_grad(preact, upstream):
    return jax.vjp(partial(jax.nn.gelu, approximate=True), preact)[1](upstream)[0]

def edge_targets(edge_slot, edge_row, edge_col, tile_row):
    active = (edge_slot < SLOTS).astype(jnp.float32)
    clamped = jnp.minimum(edge_slot, SLOTS - 1).astype(jnp.int32)
    row_tile = jnp.take_along_axis(tile_row, clamped, axis=3)
    team_ids = jnp.arange(TEAMS, dtype=jnp.int32)[None, :, None, None]
    column_ids = jnp.arange(LOOPS, dtype=jnp.int32)[None, None, :, None]
    local_target = (row_tile * TILE + edge_row).astype(jnp.int32)
    source = ((column_ids * TEAMS + team_ids) * TILE + edge_col).astype(jnp.int32)
    return (local_target, source, active)

def reference(features, weight, bias, node_scale, cotangent, edge_slot, edge_row, edge_col, tile_row):
    product = jnp.dot(features, weight, preferred_element_type=jnp.float32)
    scaled = (node_scale[:, None] * product).astype(jnp.bfloat16)
    scaled_wide = scaled.astype(jnp.float32)
    local_target, source, active = edge_targets(edge_slot, edge_row, edge_col, tile_row)

    def forward_block(inputs):
        targets, sources, weights = inputs
        values = scaled_wide[sources.reshape(-1)] * weights.reshape(-1)[:, None]
        return jax.ops.segment_sum(values, targets.reshape(-1), num_segments=BLOCK)
    edge_total = lax.map(forward_block, (local_target, source, active)).reshape(NODES, F)
    preact = node_scale[:, None] * (edge_total + scaled_wide) + bias
    output = jax.nn.gelu(preact, approximate=True).astype(jnp.bfloat16)
    grad_act = activation_grad(preact, cotangent.astype(jnp.float32))
    grad_scaled = (node_scale[:, None] * grad_act).astype(jnp.bfloat16)
    grad_wide = grad_scaled.astype(jnp.float32)
    block_ids = jnp.arange(LOOPS, dtype=jnp.int32)[:, None, None, None]
    global_target = (local_target + block_ids * BLOCK).astype(jnp.int32)

    def backward_block(totals, inputs):
        targets, sources, weights = inputs
        values = grad_wide[targets.reshape(-1)] * weights.reshape(-1)[:, None]
        return (totals + jax.ops.segment_sum(values, sources.reshape(-1), num_segments=NODES), None)
    back_total, unused = lax.scan(backward_block, jnp.zeros((NODES, F), jnp.float32), (global_target, source, active))
    grad_xw = (node_scale[:, None] * (back_total + grad_wide)).astype(jnp.bfloat16)
    feature_grad = lax.dot_general(grad_xw, weight, (((1,), (1,)), ((), ())), preferred_element_type=jnp.float32).astype(jnp.bfloat16)
    factor = 1.0 / math.sqrt(NODES)
    weight_grad = lax.dot_general(features, grad_xw, (((0,), (0,)), ((), ())), preferred_element_type=jnp.float32) * factor
    bias_grad = lax.optimization_barrier(jnp.sum(grad_act, axis=0)) * factor
    return (output, feature_grad, weight_grad, bias_grad)
```

```python
import math

import jax
import jax.numpy as jnp
from jax import lax
from jax.experimental import pallas as pl
from jax.experimental.pallas import tpu as pltpu
from jax.sharding import Mesh, PartitionSpec as P

X, Y, H, L, C = 4, 4, 2, 4, 2
XY, ZN = X * Y, H * L
TILE, F, SLOTS, EDGES = 128, 256, 4, 96
HALF = L * TILE
ROWS = C * HALF
E_ALL = XY * EDGES
WZ, WC, BB = F // ZN, F // (ZN * C), 16
ZCHUNK = TILE + WZ + BB
XCHUNK = TILE + WC + BB
F32, BF16, I32 = jnp.float32, jnp.bfloat16, jnp.int32
K0, K1 = math.sqrt(2.0 / math.pi), 0.044715
ALL = ("x", "y", "h", "l", "c")
PARAMS = pltpu.CompilerParams(vmem_limit_bytes=40 * 1024 * 1024)


def dot(a, b):
    return jnp.dot(a, b, preferred_element_type=F32)


def one_hot(index, shape, axis, base=0):
    return (index == lax.broadcasted_iota(I32, shape, axis) + base).astype(F32).astype(BF16)


def split_rows(row):
    high = row.astype(BF16).astype(F32)
    at = lax.broadcasted_iota(I32, (BB, F), 0)
    return jnp.where(at == 0, high, jnp.where(at == 1, row - high, 0.0)).astype(BF16)


def forward_kernel(x_ref, lane_ref, sub_ref, mine_ref, send_ref, gathered):
    for b in range(H):
        for j in range(XY):
            rows = pl.ds(j * EDGES, EDGES)
            pick = one_hot(sub_ref[rows, H + b : H + b + 1], (EDGES, TILE), 1)
            gathered[b, rows, :] = dot(pick, x_ref[j]).astype(BF16)
    step = 256
    for b in range(H):
        for m in range(ROWS // step):
            place = one_hot(lane_ref[b : b + 1, :], (step, E_ALL), 0, m * step)
            total = dot(place, gathered[b])
            if m * step < HALF:
                mine_ref[b, pl.ds(m * step, step), :] = total
            else:
                send_ref[b, pl.ds(m * step - HALF, step), :] = total.astype(BF16)


def middle_kernel(part_ref, x_ref, s_ref, w_ref, bias_ref, ct_ref, out_ref, g_ref, pay_ref):
    s = s_ref[...]
    z = s * x_ref[...].astype(F32)
    for k in range(ZN):
        z += part_ref[k].astype(F32)
    z_high = z.astype(BF16)
    z_low = (z - z_high.astype(F32)).astype(BF16)
    w = w_ref[...]
    p = s * (dot(z_high, w) + dot(z_low, w)) + bias_ref[...]
    square = p * p
    th = jnp.tanh(K0 * (p + K1 * (p * square)))
    out_ref[...] = (0.5 * p * (1.0 + th)).astype(BF16)
    slope = 0.5 * (1.0 + th) + 0.5 * p * (1.0 - th * th) * (K0 * (1.0 + 3.0 * K1 * square))
    grad = ct_ref[...].astype(F32) * slope
    g = (s * grad).astype(BF16)
    g_ref[...] = g
    first = (((0,), (0,)), ((), ()))
    wg = lax.dot_general(z_high, g, first, preferred_element_type=F32)
    wg += lax.dot_general(z_low, g, first, preferred_element_type=F32)
    bias_rows = split_rows(jnp.sum(grad, axis=0, keepdims=True))
    for k in range(ZN):
        pay_ref[k, pl.ds(0, TILE), :] = g
        pay_ref[k, pl.ds(TILE, WZ), :] = wg[k * WZ : (k + 1) * WZ].astype(BF16)
        pay_ref[k, pl.ds(TILE + WZ, BB), :] = bias_rows


def backward_kernel(core_ref, mine_ref, other_ref, sub_ref, col_ref, pay_ref, grads, picked):
    for b in range(H):
        for k in range(L):
            grads[b, pl.ds(k * TILE, TILE), :] = mine_ref[b * L + k, pl.ds(0, TILE), :]
            grads[b, pl.ds(HALF + k * TILE, TILE), :] = other_ref[b * L + k, pl.ds(0, TILE), :]
    wg = jnp.zeros((WZ, F), F32)
    bias_mine = jnp.zeros((BB, F), F32)
    bias_other = jnp.zeros((BB, F), F32)
    for k in range(ZN):
        rows = pl.ds(TILE, WZ)
        wg += mine_ref[k, rows, :].astype(F32) + other_ref[k, rows, :].astype(F32)
        rows = pl.ds(TILE + WZ, BB)
        bias_mine += mine_ref[k, rows, :].astype(F32)
        bias_other += other_ref[k, rows, :].astype(F32)
    bias_rows = split_rows(jnp.sum(bias_mine + bias_other, axis=0, keepdims=True))
    own = jnp.where(core_ref[0] == 0, wg[:WC], wg[WC:]).astype(BF16)
    step = 256
    for b in range(H):
        for m in range(E_ALL // step):
            rows = pl.ds(m * step, step)
            pick = one_hot(sub_ref[rows, b : b + 1], (step, ROWS), 1)
            picked[b, rows, :] = dot(pick, grads[b]).astype(BF16)
    for j in range(XY):
        total = jnp.zeros((TILE, F), F32)
        for b in range(H):
            at = b * XY + j
            place = one_hot(col_ref[at : at + 1, :], (TILE, EDGES), 0)
            total += dot(place, picked[b, pl.ds(j * EDGES, EDGES), :])
        pay_ref[j, pl.ds(0, TILE), :] = total.astype(BF16)
        pay_ref[j, pl.ds(TILE, WC), :] = own
        pay_ref[j, pl.ds(TILE + WC, BB), :] = bias_rows


def final_kernel(part_ref, g_ref, s_ref, w_ref, fg_ref, wrow_ref, bias_ref):
    factor = 1.0 / math.sqrt(XY * ZN * C * TILE)
    back = g_ref[...].astype(F32)
    tail = jnp.zeros((WC + BB, F), F32)
    for k in range(XY):
        back += part_ref[k, pl.ds(0, TILE), :].astype(F32)
        tail += part_ref[k, pl.ds(TILE, WC + BB), :].astype(F32)
    grad_xw = (s_ref[...] * back).astype(BF16)
    fg_ref[...] = lax.dot_general(
        grad_xw, w_ref[...], (((1,), (1,)), ((), ())), preferred_element_type=F32
    ).astype(BF16)
    wrow_ref[...] = tail[:WC] * factor
    bias_ref[...] = jnp.sum(tail[WC:], axis=0, keepdims=True) * factor


def call(kernel, outs, scratch=(), smem=0):
    def run(*args):
        specs = [
            pl.BlockSpec(memory_space=pltpu.SMEM if k < smem else pltpu.VMEM)
            for k in range(len(args))
        ]
        return pl.pallas_call(
            kernel,
            out_shape=[jax.ShapeDtypeStruct(shape, dtype) for shape, dtype in outs],
            in_specs=specs,
            out_specs=[pl.BlockSpec(memory_space=pltpu.VMEM)] * len(outs),
            scratch_shapes=[pltpu.VMEM(shape, dtype) for shape, dtype in scratch],
            compiler_params=PARAMS,
        )(*args)

    return run


def exchange(array, axes):
    return lax.all_to_all(array, axes, 0, 0, tiled=True)


def swap(array, axis):
    return lax.ppermute(array, axis, [(0, 1), (1, 0)])


def per_device(
    features, weight, bias, node_scale, cotangent, edge_slot, edge_row, edge_col, tile_row
):
    h, c = lax.axis_index("h"), lax.axis_index("c")
    s = node_scale[:, None]
    bias = bias[None, :]

    slot = edge_slot.reshape(XY * H, EDGES)
    tiles = tile_row.reshape(XY * H, SLOTS)
    tile = sum(jnp.where(slot == k, tiles[:, k : k + 1], 0) for k in range(SLOTS))
    target = ((tile & 1) ^ c) * HALF + (tile >> 1) * TILE + edge_row.reshape(slot.shape)
    target = jnp.where(slot < SLOTS, target, -1)
    edges = jnp.stack([target, edge_col.reshape(slot.shape)]).reshape(2, XY, H, EDGES)
    kept = lax.dynamic_index_in_dim(edges, h, 2, keepdims=False)
    came = swap(lax.dynamic_index_in_dim(edges, 1 - h, 2, keepdims=False), "h")

    scaled = (s * features.astype(F32)).astype(BF16)
    sources = exchange(jnp.broadcast_to(scaled[None], (XY, TILE, F)), ("x", "y"))

    pairs = jnp.stack([jnp.where(h == 0, kept, came), jnp.where(h == 0, came, kept)], axis=1)
    lane = pairs.reshape(2 * H, E_ALL)
    sub = lane.T
    columns = pairs[1].reshape(H * XY, EDGES)

    mine, send = call(
        forward_kernel,
        [((H, HALF, F), F32), ((H, HALF, F), BF16)],
        [((H, E_ALL, F), BF16)],
    )(sources, lane, sub)
    partial = (mine + swap(send, "c").astype(F32)).astype(BF16).reshape(ZN, TILE, F)
    partial = exchange(partial, ("h", "l"))
    output, g, pay = call(
        middle_kernel,
        [((TILE, F), BF16), ((TILE, F), BF16), ((ZN, ZCHUNK, F), BF16)],
    )(partial, features, s, weight, bias, cotangent)
    around = exchange(pay, ("h", "l"))
    other = swap(around, "c")
    (terms,) = call(
        backward_kernel,
        [((XY, XCHUNK, F), BF16)],
        [((H, ROWS, F), BF16), ((H, E_ALL, F), BF16)],
        smem=1,
    )(c.astype(I32)[None], around, other, sub, columns)
    terms = exchange(terms, ("x", "y"))
    feature_grad, w_rows, bias_grad = call(
        final_kernel,
        [((TILE, F), BF16), ((WC, F), F32), ((1, F), F32)],
    )(terms, g, s, weight)
    w_other = swap(w_rows, "c")
    w_pair = jnp.where(
        c == 0, jnp.concatenate([w_rows, w_other]), jnp.concatenate([w_other, w_rows])
    )
    w_grad = exchange(jnp.broadcast_to(w_pair[None], (ZN, WZ, F)), ("h", "l"))
    return output, feature_grad, w_grad.reshape(F, F), bias_grad.reshape(F)


def solution(mesh):
    fine = Mesh(mesh.devices.reshape(X, Y, H, L, C), ALL)
    rows, edges = P(ALL, None), P(("x", "y", "h"), ("l", "c"), None, None)
    return jax.shard_map(
        per_device,
        mesh=fine,
        in_specs=(rows, P(), P(), P(ALL), rows, edges, edges, edges, edges),
        out_specs=(rows, rows, P(), P()),
        check_vma=False,
    )
```

```python
import math

import jax
import jax.numpy as jnp
from jax import lax
from jax.experimental import pallas as pl
from jax.experimental.pallas import tpu as pltpu
from jax.sharding import Mesh, PartitionSpec as P

X, Y, H, L, C = 4, 4, 2, 4, 2
XY, ZN = X * Y, H * L
TILE, F, SLOTS, EDGES = 128, 256, 4, 96
HALF = L * TILE
ROWS = C * HALF
E_ALL = XY * EDGES
WR, BB = F // XY, 16
ZCHUNK = TILE + WR + BB
XCHUNK = TILE + WR
F32, BF16, I32 = jnp.float32, jnp.bfloat16, jnp.int32
K0, K1 = math.sqrt(2.0 / math.pi), 0.044715
ALL = ("x", "y", "h", "l", "c")
PARAMS = pltpu.CompilerParams(vmem_limit_bytes=40 * 1024 * 1024)


def dot(a, b):
    return jnp.dot(a, b, preferred_element_type=F32)


def one_hot(index, shape, axis, base=0):
    return (index == lax.broadcasted_iota(I32, shape, axis) + base).astype(F32).astype(BF16)


def split_rows(row):
    high = row.astype(BF16).astype(F32)
    at = lax.broadcasted_iota(I32, (BB, F), 0)
    return jnp.where(at == 0, high, jnp.where(at == 1, row - high, 0.0)).astype(BF16)


def forward_kernel(x_ref, lane_ref, sub_ref, mine_ref, send_ref, gathered):
    for b in range(H):
        for j in range(XY):
            rows = pl.ds(j * EDGES, EDGES)
            pick = one_hot(sub_ref[rows, H + b : H + b + 1], (EDGES, TILE), 1)
            gathered[b, rows, :] = dot(pick, x_ref[j]).astype(BF16)
    step = 256
    for b in range(H):
        for m in range(ROWS // step):
            place = one_hot(lane_ref[b : b + 1, :], (step, E_ALL), 0, m * step)
            total = dot(place, gathered[b])
            if m * step < HALF:
                mine_ref[b, pl.ds(m * step, step), :] = total
            else:
                send_ref[b, pl.ds(m * step - HALF, step), :] = total.astype(BF16)


def middle_kernel(part_ref, x_ref, s_ref, w_ref, bias_ref, ct_ref, out_ref, g_ref, wp_ref):
    s = s_ref[...]
    z = s * x_ref[...].astype(F32)
    for k in range(ZN):
        z += part_ref[k].astype(F32)
    z_high = z.astype(BF16)
    z_low = (z - z_high.astype(F32)).astype(BF16)
    w = w_ref[...]
    p = s * (dot(z_high, w) + dot(z_low, w)) + bias_ref[...]
    square = p * p
    th = jnp.tanh(K0 * (p + K1 * (p * square)))
    out_ref[...] = (0.5 * p * (1.0 + th)).astype(BF16)
    slope = 0.5 * (1.0 + th) + 0.5 * p * (1.0 - th * th) * (K0 * (1.0 + 3.0 * K1 * square))
    grad = ct_ref[...].astype(F32) * slope
    g = (s * grad).astype(BF16)
    g_ref[...] = g
    first = (((0,), (0,)), ((), ()))
    wg = lax.dot_general(z_high, g, first, preferred_element_type=F32)
    wg += lax.dot_general(z_low, g, first, preferred_element_type=F32)
    bias_rows = split_rows(jnp.sum(grad, axis=0, keepdims=True))
    for k in range(XY):
        wp_ref[k, pl.ds(0, WR), :] = wg[k * WR : (k + 1) * WR].astype(BF16)
        wp_ref[k, pl.ds(WR, BB), :] = bias_rows


def load_kernel(w_ref, g_ref, pay_ref):
    tail = jnp.zeros((WR + BB, F), F32)
    for k in range(XY):
        tail += w_ref[k].astype(F32)
    own = tail[:WR].astype(BF16)
    bias_rows = split_rows(jnp.sum(tail[WR:], axis=0, keepdims=True))
    g = g_ref[...]
    for k in range(ZN):
        pay_ref[k, pl.ds(0, TILE), :] = g
        pay_ref[k, pl.ds(TILE, WR), :] = own
        pay_ref[k, pl.ds(TILE + WR, BB), :] = bias_rows


def backward_kernel(mine_ref, other_ref, sub_ref, col_ref, pay_ref, bias_ref, grads, picked):
    for b in range(H):
        for k in range(L):
            grads[b, pl.ds(k * TILE, TILE), :] = mine_ref[b * L + k, pl.ds(0, TILE), :]
            grads[b, pl.ds(HALF + k * TILE, TILE), :] = other_ref[b * L + k, pl.ds(0, TILE), :]
    factor = 1.0 / math.sqrt(XY * ZN * C * TILE)
    tail_mine = jnp.zeros((WR + BB, F), F32)
    tail_other = jnp.zeros((WR + BB, F), F32)
    for k in range(ZN):
        rows = pl.ds(TILE, WR + BB)
        tail_mine += mine_ref[k, rows, :].astype(F32)
        tail_other += other_ref[k, rows, :].astype(F32)
    tail = (tail_mine + tail_other) * factor
    own = tail[:WR].astype(BF16)
    bias_ref[...] = jnp.sum(tail[WR:], axis=0, keepdims=True)
    step = 256
    for b in range(H):
        for m in range(E_ALL // step):
            rows = pl.ds(m * step, step)
            pick = one_hot(sub_ref[rows, b : b + 1], (step, ROWS), 1)
            picked[b, rows, :] = dot(pick, grads[b]).astype(BF16)
    for j in range(XY):
        total = jnp.zeros((TILE, F), F32)
        for b in range(H):
            at = b * XY + j
            place = one_hot(col_ref[at : at + 1, :], (TILE, EDGES), 0)
            total += dot(place, picked[b, pl.ds(j * EDGES, EDGES), :])
        pay_ref[j, pl.ds(0, TILE), :] = total.astype(BF16)
        pay_ref[j, pl.ds(TILE, WR), :] = own


def final_kernel(part_ref, g_ref, s_ref, w_ref, fg_ref, wg_ref):
    back = g_ref[...].astype(F32)
    for k in range(XY):
        back += part_ref[k, pl.ds(0, TILE), :].astype(F32)
        wg_ref[pl.ds(k * WR, WR), :] = part_ref[k, pl.ds(TILE, WR), :].astype(F32)
    grad_xw = (s_ref[...] * back).astype(BF16)
    fg_ref[...] = lax.dot_general(
        grad_xw, w_ref[...], (((1,), (1,)), ((), ())), preferred_element_type=F32
    ).astype(BF16)


def call(kernel, outs, scratch=()):
    return pl.pallas_call(
        kernel,
        out_shape=[jax.ShapeDtypeStruct(shape, dtype) for shape, dtype in outs],
        out_specs=[pl.BlockSpec(memory_space=pltpu.VMEM)] * len(outs),
        scratch_shapes=[pltpu.VMEM(shape, dtype) for shape, dtype in scratch],
        compiler_params=PARAMS,
    )


def exchange(array, axes):
    return lax.all_to_all(array, axes, 0, 0, tiled=True)


def swap(array, axis):
    return lax.ppermute(array, axis, [(0, 1), (1, 0)])


def per_device(
    features, weight, bias, node_scale, cotangent, edge_slot, edge_row, edge_col, tile_row
):
    h, c = lax.axis_index("h"), lax.axis_index("c")
    s = node_scale[:, None]
    bias = bias[None, :]

    slot = edge_slot.reshape(XY * H, EDGES)
    tiles = tile_row.reshape(XY * H, SLOTS)
    tile = sum(jnp.where(slot == k, tiles[:, k : k + 1], 0) for k in range(SLOTS))
    target = ((tile & 1) ^ c) * HALF + (tile >> 1) * TILE + edge_row.reshape(slot.shape)
    target = jnp.where(slot < SLOTS, target, -1)
    edges = jnp.stack([target, edge_col.reshape(slot.shape)]).reshape(2, XY, H, EDGES)
    kept = lax.dynamic_index_in_dim(edges, h, 2, keepdims=False)
    came = swap(lax.dynamic_index_in_dim(edges, 1 - h, 2, keepdims=False), "h")

    scaled = (s * features.astype(F32)).astype(BF16)
    sources = exchange(jnp.broadcast_to(scaled[None], (XY, TILE, F)), ("x", "y"))

    pairs = jnp.stack([jnp.where(h == 0, kept, came), jnp.where(h == 0, came, kept)], axis=1)
    lane = pairs.reshape(2 * H, E_ALL)
    sub = lane.T
    columns = pairs[1].reshape(H * XY, EDGES)

    mine, send = call(
        forward_kernel,
        [((H, HALF, F), F32), ((H, HALF, F), BF16)],
        [((H, E_ALL, F), BF16)],
    )(sources, lane, sub)
    partial = (mine + swap(send, "c").astype(F32)).astype(BF16).reshape(ZN, TILE, F)
    partial = exchange(partial, ("h", "l"))
    output, g, w_parts = call(
        middle_kernel,
        [((TILE, F), BF16), ((TILE, F), BF16), ((XY, WR + BB, F), BF16)],
    )(partial, features, s, weight, bias, cotangent)
    w_parts = exchange(w_parts, ("x", "y"))
    (pay,) = call(load_kernel, [((ZN, ZCHUNK, F), BF16)])(w_parts, g)
    around = exchange(pay, ("h", "l"))
    other = swap(around, "c")
    terms, bias_grad = call(
        backward_kernel,
        [((XY, XCHUNK, F), BF16), ((1, F), F32)],
        [((H, ROWS, F), BF16), ((H, E_ALL, F), BF16)],
    )(around, other, sub, columns)
    terms = exchange(terms, ("x", "y"))
    feature_grad, weight_grad = call(
        final_kernel, [((TILE, F), BF16), ((F, F), F32)]
    )(terms, g, s, weight)
    return output, feature_grad, weight_grad, bias_grad.reshape(F)


def solution(mesh):
    fine = Mesh(mesh.devices.reshape(X, Y, H, L, C), ALL)
    rows, edges = P(ALL, None), P(("x", "y", "h"), ("l", "c"), None, None)
    return jax.shard_map(
        per_device,
        mesh=fine,
        in_specs=(rows, P(), P(), P(ALL), rows, edges, edges, edges, edges),
        out_specs=(rows, rows, P(), P()),
        check_vma=False,
    )
```

```python
import math

import jax
import jax.numpy as jnp
from jax import lax
from jax.experimental import pallas as pl
from jax.experimental.pallas import tpu as pltpu
from jax.sharding import Mesh, PartitionSpec as P

X, Y, H, L, C = 4, 4, 2, 4, 2
XY, ZN = X * Y, H * L
TILE, F, SLOTS, EDGES = 128, 256, 4, 96
HALF = L * TILE
ROWS = C * HALF
E_ALL = XY * EDGES
STEP = 256
WR, BB = F // XY, 16
ZCHUNK = TILE + WR + BB
XCHUNK = TILE + WR
F32, BF16, I32 = jnp.float32, jnp.bfloat16, jnp.int32
K0, K1 = math.sqrt(2.0 / math.pi), 0.044715
ALL = ("x", "y", "h", "l", "c")
PARAMS = pltpu.CompilerParams(vmem_limit_bytes=40 * 1024 * 1024)


def dot(a, b):
    return jnp.dot(a, b, preferred_element_type=F32)


def one_hot(index, shape, axis, base=0):
    return (index == lax.broadcasted_iota(I32, shape, axis) + base).astype(F32).astype(BF16)


def split_rows(row):
    high = row.astype(BF16).astype(F32)
    at = lax.broadcasted_iota(I32, (BB, F), 0)
    return jnp.where(at == 0, high, jnp.where(at == 1, row - high, 0.0)).astype(BF16)


def spread_kernel(x_ref, s_ref, out_ref):
    scale = jnp.transpose(jnp.broadcast_to(s_ref[...], (TILE, TILE)))
    for k in range(F // TILE):
        part = pl.ds(k * TILE, TILE)
        scaled = (scale * x_ref[:, part].astype(F32)).astype(BF16)
        for j in range(XY):
            out_ref[j, :, part] = scaled


def forward_send_kernel(x_ref, lane_ref, sub_ref, gathered_ref, send_ref):
    for b in range(H):
        for j in range(XY):
            rows = pl.ds(j * EDGES, EDGES)
            pick = one_hot(sub_ref[rows, H + b : H + b + 1], (EDGES, TILE), 1)
            gathered_ref[b, rows, :] = dot(pick, x_ref[j]).astype(BF16)
    for b in range(H):
        for m in range(HALF // STEP):
            place = one_hot(lane_ref[b : b + 1, :], (STEP, E_ALL), 0, HALF + m * STEP)
            send_ref[b, pl.ds(m * STEP, STEP), :] = dot(place, gathered_ref[b]).astype(BF16)


def forward_keep_kernel(gathered_ref, lane_ref, mine_ref):
    for b in range(H):
        for m in range(HALF // STEP):
            place = one_hot(lane_ref[b : b + 1, :], (STEP, E_ALL), 0, m * STEP)
            mine_ref[b, pl.ds(m * STEP, STEP), :] = dot(place, gathered_ref[b])


def add_kernel(mine_ref, other_ref, out_ref):
    out_ref[...] = (mine_ref[...] + other_ref[...].astype(F32)).astype(BF16)


def middle_kernel(part_ref, x_ref, s_ref, w_ref, bias_ref, ct_ref, out_ref, g_ref, wp_ref):
    s = s_ref[...]
    z = s * x_ref[...].astype(F32)
    for k in range(ZN):
        z += part_ref[k].astype(F32)
    z_high = z.astype(BF16)
    z_low = (z - z_high.astype(F32)).astype(BF16)
    w = w_ref[...]
    p = s * (dot(z_high, w) + dot(z_low, w)) + bias_ref[...]
    square = p * p
    th = jnp.tanh(K0 * (p + K1 * (p * square)))
    out_ref[...] = (0.5 * p * (1.0 + th)).astype(BF16)
    slope = 0.5 * (1.0 + th) + 0.5 * p * (1.0 - th * th) * (K0 * (1.0 + 3.0 * K1 * square))
    grad = ct_ref[...].astype(F32) * slope
    g = (s * grad).astype(BF16)
    g_ref[...] = g
    first = (((0,), (0,)), ((), ()))
    wg = lax.dot_general(z_high, g, first, preferred_element_type=F32)
    wg += lax.dot_general(z_low, g, first, preferred_element_type=F32)
    bias_rows = split_rows(jnp.sum(grad, axis=0, keepdims=True))
    for k in range(XY):
        wp_ref[k, pl.ds(0, WR), :] = wg[k * WR : (k + 1) * WR].astype(BF16)
        wp_ref[k, pl.ds(WR, BB), :] = bias_rows


def load_kernel(w_ref, g_ref, pay_ref):
    tail = jnp.zeros((WR + BB, F), F32)
    for k in range(XY):
        tail += w_ref[k].astype(F32)
    own = tail[:WR].astype(BF16)
    bias_rows = split_rows(jnp.sum(tail[WR:], axis=0, keepdims=True))
    g = g_ref[...]
    for k in range(ZN):
        pay_ref[k, pl.ds(0, TILE), :] = g
        pay_ref[k, pl.ds(TILE, WR), :] = own
        pay_ref[k, pl.ds(TILE + WR, BB), :] = bias_rows


def backward_mine_kernel(mine_ref, sub_ref, picked_ref, grads):
    for b in range(H):
        for k in range(L):
            grads[pl.ds(k * TILE, TILE), :] = mine_ref[b * L + k, pl.ds(0, TILE), :]
        for m in range(E_ALL // STEP):
            rows = pl.ds(m * STEP, STEP)
            pick = one_hot(sub_ref[rows, b : b + 1], (STEP, HALF), 1)
            picked_ref[b, rows, :] = dot(pick, grads[...]).astype(BF16)


def backward_kernel(
    picked_ref, mine_ref, other_ref, sub_ref, col_ref, pay_ref, bias_ref, grads, picked
):
    factor = 1.0 / math.sqrt(XY * ZN * C * TILE)
    tail_mine = jnp.zeros((WR + BB, F), F32)
    tail_other = jnp.zeros((WR + BB, F), F32)
    for k in range(ZN):
        rows = pl.ds(TILE, WR + BB)
        tail_mine += mine_ref[k, rows, :].astype(F32)
        tail_other += other_ref[k, rows, :].astype(F32)
    tail = (tail_mine + tail_other) * factor
    own = tail[:WR].astype(BF16)
    bias_ref[...] = jnp.sum(tail[WR:], axis=0, keepdims=True)
    for b in range(H):
        for k in range(L):
            grads[pl.ds(k * TILE, TILE), :] = other_ref[b * L + k, pl.ds(0, TILE), :]
        for m in range(E_ALL // STEP):
            rows = pl.ds(m * STEP, STEP)
            pick = one_hot(sub_ref[rows, b : b + 1], (STEP, HALF), 1, HALF)
            value = dot(pick, grads[...]) + picked_ref[b, rows, :].astype(F32)
            picked[b, rows, :] = value.astype(BF16)
    for j in range(XY):
        total = jnp.zeros((TILE, F), F32)
        for b in range(H):
            at = b * XY + j
            place = one_hot(col_ref[at : at + 1, :], (TILE, EDGES), 0)
            total += dot(place, picked[b, pl.ds(j * EDGES, EDGES), :])
        pay_ref[j, pl.ds(0, TILE), :] = total.astype(BF16)
        pay_ref[j, pl.ds(TILE, WR), :] = own


def final_kernel(part_ref, g_ref, s_ref, w_ref, fg_ref, wg_ref):
    back = g_ref[...].astype(F32)
    for k in range(XY):
        back += part_ref[k, pl.ds(0, TILE), :].astype(F32)
        wg_ref[pl.ds(k * WR, WR), :] = part_ref[k, pl.ds(TILE, WR), :].astype(F32)
    grad_xw = (s_ref[...] * back).astype(BF16)
    fg_ref[...] = lax.dot_general(
        grad_xw, w_ref[...], (((1,), (1,)), ((), ())), preferred_element_type=F32
    ).astype(BF16)


def call(kernel, outs, scratch=(), flops=TILE * F * F):
    return pl.pallas_call(
        kernel,
        out_shape=[jax.ShapeDtypeStruct(shape, dtype) for shape, dtype in outs],
        out_specs=[pl.BlockSpec(memory_space=pltpu.VMEM)] * len(outs),
        scratch_shapes=[pltpu.VMEM(shape, dtype) for shape, dtype in scratch],
        compiler_params=PARAMS,
        cost_estimate=pl.CostEstimate(
            flops=flops, bytes_accessed=2 * 1024 * 1024, transcendentals=0
        ),
    )


def exchange(array, axes):
    return lax.all_to_all(array, axes, 0, 0, tiled=True)


def swap(array, axis):
    return lax.ppermute(array, axis, [(0, 1), (1, 0)])


def per_device(
    features, weight, bias, node_scale, cotangent, edge_slot, edge_row, edge_col, tile_row
):
    h, c = lax.axis_index("h"), lax.axis_index("c")
    s = node_scale[:, None]
    bias = bias[None, :]

    slot = edge_slot.reshape(XY * H, EDGES)
    tiles = tile_row.reshape(XY * H, SLOTS)
    tile = sum(jnp.where(slot == k, tiles[:, k : k + 1], 0) for k in range(SLOTS))
    target = ((tile & 1) ^ c) * HALF + (tile >> 1) * TILE + edge_row.reshape(slot.shape)
    target = jnp.where(slot < SLOTS, target, -1)
    edges = jnp.stack([target, edge_col.reshape(slot.shape)]).reshape(2, XY, H, EDGES)
    kept = lax.dynamic_index_in_dim(edges, h, 2, keepdims=False)
    came = swap(lax.dynamic_index_in_dim(edges, 1 - h, 2, keepdims=False), "h")

    (spread,) = call(spread_kernel, [((XY, TILE, F), BF16)])(features, node_scale[None, :])
    sources = exchange(spread, ("x", "y"))

    pairs = jnp.stack([jnp.where(h == 0, kept, came), jnp.where(h == 0, came, kept)], axis=1)
    lane = pairs.reshape(2 * H, E_ALL)
    sub = lane.T
    columns = pairs[1].reshape(H * XY, EDGES)

    gathered, send = call(
        forward_send_kernel,
        [((H, E_ALL, F), BF16), ((H, HALF, F), BF16)],
        flops=4 * E_ALL * F * (HALF + TILE),
    )(sources, lane, sub)
    other = swap(send, "c")
    (mine,) = call(
        forward_keep_kernel, [((H, HALF, F), F32)], flops=4 * E_ALL * F * HALF
    )(gathered, lane)
    (partial,) = call(add_kernel, [((H, HALF, F), BF16)])(mine, other)
    partial = partial.reshape(ZN, TILE, F)
    partial = exchange(partial, ("h", "l"))
    output, g, w_parts = call(
        middle_kernel,
        [((TILE, F), BF16), ((TILE, F), BF16), ((XY, WR + BB, F), BF16)],
    )(partial, features, s, weight, bias, cotangent)
    w_parts = exchange(w_parts, ("x", "y"))
    (pay,) = call(load_kernel, [((ZN, ZCHUNK, F), BF16)])(w_parts, g)
    around = exchange(pay, ("h", "l"))
    other = swap(around, "c")
    (picked,) = call(
        backward_mine_kernel,
        [((H, E_ALL, F), BF16)],
        [((HALF, F), BF16)],
        flops=4 * E_ALL * F * HALF,
    )(around, sub)
    terms, bias_grad = call(
        backward_kernel,
        [((XY, XCHUNK, F), BF16), ((1, F), F32)],
        [((HALF, F), BF16), ((H, E_ALL, F), BF16)],
        flops=4 * E_ALL * F * (HALF + TILE),
    )(picked, around, other, sub, columns)
    terms = exchange(terms, ("x", "y"))
    feature_grad, weight_grad = call(
        final_kernel, [((TILE, F), BF16), ((F, F), F32)]
    )(terms, g, s, weight)
    return output, feature_grad, weight_grad, bias_grad.reshape(F)


def solution(mesh):
    fine = Mesh(mesh.devices.reshape(X, Y, H, L, C), ALL)
    rows, edges = P(ALL, None), P(("x", "y", "h"), ("l", "c"), None, None)
    return jax.shard_map(
        per_device,
        mesh=fine,
        in_specs=(rows, P(), P(), P(ALL), rows, edges, edges, edges, edges),
        out_specs=(rows, rows, P(), P()),
        check_vma=False,
    )
```

```python
import functools
import math

import jax
import jax.numpy as jnp
from jax import lax
from jax.experimental import pallas as pl
from jax.experimental.pallas import tpu as pltpu
from jax.sharding import Mesh, PartitionSpec as P

X, Y, H, L, C = 4, 4, 2, 4, 2
XY, ZN = X * Y, H * L
TILE, F, SLOTS, EDGES = 128, 256, 4, 96
HALF = L * TILE
ROWS = C * HALF
E_ALL = XY * EDGES
STEP = 256
WR, BB = F // XY, 16
ZCHUNK = TILE + WR + BB
F32, BF16, I32 = jnp.float32, jnp.bfloat16, jnp.int32
K0, K1 = math.sqrt(2.0 / math.pi), 0.044715
ALL = ("x", "y", "h", "l", "c")
PARAMS = pltpu.CompilerParams(vmem_limit_bytes=40 * 1024 * 1024)


def dot(a, b):
    return jnp.dot(a, b, preferred_element_type=F32)


def one_hot(index, shape, axis, base=0):
    return (index == lax.broadcasted_iota(I32, shape, axis) + base).astype(F32).astype(BF16)


def split_rows(row):
    high = row.astype(BF16).astype(F32)
    at = lax.broadcasted_iota(I32, (BB, F), 0)
    return jnp.where(at == 0, high, jnp.where(at == 1, row - high, 0.0)).astype(BF16)


def forward_send_kernel(x_ref, lane_ref, sub_ref, gathered_ref, send_ref):
    for b in range(H):
        for j in range(XY):
            rows = pl.ds(j * EDGES, EDGES)
            pick = one_hot(sub_ref[rows, H + b : H + b + 1], (EDGES, TILE), 1)
            gathered_ref[b, rows, :] = dot(pick, x_ref[j]).astype(BF16)
    for b in range(H):
        for m in range(HALF // STEP):
            place = one_hot(lane_ref[b : b + 1, :], (STEP, E_ALL), 0, HALF + m * STEP)
            send_ref[b, pl.ds(m * STEP, STEP), :] = dot(place, gathered_ref[b]).astype(BF16)


def forward_keep_kernel(gathered_ref, lane_ref, mine_ref):
    for b in range(H):
        for m in range(HALF // STEP):
            place = one_hot(lane_ref[b : b + 1, :], (STEP, E_ALL), 0, m * STEP)
            mine_ref[b, pl.ds(m * STEP, STEP), :] = dot(place, gathered_ref[b])


def add_kernel(mine_ref, other_ref, out_ref):
    out_ref[...] = (mine_ref[...] + other_ref[...].astype(F32)).astype(BF16)


def middle_kernel(part_ref, x_ref, s_ref, w_ref, bias_ref, ct_ref, out_ref, g_ref, wp_ref):
    s = s_ref[...]
    z = s * x_ref[...].astype(F32)
    for k in range(ZN):
        z += part_ref[k].astype(F32)
    z_high = z.astype(BF16)
    z_low = (z - z_high.astype(F32)).astype(BF16)
    w = w_ref[...]
    p = s * (dot(z_high, w) + dot(z_low, w)) + bias_ref[...]
    square = p * p
    th = jnp.tanh(K0 * (p + K1 * (p * square)))
    out_ref[...] = (0.5 * p * (1.0 + th)).astype(BF16)
    slope = 0.5 * (1.0 + th) + 0.5 * p * (1.0 - th * th) * (K0 * (1.0 + 3.0 * K1 * square))
    grad = ct_ref[...].astype(F32) * slope
    g = (s * grad).astype(BF16)
    g_ref[...] = g
    first = (((0,), (0,)), ((), ()))
    wg = lax.dot_general(z_high, g, first, preferred_element_type=F32)
    wg += lax.dot_general(z_low, g, first, preferred_element_type=F32)
    bias_rows = split_rows(jnp.sum(grad, axis=0, keepdims=True))
    for k in range(XY):
        wp_ref[k, pl.ds(0, WR), :] = wg[k * WR : (k + 1) * WR].astype(BF16)
        wp_ref[k, pl.ds(WR, BB), :] = bias_rows


def load_kernel(w_ref, g_ref, pay_ref):
    tail = jnp.zeros((WR + BB, F), F32)
    for k in range(XY):
        tail += w_ref[k].astype(F32)
    own = tail[:WR].astype(BF16)
    bias_rows = split_rows(jnp.sum(tail[WR:], axis=0, keepdims=True))
    g = g_ref[...]
    for k in range(ZN):
        pay_ref[k, pl.ds(0, TILE), :] = g
        pay_ref[k, pl.ds(TILE, WR), :] = own
        pay_ref[k, pl.ds(TILE + WR, BB), :] = bias_rows


def backward_mine_kernel(mine_ref, sub_ref, picked_ref, grads):
    for b in range(H):
        for k in range(L):
            grads[pl.ds(k * TILE, TILE), :] = mine_ref[b * L + k, pl.ds(0, TILE), :]
        for m in range(E_ALL // STEP):
            rows = pl.ds(m * STEP, STEP)
            pick = one_hot(sub_ref[rows, b : b + 1], (STEP, HALF), 1)
            picked_ref[b, rows, :] = dot(pick, grads[...]).astype(BF16)


def backward_pick_kernel(picked_ref, mine_ref, other_ref, sub_ref, all_ref, w_ref, bias_ref, grads):
    factor = 1.0 / math.sqrt(XY * ZN * C * TILE)
    tail_mine = jnp.zeros((WR + BB, F), F32)
    tail_other = jnp.zeros((WR + BB, F), F32)
    for k in range(ZN):
        rows = pl.ds(TILE, WR + BB)
        tail_mine += mine_ref[k, rows, :].astype(F32)
        tail_other += other_ref[k, rows, :].astype(F32)
    tail = (tail_mine + tail_other) * factor
    w_ref[...] = tail[:WR].astype(BF16)
    bias_ref[...] = jnp.sum(tail[WR:], axis=0, keepdims=True)
    for b in range(H):
        for k in range(L):
            grads[pl.ds(k * TILE, TILE), :] = other_ref[b * L + k, pl.ds(0, TILE), :]
        for m in range(E_ALL // STEP):
            rows = pl.ds(m * STEP, STEP)
            pick = one_hot(sub_ref[rows, b : b + 1], (STEP, HALF), 1, HALF)
            value = dot(pick, grads[...]) + picked_ref[b, rows, :].astype(F32)
            all_ref[b, rows, :] = value.astype(BF16)


def place_terms(at_x, picked_ref, col_ref, out_ref, dtype):
    for y in range(Y):
        total = jnp.zeros((TILE, F), F32)
        j = at_x * Y + y
        for b in range(H):
            place = one_hot(col_ref[pl.ds(b * XY + j, 1), :], (TILE, EDGES), 0)
            rows = pl.ds(pl.multiple_of(j * EDGES, 32), EDGES)
            total += dot(place, picked_ref[b, rows, :])
        out_ref[pl.ds(y * TILE, TILE), :] = total.astype(dtype)


def terms_kernel(step, at_ref, picked_ref, col_ref, w_ref, out_ref):
    place_terms(lax.rem(at_ref[0] + step, X), picked_ref, col_ref, out_ref, BF16)
    out_ref[pl.ds(Y * TILE, WR), :] = w_ref[...]


def own_terms_kernel(at_ref, picked_ref, col_ref, out_ref):
    place_terms(at_ref[0], picked_ref, col_ref, out_ref, F32)


def x_sum_kernel(at_ref, own_ref, w_ref, first, second, third, one_ref, two_ref, three_ref, keep_ref, total, rows):
    x, y = at_ref[0], at_ref[1]
    parts = (first, second, third)
    value = own_ref[...]
    for part in parts:
        value += part[pl.ds(0, Y * TILE), :].astype(F32)
    total[...] = value
    rows[pl.ds(pl.multiple_of(x * WR, WR), WR), :] = w_ref[...].astype(F32)
    for step, part in enumerate(parts, 1):
        at = pl.multiple_of(lax.rem(x + X - step, X) * WR, WR)
        rows[pl.ds(at, WR), :] = part[pl.ds(Y * TILE, WR), :].astype(F32)
    for step, out in enumerate((one_ref, two_ref, three_ref), 1):
        at = pl.multiple_of(lax.rem(y + step, Y) * TILE, TILE)
        out[pl.ds(0, TILE), :] = total[pl.ds(at, TILE), :].astype(BF16)
        out[pl.ds(TILE, X * WR), :] = rows[...].astype(BF16)
    keep_ref[pl.ds(0, TILE), :] = total[pl.ds(pl.multiple_of(y * TILE, TILE), TILE), :]
    keep_ref[pl.ds(TILE, X * WR), :] = rows[...]


def final_kernel(at_ref, keep_ref, first, second, third, g_ref, s_ref, weight_ref, fg_ref, wg_ref):
    y = at_ref[1]
    back = g_ref[...].astype(F32) + keep_ref[pl.ds(0, TILE), :]
    for step, part in enumerate((keep_ref, first, second, third)):
        if step:
            back += part[pl.ds(0, TILE), :].astype(F32)
        for x in range(X):
            at = pl.multiple_of((x * Y + lax.rem(y + Y - step, Y)) * WR, WR)
            wg_ref[pl.ds(at, WR), :] = part[pl.ds(TILE + x * WR, WR), :].astype(F32)
    grad_xw = (s_ref[...] * back).astype(BF16)
    fg_ref[...] = lax.dot_general(
        grad_xw, weight_ref[...], (((1,), (1,)), ((), ())), preferred_element_type=F32
    ).astype(BF16)


def call(kernel, outs, scratch=(), smem=0, flops=TILE * F * F):
    def run(*args):
        spaces = [pltpu.SMEM if k < smem else pltpu.VMEM for k in range(len(args))]
        return pl.pallas_call(
            kernel,
            out_shape=[jax.ShapeDtypeStruct(shape, dtype) for shape, dtype in outs],
            in_specs=[pl.BlockSpec(memory_space=space) for space in spaces],
            out_specs=[pl.BlockSpec(memory_space=pltpu.VMEM)] * len(outs),
            scratch_shapes=[pltpu.VMEM(shape, dtype) for shape, dtype in scratch],
            compiler_params=PARAMS,
            cost_estimate=pl.CostEstimate(
                flops=flops, bytes_accessed=2 * 1024 * 1024, transcendentals=0
            ),
        )(*args)

    return run


def exchange(array, axes):
    return lax.all_to_all(array, axes, 0, 0, tiled=True)


def shift(array, axis, size, step):
    return lax.ppermute(array, axis, [(k, (k + step) % size) for k in range(size)])


def swap(array, axis):
    return shift(array, axis, 2, 1)


def per_device(
    features, weight, bias, node_scale, cotangent, edge_slot, edge_row, edge_col, tile_row
):
    h, c = lax.axis_index("h"), lax.axis_index("c")
    s = node_scale[:, None]
    bias = bias[None, :]

    slot = edge_slot.reshape(XY * H, EDGES)
    tiles = tile_row.reshape(XY * H, SLOTS)
    tile = sum(jnp.where(slot == k, tiles[:, k : k + 1], 0) for k in range(SLOTS))
    target = ((tile & 1) ^ c) * HALF + (tile >> 1) * TILE + edge_row.reshape(slot.shape)
    target = jnp.where(slot < SLOTS, target, -1)
    edges = jnp.stack([target, edge_col.reshape(slot.shape)]).reshape(2, XY, H, EDGES)
    kept = lax.dynamic_index_in_dim(edges, h, 2, keepdims=False)
    came = swap(lax.dynamic_index_in_dim(edges, 1 - h, 2, keepdims=False), "h")

    ones = lax.optimization_barrier(jnp.ones((XY, 1, 1), F32))
    spread = (ones * s[None] * features.astype(F32)[None]).astype(BF16)
    sources = exchange(spread, ("x", "y"))

    pairs = jnp.stack([jnp.where(h == 0, kept, came), jnp.where(h == 0, came, kept)], axis=1)
    lane = pairs.reshape(2 * H, E_ALL)
    sub = lane.T
    columns = pairs[1].reshape(H * XY, EDGES)

    gathered, send = call(
        forward_send_kernel,
        [((H, E_ALL, F), BF16), ((H, HALF, F), BF16)],
        flops=4 * E_ALL * F * (HALF + TILE),
    )(sources, lane, sub)
    other = swap(send, "c")
    (mine,) = call(
        forward_keep_kernel, [((H, HALF, F), F32)], flops=4 * E_ALL * F * HALF
    )(gathered, lane)
    (partial,) = call(add_kernel, [((H, HALF, F), BF16)])(mine, other)
    partial = partial.reshape(ZN, TILE, F)
    partial = exchange(partial, ("h", "l"))
    output, g, w_parts = call(
        middle_kernel,
        [((TILE, F), BF16), ((TILE, F), BF16), ((XY, WR + BB, F), BF16)],
    )(partial, features, s, weight, bias, cotangent)
    w_parts = exchange(w_parts, ("x", "y"))
    (pay,) = call(load_kernel, [((ZN, ZCHUNK, F), BF16)])(w_parts, g)
    around = exchange(pay, ("h", "l"))
    other = swap(around, "c")
    (picked,) = call(
        backward_mine_kernel,
        [((H, E_ALL, F), BF16)],
        [((HALF, F), BF16)],
        flops=4 * E_ALL * F * HALF,
    )(around, sub)
    at = jnp.stack([lax.axis_index("x"), lax.axis_index("y")]).astype(I32)
    picked, w_own, bias_grad = call(
        backward_pick_kernel,
        [((H, E_ALL, F), BF16), ((WR, F), BF16), ((1, F), F32)],
        [((HALF, F), BF16)],
        flops=4 * E_ALL * F * HALF,
    )(picked, around, other, sub)
    x_rows, y_rows = Y * TILE + WR, TILE + X * WR
    came = [None] * X
    for step in (2, 1, 3):
        (terms,) = call(
            functools.partial(terms_kernel, step),
            [((x_rows, F), BF16)],
            smem=1,
            flops=E_ALL * F * TILE,
        )(at, picked, columns, w_own)
        came[step] = shift(terms, "x", X, step)
    (own,) = call(
        own_terms_kernel, [((Y * TILE, F), F32)], smem=1, flops=E_ALL * F * TILE
    )(at, picked, columns)
    *sends, keep = call(
        x_sum_kernel,
        [((y_rows, F), BF16)] * 3 + [((y_rows, F), F32)],
        [((Y * TILE, F), F32), ((X * WR, F), F32)],
        smem=1,
    )(at, own, w_own, *came[1:])
    came = [shift(sends[step - 1], "y", Y, step) for step in (1, 2, 3)]
    feature_grad, weight_grad = call(
        final_kernel, [((TILE, F), BF16), ((F, F), F32)], smem=1
    )(at, keep, *came, g, s, weight)
    return output, feature_grad, weight_grad, bias_grad.reshape(F)


def solution(mesh):
    fine = Mesh(mesh.devices.reshape(X, Y, H, L, C), ALL)
    rows, edges = P(ALL, None), P(("x", "y", "h"), ("l", "c"), None, None)
    return jax.shard_map(
        per_device,
        mesh=fine,
        in_specs=(rows, P(), P(), P(ALL), rows, edges, edges, edges, edges),
        out_specs=(rows, rows, P(), P()),
        check_vma=False,
    )
```

```python
import math

import jax
import jax.numpy as jnp
from jax import lax
from jax.experimental import pallas as pl
from jax.experimental.pallas import tpu as pltpu
from jax.sharding import Mesh, PartitionSpec as P

X, Y, H, L, C = 4, 4, 2, 4, 2
XY, ZN = X * Y, H * L
TILE, F, SLOTS, EDGES = 128, 256, 4, 96
HALF = L * TILE
ROWS = C * HALF
E_ALL = XY * EDGES
STEP = 4 * EDGES
WR, BB = F // XY, 16
ZCHUNK = TILE + WR + BB
XCHUNK = TILE + WR
F32, BF16, I32 = jnp.float32, jnp.bfloat16, jnp.int32
K0, K1 = math.sqrt(2.0 / math.pi), 0.044715
ALL = ("x", "y", "h", "l", "c")
PARAMS = pltpu.CompilerParams(vmem_limit_bytes=40 * 1024 * 1024)


def dot(a, b):
    return jnp.dot(a, b, preferred_element_type=F32)


def one_hot(index, shape, axis, base=0):
    return (index == lax.broadcasted_iota(I32, shape, axis) + base).astype(F32).astype(BF16)


def split_rows(row):
    high = row.astype(BF16).astype(F32)
    at = lax.broadcasted_iota(I32, (BB, F), 0)
    return jnp.where(at == 0, high, jnp.where(at == 1, row - high, 0.0)).astype(BF16)


def spread_kernel(x_ref, s_ref, out_ref, x, s, scaled, sems):
    loads = [
        pltpu.make_async_copy(x_ref, x, sems.at[0]),
        pltpu.make_async_copy(s_ref, s, sems.at[1]),
    ]
    for load in loads:
        load.start()
    for load in loads:
        load.wait()
    scale = jnp.transpose(jnp.broadcast_to(s[...], (TILE, TILE)))
    for k in range(F // TILE):
        part = pl.ds(k * TILE, TILE)
        scaled[:, part] = (scale * x[:, part].astype(F32)).astype(BF16)
    stores = [
        pltpu.make_async_copy(scaled, out_ref.at[j], sems.at[2 + j]) for j in range(XY)
    ]
    for store in stores:
        store.start()
    for store in stores:
        store.wait()


def spread(features, node_scale):
    return pl.pallas_call(
        spread_kernel,
        out_shape=jax.ShapeDtypeStruct((XY, TILE, F), BF16),
        in_specs=[pl.BlockSpec(memory_space=pltpu.HBM)] * 2,
        out_specs=pl.BlockSpec(memory_space=pltpu.HBM),
        scratch_shapes=[
            pltpu.VMEM((TILE, F), BF16),
            pltpu.VMEM((1, TILE), F32),
            pltpu.VMEM((TILE, F), BF16),
            pltpu.SemaphoreType.DMA((2 + XY,)),
        ],
        compiler_params=pltpu.CompilerParams(vmem_limit_bytes=63_480_000),
    )(features, node_scale[None, :])


def forward_send_kernel(x_ref, lane_ref, sub_ref, gathered_ref, send_ref):
    for b in range(H):
        for j in range(XY):
            rows = pl.ds(j * EDGES, EDGES)
            pick = one_hot(sub_ref[rows, H + b : H + b + 1], (EDGES, TILE), 1)
            gathered_ref[b, rows, :] = dot(pick, x_ref[j]).astype(BF16)
    for b in range(H):
        place = one_hot(lane_ref[b : b + 1, :], (HALF, E_ALL), 0, HALF)
        send_ref[b] = dot(place, gathered_ref[b]).astype(BF16)


def forward_keep_kernel(gathered_ref, lane_ref, mine_ref):
    for b in range(H):
        place = one_hot(lane_ref[b : b + 1, :], (HALF, E_ALL), 0)
        mine_ref[b] = dot(place, gathered_ref[b])


def add_kernel(mine_ref, other_ref, out_ref):
    out_ref[...] = (mine_ref[...] + other_ref[...].astype(F32)).astype(BF16)


def middle_kernel(part_ref, x_ref, s_ref, w_ref, bias_ref, ct_ref, out_ref, g_ref, wp_ref):
    s = s_ref[...]
    z = s * x_ref[...].astype(F32)
    for k in range(ZN):
        z += part_ref[k].astype(F32)
    z_high = z.astype(BF16)
    z_low = (z - z_high.astype(F32)).astype(BF16)
    w = w_ref[...]
    p = s * (dot(z_high, w) + dot(z_low, w)) + bias_ref[...]
    square = p * p
    th = jnp.tanh(K0 * (p + K1 * (p * square)))
    out_ref[...] = (0.5 * p * (1.0 + th)).astype(BF16)
    slope = 0.5 * (1.0 + th) + 0.5 * p * (1.0 - th * th) * (K0 * (1.0 + 3.0 * K1 * square))
    grad = ct_ref[...].astype(F32) * slope
    g = (s * grad).astype(BF16)
    g_ref[...] = g
    first = (((0,), (0,)), ((), ()))
    wg = lax.dot_general(z_high, g, first, preferred_element_type=F32)
    wg += lax.dot_general(z_low, g, first, preferred_element_type=F32)
    bias_rows = split_rows(jnp.sum(grad, axis=0, keepdims=True))
    for k in range(XY):
        wp_ref[k, pl.ds(0, WR), :] = wg[k * WR : (k + 1) * WR].astype(BF16)
        wp_ref[k, pl.ds(WR, BB), :] = bias_rows


def load_kernel(w_ref, g_ref, pay_ref):
    tail = jnp.zeros((WR + BB, F), F32)
    for k in range(XY):
        tail += w_ref[k].astype(F32)
    own = tail[:WR].astype(BF16)
    bias_rows = split_rows(jnp.sum(tail[WR:], axis=0, keepdims=True))
    g = g_ref[...]
    for k in range(ZN):
        pay_ref[k, pl.ds(0, TILE), :] = g
        pay_ref[k, pl.ds(TILE, WR), :] = own
        pay_ref[k, pl.ds(TILE + WR, BB), :] = bias_rows


def backward_mine_kernel(mine_ref, sub_ref, picked_ref, grads):
    for b in range(H):
        for k in range(L):
            grads[pl.ds(k * TILE, TILE), :] = mine_ref[b * L + k, pl.ds(0, TILE), :]
        for m in range(E_ALL // STEP):
            pick = one_hot(sub_ref[pl.ds(m * STEP, STEP), b : b + 1], (STEP, HALF), 1)
            value = dot(pick, grads[...]).astype(BF16)
            for q in range(STEP // EDGES):
                picked_ref[m * (STEP // EDGES) + q, pl.ds(b * EDGES, EDGES), :] = value[
                    q * EDGES : (q + 1) * EDGES
                ]


def backward_kernel(
    picked_ref, mine_ref, other_ref, sub_ref, col_ref, pay_ref, bias_ref, grads, picked
):
    factor = 1.0 / math.sqrt(XY * ZN * C * TILE)
    tail_mine = jnp.zeros((WR + BB, F), F32)
    tail_other = jnp.zeros((WR + BB, F), F32)
    for k in range(ZN):
        rows = pl.ds(TILE, WR + BB)
        tail_mine += mine_ref[k, rows, :].astype(F32)
        tail_other += other_ref[k, rows, :].astype(F32)
    tail = (tail_mine + tail_other) * factor
    own = tail[:WR].astype(BF16)
    bias_ref[...] = jnp.sum(tail[WR:], axis=0, keepdims=True)
    for b in range(H):
        for k in range(L):
            grads[pl.ds(k * TILE, TILE), :] = other_ref[b * L + k, pl.ds(0, TILE), :]
        for m in range(E_ALL // STEP):
            pick = one_hot(sub_ref[pl.ds(m * STEP, STEP), b : b + 1], (STEP, HALF), 1, HALF)
            value = dot(pick, grads[...])
            for q in range(STEP // EDGES):
                j, rows = m * (STEP // EDGES) + q, pl.ds(b * EDGES, EDGES)
                both = value[q * EDGES : (q + 1) * EDGES] + picked_ref[j, rows, :].astype(F32)
                picked[j, rows, :] = both.astype(BF16)
    for j in range(XY):
        place = one_hot(col_ref[j : j + 1, :], (TILE, H * EDGES), 0)
        total = dot(place, picked[j])
        pay_ref[j, pl.ds(0, TILE), :] = total.astype(BF16)
        pay_ref[j, pl.ds(TILE, WR), :] = own


def final_kernel(part_ref, g_ref, s_ref, w_ref, fg_ref, wg_ref):
    back = g_ref[...].astype(F32)
    for k in range(XY):
        back += part_ref[k, pl.ds(0, TILE), :].astype(F32)
        wg_ref[pl.ds(k * WR, WR), :] = part_ref[k, pl.ds(TILE, WR), :].astype(F32)
    grad_xw = (s_ref[...] * back).astype(BF16)
    fg_ref[...] = lax.dot_general(
        grad_xw, w_ref[...], (((1,), (1,)), ((), ())), preferred_element_type=F32
    ).astype(BF16)


def call(kernel, outs, scratch=(), flops=TILE * F * F):
    return pl.pallas_call(
        kernel,
        out_shape=[jax.ShapeDtypeStruct(shape, dtype) for shape, dtype in outs],
        out_specs=[pl.BlockSpec(memory_space=pltpu.VMEM)] * len(outs),
        scratch_shapes=[pltpu.VMEM(shape, dtype) for shape, dtype in scratch],
        compiler_params=PARAMS,
        cost_estimate=pl.CostEstimate(
            flops=flops, bytes_accessed=2 * 1024 * 1024, transcendentals=0
        ),
    )


def exchange(array, axes):
    return lax.all_to_all(array, axes, 0, 0, tiled=True)


def swap(array, axis):
    return lax.ppermute(array, axis, [(0, 1), (1, 0)])


def per_device(
    features, weight, bias, node_scale, cotangent, edge_slot, edge_row, edge_col, tile_row
):
    h, c = lax.axis_index("h"), lax.axis_index("c")
    s = node_scale[:, None]
    bias = bias[None, :]

    slot = edge_slot.reshape(XY * H, EDGES)
    tiles = tile_row.reshape(XY * H, SLOTS)
    tile = sum(jnp.where(slot == k, tiles[:, k : k + 1], 0) for k in range(SLOTS))
    target = ((tile & 1) ^ c) * HALF + (tile >> 1) * TILE + edge_row.reshape(slot.shape)
    target = jnp.where(slot < SLOTS, target, -1)
    edges = jnp.stack([target, edge_col.reshape(slot.shape)]).reshape(2, XY, H, EDGES)
    kept = lax.dynamic_index_in_dim(edges, h, 2, keepdims=False)
    came = swap(lax.dynamic_index_in_dim(edges, 1 - h, 2, keepdims=False), "h")

    sources = exchange(spread(features, node_scale), ("x", "y"))

    pairs = jnp.stack([jnp.where(h == 0, kept, came), jnp.where(h == 0, came, kept)], axis=1)
    lane = pairs.reshape(2 * H, E_ALL)
    sub = lane.T
    columns = jnp.concatenate([pairs[1, 0], pairs[1, 1]], axis=1)

    gathered, send = call(
        forward_send_kernel,
        [((H, E_ALL, F), BF16), ((H, HALF, F), BF16)],
        flops=4 * E_ALL * F * (HALF + TILE),
    )(sources, lane, sub)
    other = swap(send, "c")
    (mine,) = call(
        forward_keep_kernel, [((H, HALF, F), F32)], flops=4 * E_ALL * F * HALF
    )(gathered, lane)
    (partial,) = call(add_kernel, [((H, HALF, F), BF16)])(mine, other)
    partial = partial.reshape(ZN, TILE, F)
    partial = exchange(partial, ("h", "l"))
    output, g, w_parts = call(
        middle_kernel,
        [((TILE, F), BF16), ((TILE, F), BF16), ((XY, WR + BB, F), BF16)],
    )(partial, features, s, weight, bias, cotangent)
    w_parts = exchange(w_parts, ("x", "y"))
    (pay,) = call(load_kernel, [((ZN, ZCHUNK, F), BF16)])(w_parts, g)
    around = exchange(pay, ("h", "l"))
    other = swap(around, "c")
    (picked,) = call(
        backward_mine_kernel,
        [((XY, H * EDGES, F), BF16)],
        [((HALF, F), BF16)],
        flops=4 * E_ALL * F * HALF,
    )(around, sub)
    terms, bias_grad = call(
        backward_kernel,
        [((XY, XCHUNK, F), BF16), ((1, F), F32)],
        [((HALF, F), BF16), ((XY, H * EDGES, F), BF16)],
        flops=4 * E_ALL * F * (HALF + TILE),
    )(picked, around, other, sub, columns)
    terms = exchange(terms, ("x", "y"))
    feature_grad, weight_grad = call(
        final_kernel, [((TILE, F), BF16), ((F, F), F32)]
    )(terms, g, s, weight)
    return output, feature_grad, weight_grad, bias_grad.reshape(F)


def solution(mesh):
    fine = Mesh(mesh.devices.reshape(X, Y, H, L, C), ALL)
    rows, edges = P(ALL, None), P(("x", "y", "h"), ("l", "c"), None, None)
    return jax.shard_map(
        per_device,
        mesh=fine,
        in_specs=(rows, P(), P(), P(ALL), rows, edges, edges, edges, edges),
        out_specs=(rows, rows, P(), P()),
        check_vma=False,
    )
```

```python
import math

import jax
import jax.numpy as jnp
from jax import lax
from jax.experimental import pallas as pl
from jax.experimental.pallas import tpu as pltpu
from jax.sharding import Mesh, PartitionSpec as P

X, Y, H, L, C = 4, 4, 2, 4, 2
XY, ZN = X * Y, H * L
TILE, F, SLOTS, EDGES = 128, 256, 4, 96
HALF = L * TILE
ROWS = C * HALF
E_ALL = XY * EDGES
STEP = 4 * EDGES
WR, BB = F // XY, 16
ZCHUNK = TILE + WR + BB
XCHUNK = TILE + WR
F32, BF16, I32 = jnp.float32, jnp.bfloat16, jnp.int32
K0, K1 = math.sqrt(2.0 / math.pi), 0.044715
ALL = ("x", "y", "h", "l", "c")
PARAMS = pltpu.CompilerParams(vmem_limit_bytes=40 * 1024 * 1024)


def dot(a, b):
    return jnp.dot(a, b, preferred_element_type=F32)


def one_hot(index, shape, axis, base=0):
    return (index == lax.broadcasted_iota(I32, shape, axis) + base).astype(F32).astype(BF16)


def split_rows(row):
    high = row.astype(BF16).astype(F32)
    at = lax.broadcasted_iota(I32, (BB, F), 0)
    return jnp.where(at == 0, high, jnp.where(at == 1, row - high, 0.0)).astype(BF16)


def column(row):
    return jnp.transpose(jnp.broadcast_to(row, (TILE, TILE)))[:, :1]


def spread_kernel(x_ref, s_ref, out_ref, x, s, scaled, sems):
    loads = [
        pltpu.make_async_copy(x_ref, x, sems.at[0]),
        pltpu.make_async_copy(s_ref, s, sems.at[1]),
    ]
    for load in loads:
        load.start()
    for load in loads:
        load.wait()
    scaled[...] = (column(s[...]) * x[...].astype(F32)).astype(BF16)
    stores = [
        pltpu.make_async_copy(scaled, out_ref.at[j], sems.at[2 + j]) for j in range(XY)
    ]
    for store in stores:
        store.start()
    for store in stores:
        store.wait()


def spread(features, node_scale):
    return pl.pallas_call(
        spread_kernel,
        out_shape=jax.ShapeDtypeStruct((XY, TILE, F), BF16),
        in_specs=[pl.BlockSpec(memory_space=pltpu.HBM)] * 2,
        out_specs=pl.BlockSpec(memory_space=pltpu.HBM),
        scratch_shapes=[
            pltpu.VMEM((TILE, F), BF16),
            pltpu.VMEM((1, TILE), F32),
            pltpu.VMEM((TILE, F), BF16),
            pltpu.SemaphoreType.DMA((2 + XY,)),
        ],
        compiler_params=pltpu.CompilerParams(vmem_limit_bytes=63_480_000),
    )(features, node_scale)


def forward_send_kernel(x_ref, lane_ref, sub_ref, gathered_ref, send_ref):
    for b in range(H):
        for j in range(XY):
            rows = pl.ds(j * EDGES, EDGES)
            pick = one_hot(sub_ref[rows, H + b : H + b + 1], (EDGES, TILE), 1)
            gathered_ref[b, rows, :] = dot(pick, x_ref[j]).astype(BF16)
    for b in range(H):
        place = one_hot(lane_ref[b : b + 1, :], (HALF, E_ALL), 0, HALF)
        send_ref[b] = dot(place, gathered_ref[b]).astype(BF16)


def forward_keep_kernel(gathered_ref, lane_ref, mine_ref):
    for b in range(H):
        place = one_hot(lane_ref[b : b + 1, :], (HALF, E_ALL), 0)
        mine_ref[b] = dot(place, gathered_ref[b])


def add_kernel(mine_ref, other_ref, out_ref):
    out_ref[...] = (mine_ref[...] + other_ref[...].astype(F32)).astype(BF16)


def middle_kernel(part_ref, x_ref, s_ref, w_ref, bias_ref, ct_ref, out_ref, g_ref, wp_ref):
    s = column(s_ref[...])
    z = s * x_ref[...].astype(F32)
    for k in range(ZN):
        z += part_ref[k].astype(F32)
    z_high = z.astype(BF16)
    z_low = (z - z_high.astype(F32)).astype(BF16)
    w = w_ref[...]
    p = s * (dot(z_high, w) + dot(z_low, w)) + bias_ref[...]
    square = p * p
    th = jnp.tanh(K0 * (p + K1 * (p * square)))
    out_ref[...] = (0.5 * p * (1.0 + th)).astype(BF16)
    slope = 0.5 * (1.0 + th) + 0.5 * p * (1.0 - th * th) * (K0 * (1.0 + 3.0 * K1 * square))
    grad = ct_ref[...].astype(F32) * slope
    g = (s * grad).astype(BF16)
    g_ref[...] = g
    first = (((0,), (0,)), ((), ()))
    wg = lax.dot_general(z_high, g, first, preferred_element_type=F32)
    wg += lax.dot_general(z_low, g, first, preferred_element_type=F32)
    bias_rows = split_rows(jnp.sum(grad, axis=0, keepdims=True))
    for k in range(XY):
        wp_ref[k, pl.ds(0, WR), :] = wg[k * WR : (k + 1) * WR].astype(BF16)
        wp_ref[k, pl.ds(WR, BB), :] = bias_rows


def load_kernel(w_ref, g_ref, pay_ref):
    tail = jnp.zeros((WR + BB, F), F32)
    for k in range(XY):
        tail += w_ref[k].astype(F32)
    own = tail[:WR].astype(BF16)
    bias_rows = split_rows(jnp.sum(tail[WR:], axis=0, keepdims=True))
    g = g_ref[...]
    for k in range(ZN):
        pay_ref[k, pl.ds(0, TILE), :] = g
        pay_ref[k, pl.ds(TILE, WR), :] = own
        pay_ref[k, pl.ds(TILE + WR, BB), :] = bias_rows


def backward_mine_kernel(mine_ref, sub_ref, picked_ref, grads):
    for b in range(H):
        for k in range(L):
            grads[pl.ds(k * TILE, TILE), :] = mine_ref[b * L + k, pl.ds(0, TILE), :]
        for m in range(E_ALL // STEP):
            pick = one_hot(sub_ref[pl.ds(m * STEP, STEP), b : b + 1], (STEP, HALF), 1)
            value = dot(pick, grads[...]).astype(BF16)
            for q in range(STEP // EDGES):
                picked_ref[m * (STEP // EDGES) + q, pl.ds(b * EDGES, EDGES), :] = value[
                    q * EDGES : (q + 1) * EDGES
                ]


def backward_kernel(
    picked_ref, mine_ref, other_ref, sub_ref, col_ref, pay_ref, bias_ref, grads, picked
):
    factor = 1.0 / math.sqrt(XY * ZN * C * TILE)
    tail_mine = jnp.zeros((WR + BB, F), F32)
    tail_other = jnp.zeros((WR + BB, F), F32)
    for k in range(ZN):
        rows = pl.ds(TILE, WR + BB)
        tail_mine += mine_ref[k, rows, :].astype(F32)
        tail_other += other_ref[k, rows, :].astype(F32)
    tail = (tail_mine + tail_other) * factor
    own = tail[:WR].astype(BF16)
    bias_ref[...] = jnp.sum(tail[WR:], axis=0, keepdims=True)
    for b in range(H):
        for k in range(L):
            grads[pl.ds(k * TILE, TILE), :] = other_ref[b * L + k, pl.ds(0, TILE), :]
        for m in range(E_ALL // STEP):
            pick = one_hot(sub_ref[pl.ds(m * STEP, STEP), b : b + 1], (STEP, HALF), 1, HALF)
            value = dot(pick, grads[...])
            for q in range(STEP // EDGES):
                j, rows = m * (STEP // EDGES) + q, pl.ds(b * EDGES, EDGES)
                both = value[q * EDGES : (q + 1) * EDGES] + picked_ref[j, rows, :].astype(F32)
                picked[j, rows, :] = both.astype(BF16)
    for j in range(XY):
        place = one_hot(col_ref[j : j + 1, :], (TILE, H * EDGES), 0)
        total = dot(place, picked[j])
        pay_ref[j, pl.ds(0, TILE), :] = total.astype(BF16)
        pay_ref[j, pl.ds(TILE, WR), :] = own


def final_kernel(part_ref, g_ref, s_ref, w_ref, fg_ref, wg_ref):
    back = g_ref[...].astype(F32)
    for k in range(XY):
        back += part_ref[k, pl.ds(0, TILE), :].astype(F32)
        wg_ref[pl.ds(k * WR, WR), :] = part_ref[k, pl.ds(TILE, WR), :].astype(F32)
    grad_xw = (column(s_ref[...]) * back).astype(BF16)
    fg_ref[...] = lax.dot_general(
        grad_xw, w_ref[...], (((1,), (1,)), ((), ())), preferred_element_type=F32
    ).astype(BF16)


def call(kernel, outs, scratch=(), flops=TILE * F * F):
    return pl.pallas_call(
        kernel,
        out_shape=[jax.ShapeDtypeStruct(shape, dtype) for shape, dtype in outs],
        out_specs=[pl.BlockSpec(memory_space=pltpu.VMEM)] * len(outs),
        scratch_shapes=[pltpu.VMEM(shape, dtype) for shape, dtype in scratch],
        compiler_params=PARAMS,
        cost_estimate=pl.CostEstimate(
            flops=flops, bytes_accessed=2 * 1024 * 1024, transcendentals=0
        ),
    )


def exchange(array, axes):
    return lax.all_to_all(array, axes, 0, 0, tiled=True)


def swap(array, axis):
    return lax.ppermute(array, axis, [(0, 1), (1, 0)])


def per_device(
    features, weight, bias, node_scale, cotangent, edge_slot, edge_row, edge_col, tile_row
):
    h, c = lax.axis_index("h"), lax.axis_index("c")
    s = node_scale[None, :]
    bias = bias[None, :]

    slot = edge_slot.reshape(XY * H, EDGES)
    tiles = tile_row.reshape(XY * H, SLOTS)
    tile = sum(jnp.where(slot == k, tiles[:, k : k + 1], 0) for k in range(SLOTS))
    target = ((tile & 1) ^ c) * HALF + (tile >> 1) * TILE + edge_row.reshape(slot.shape)
    target = jnp.where(slot < SLOTS, target, -1)
    edges = jnp.stack([target, edge_col.reshape(slot.shape)]).reshape(2, XY, H, EDGES)
    kept = lax.dynamic_index_in_dim(edges, h, 2, keepdims=False)
    came = swap(lax.dynamic_index_in_dim(edges, 1 - h, 2, keepdims=False), "h")

    sources = exchange(spread(features, s), ("x", "y"))

    pairs = jnp.stack([jnp.where(h == 0, kept, came), jnp.where(h == 0, came, kept)], axis=1)
    lane = pairs.reshape(2 * H, E_ALL)
    sub = lane.T
    columns = jnp.concatenate([pairs[1, 0], pairs[1, 1]], axis=1)

    gathered, send = call(
        forward_send_kernel,
        [((H, E_ALL, F), BF16), ((H, HALF, F), BF16)],
        flops=4 * E_ALL * F * (HALF + TILE),
    )(sources, lane, sub)
    other = swap(send, "c")
    (mine,) = call(
        forward_keep_kernel, [((H, HALF, F), F32)], flops=4 * E_ALL * F * HALF
    )(gathered, lane)
    (partial,) = call(add_kernel, [((H, HALF, F), BF16)])(mine, other)
    partial = partial.reshape(ZN, TILE, F)
    partial = exchange(partial, ("h", "l"))
    output, g, w_parts = call(
        middle_kernel,
        [((TILE, F), BF16), ((TILE, F), BF16), ((XY, WR + BB, F), BF16)],
    )(partial, features, s, weight, bias, cotangent)
    w_parts = exchange(w_parts, ("x", "y"))
    (pay,) = call(load_kernel, [((ZN, ZCHUNK, F), BF16)])(w_parts, g)
    around = exchange(pay, ("h", "l"))
    other = swap(around, "c")
    (picked,) = call(
        backward_mine_kernel,
        [((XY, H * EDGES, F), BF16)],
        [((HALF, F), BF16)],
        flops=4 * E_ALL * F * HALF,
    )(around, sub)
    terms, bias_grad = call(
        backward_kernel,
        [((XY, XCHUNK, F), BF16), ((1, F), F32)],
        [((HALF, F), BF16), ((XY, H * EDGES, F), BF16)],
        flops=4 * E_ALL * F * (HALF + TILE),
    )(picked, around, other, sub, columns)
    terms = exchange(terms, ("x", "y"))
    feature_grad, weight_grad = call(
        final_kernel, [((TILE, F), BF16), ((F, F), F32)]
    )(terms, g, s, weight)
    return output, feature_grad, weight_grad, bias_grad.reshape(F)


def solution(mesh):
    fine = Mesh(mesh.devices.reshape(X, Y, H, L, C), ALL)
    rows, edges = P(ALL, None), P(("x", "y", "h"), ("l", "c"), None, None)
    return jax.shard_map(
        per_device,
        mesh=fine,
        in_specs=(rows, P(), P(), P(ALL), rows, edges, edges, edges, edges),
        out_specs=(rows, rows, P(), P()),
        check_vma=False,
    )
```

```python
import math

import jax
import jax.numpy as jnp
from jax import lax
from jax.experimental import pallas as pl
from jax.experimental.pallas import tpu as pltpu
from jax.sharding import Mesh, PartitionSpec as P

X, Y, H, L, C = 4, 4, 2, 4, 2
XY, ZN = X * Y, H * L
TILE, F, SLOTS, EDGES = 128, 256, 4, 96
HALF = L * TILE
ROWS = C * HALF
E_ALL = XY * EDGES
STEP = 4 * EDGES
WR, BB = F // XY, 8
ZCHUNK = TILE + WR + BB
XCHUNK = TILE + WR
F32, BF16, I32 = jnp.float32, jnp.bfloat16, jnp.int32
K0, K1 = math.sqrt(2.0 / math.pi), 0.044715
ALL = ("x", "y", "h", "l", "c")
PARAMS = pltpu.CompilerParams(vmem_limit_bytes=40 * 1024 * 1024)


def dot(a, b):
    return jnp.dot(a, b, preferred_element_type=F32)


def one_hot(index, shape, axis, base=0):
    return (index == lax.broadcasted_iota(I32, shape, axis) + base).astype(F32).astype(BF16)


def split_rows(row):
    high = row.astype(BF16).astype(F32)
    at = lax.broadcasted_iota(I32, (BB, F), 0)
    return jnp.where(at == 0, high, jnp.where(at == 1, row - high, 0.0)).astype(BF16)


def column(row):
    return jnp.transpose(jnp.broadcast_to(row, (TILE, TILE)))[:, :1]


def spread_kernel(x_ref, s_ref, out_ref, x, s, scaled, sems):
    loads = [
        pltpu.make_async_copy(x_ref, x, sems.at[0]),
        pltpu.make_async_copy(s_ref, s, sems.at[1]),
    ]
    for load in loads:
        load.start()
    for load in loads:
        load.wait()
    scaled[...] = (column(s[...]) * x[...].astype(F32)).astype(BF16)
    stores = [
        pltpu.make_async_copy(scaled, out_ref.at[j], sems.at[2 + j]) for j in range(XY)
    ]
    for store in stores:
        store.start()
    for store in stores:
        store.wait()


def spread(features, node_scale):
    return pl.pallas_call(
        spread_kernel,
        out_shape=jax.ShapeDtypeStruct((XY, TILE, F), BF16),
        in_specs=[pl.BlockSpec(memory_space=pltpu.HBM)] * 2,
        out_specs=pl.BlockSpec(memory_space=pltpu.HBM),
        scratch_shapes=[
            pltpu.VMEM((TILE, F), BF16),
            pltpu.VMEM((1, TILE), F32),
            pltpu.VMEM((TILE, F), BF16),
            pltpu.SemaphoreType.DMA((2 + XY,)),
        ],
        compiler_params=pltpu.CompilerParams(vmem_limit_bytes=63_480_000),
    )(features, node_scale)


def forward_send_kernel(x_ref, lane_ref, sub_ref, gathered_ref, send_ref):
    for b in range(H):
        for j in range(XY):
            rows = pl.ds(j * EDGES, EDGES)
            pick = one_hot(sub_ref[rows, H + b : H + b + 1], (EDGES, TILE), 1)
            gathered_ref[b, rows, :] = dot(pick, x_ref[j]).astype(BF16)
    for b in range(H):
        place = one_hot(lane_ref[b : b + 1, :], (HALF, E_ALL), 0, HALF)
        send_ref[b] = dot(place, gathered_ref[b]).astype(BF16)


def forward_keep_kernel(gathered_ref, lane_ref, mine_ref):
    for b in range(H):
        place = one_hot(lane_ref[b : b + 1, :], (HALF, E_ALL), 0)
        mine_ref[b] = dot(place, gathered_ref[b])


def add_kernel(mine_ref, other_ref, out_ref):
    out_ref[...] = (mine_ref[...] + other_ref[...].astype(F32)).astype(BF16)


def middle_kernel(part_ref, x_ref, s_ref, w_ref, bias_ref, ct_ref, out_ref, g_ref, wp_ref):
    s = column(s_ref[...])
    z = s * x_ref[...].astype(F32)
    for k in range(ZN):
        z += part_ref[k].astype(F32)
    z_high = z.astype(BF16)
    z_low = (z - z_high.astype(F32)).astype(BF16)
    w = w_ref[...]
    p = s * (dot(z_high, w) + dot(z_low, w)) + bias_ref[...]
    square = p * p
    th = jnp.tanh(K0 * (p + K1 * (p * square)))
    out_ref[...] = (0.5 * p * (1.0 + th)).astype(BF16)
    slope = 0.5 * (1.0 + th) + 0.5 * p * (1.0 - th * th) * (K0 * (1.0 + 3.0 * K1 * square))
    grad = ct_ref[...].astype(F32) * slope
    g = (s * grad).astype(BF16)
    g_ref[...] = g
    first = (((0,), (0,)), ((), ()))
    wg = lax.dot_general(z_high, g, first, preferred_element_type=F32)
    wg += lax.dot_general(z_low, g, first, preferred_element_type=F32)
    bias_rows = split_rows(jnp.sum(grad, axis=0, keepdims=True))
    for k in range(XY):
        wp_ref[k, pl.ds(0, WR), :] = wg[k * WR : (k + 1) * WR].astype(BF16)
        wp_ref[k, pl.ds(WR, BB), :] = bias_rows


def load_kernel(w_ref, g_ref, pay_ref):
    tail = jnp.zeros((WR + BB, F), F32)
    for k in range(XY):
        tail += w_ref[k].astype(F32)
    own = tail[:WR].astype(BF16)
    bias_rows = split_rows(jnp.sum(tail[WR:], axis=0, keepdims=True))
    g = g_ref[...]
    for k in range(ZN):
        pay_ref[k, pl.ds(0, TILE), :] = g
        pay_ref[k, pl.ds(TILE, WR), :] = own
        pay_ref[k, pl.ds(TILE + WR, BB), :] = bias_rows


def backward_mine_kernel(mine_ref, sub_ref, act_ref, picked_ref, out_ref, grads):
    out_ref[...] = act_ref[...]
    for b in range(H):
        for k in range(L):
            grads[pl.ds(k * TILE, TILE), :] = mine_ref[b * L + k, pl.ds(0, TILE), :]
        for m in range(E_ALL // STEP):
            pick = one_hot(sub_ref[pl.ds(m * STEP, STEP), b : b + 1], (STEP, HALF), 1)
            value = dot(pick, grads[...]).astype(BF16)
            for q in range(STEP // EDGES):
                picked_ref[m * (STEP // EDGES) + q, pl.ds(b * EDGES, EDGES), :] = value[
                    q * EDGES : (q + 1) * EDGES
                ]


def backward_kernel(
    picked_ref, mine_ref, other_ref, sub_ref, col_ref, pay_ref, bias_ref, grads, picked
):
    factor = 1.0 / math.sqrt(XY * ZN * C * TILE)
    tail_mine = jnp.zeros((WR + BB, F), F32)
    tail_other = jnp.zeros((WR + BB, F), F32)
    for k in range(ZN):
        rows = pl.ds(TILE, WR + BB)
        tail_mine += mine_ref[k, rows, :].astype(F32)
        tail_other += other_ref[k, rows, :].astype(F32)
    tail = (tail_mine + tail_other) * factor
    own = tail[:WR].astype(BF16)
    bias_ref[...] = jnp.sum(tail[WR:], axis=0, keepdims=True)
    for b in range(H):
        for k in range(L):
            grads[pl.ds(k * TILE, TILE), :] = other_ref[b * L + k, pl.ds(0, TILE), :]
        for m in range(E_ALL // STEP):
            pick = one_hot(sub_ref[pl.ds(m * STEP, STEP), b : b + 1], (STEP, HALF), 1, HALF)
            value = dot(pick, grads[...])
            for q in range(STEP // EDGES):
                j, rows = m * (STEP // EDGES) + q, pl.ds(b * EDGES, EDGES)
                both = value[q * EDGES : (q + 1) * EDGES] + picked_ref[j, rows, :].astype(F32)
                picked[j, rows, :] = both.astype(BF16)
    for j in range(XY):
        place = one_hot(col_ref[j : j + 1, :], (TILE, H * EDGES), 0)
        total = dot(place, picked[j])
        pay_ref[j, pl.ds(0, TILE), :] = total.astype(BF16)
        pay_ref[j, pl.ds(TILE, WR), :] = own


def final_kernel(part_ref, g_ref, s_ref, w_ref, bias_ref, fg_ref, wg_ref, out_ref):
    out_ref[...] = bias_ref[...]
    back = g_ref[...].astype(F32)
    for k in range(XY):
        back += part_ref[k, pl.ds(0, TILE), :].astype(F32)
        wg_ref[pl.ds(k * WR, WR), :] = part_ref[k, pl.ds(TILE, WR), :].astype(F32)
    grad_xw = (column(s_ref[...]) * back).astype(BF16)
    fg_ref[...] = lax.dot_general(
        grad_xw, w_ref[...], (((1,), (1,)), ((), ())), preferred_element_type=F32
    ).astype(BF16)


def call(kernel, outs, scratch=(), flops=TILE * F * F):
    return pl.pallas_call(
        kernel,
        out_shape=[jax.ShapeDtypeStruct(shape, dtype) for shape, dtype in outs],
        out_specs=[pl.BlockSpec(memory_space=pltpu.VMEM)] * len(outs),
        scratch_shapes=[pltpu.VMEM(shape, dtype) for shape, dtype in scratch],
        compiler_params=PARAMS,
        cost_estimate=pl.CostEstimate(
            flops=flops, bytes_accessed=2 * 1024 * 1024, transcendentals=0
        ),
    )


def exchange(array, axes):
    return lax.all_to_all(array, axes, 0, 0, tiled=True)


def swap(array, axis):
    return lax.ppermute(array, axis, [(0, 1), (1, 0)])


def per_device(
    features, weight, bias, node_scale, cotangent, edge_slot, edge_row, edge_col, tile_row
):
    h, c = lax.axis_index("h"), lax.axis_index("c")
    s = node_scale[None, :]
    bias = bias[None, :]

    slot = edge_slot.reshape(XY * H, EDGES)
    tiles = tile_row.reshape(XY * H, SLOTS)
    tile = sum(jnp.where(slot == k, tiles[:, k : k + 1], 0) for k in range(SLOTS))
    target = ((tile & 1) ^ c) * HALF + (tile >> 1) * TILE + edge_row.reshape(slot.shape)
    target = jnp.where(slot < SLOTS, target, -1)
    edges = jnp.stack([target, edge_col.reshape(slot.shape)]).reshape(2, XY, H, EDGES)
    kept = lax.dynamic_index_in_dim(edges, h, 2, keepdims=False)
    came = swap(lax.dynamic_index_in_dim(edges, 1 - h, 2, keepdims=False), "h")

    sources = exchange(spread(features, s), ("x", "y"))

    pairs = jnp.stack([jnp.where(h == 0, kept, came), jnp.where(h == 0, came, kept)], axis=1)
    lane = pairs.reshape(2 * H, E_ALL)
    sub = lane.T
    columns = jnp.concatenate([pairs[1, 0], pairs[1, 1]], axis=1)

    gathered, send = call(
        forward_send_kernel,
        [((H, E_ALL, F), BF16), ((H, HALF, F), BF16)],
        flops=4 * E_ALL * F * (HALF + TILE),
    )(sources, lane, sub)
    other = swap(send, "c")
    (mine,) = call(
        forward_keep_kernel, [((H, HALF, F), F32)], flops=4 * E_ALL * F * HALF
    )(gathered, lane)
    (partial,) = call(add_kernel, [((H, HALF, F), BF16)])(mine, other)
    partial = partial.reshape(ZN, TILE, F)
    partial = exchange(partial, ("h", "l"))
    act, g, w_parts = call(
        middle_kernel,
        [((TILE, F), BF16), ((TILE, F), BF16), ((XY, WR + BB, F), BF16)],
    )(partial, features, s, weight, bias, cotangent)
    w_parts = exchange(w_parts, ("x", "y"))
    (pay,) = call(load_kernel, [((ZN, ZCHUNK, F), BF16)])(w_parts, g)
    around = exchange(pay, ("h", "l"))
    other = swap(around, "c")
    picked, output = call(
        backward_mine_kernel,
        [((XY, H * EDGES, F), BF16), ((TILE, F), BF16)],
        [((HALF, F), BF16)],
        flops=4 * E_ALL * F * HALF,
    )(around, sub, act)
    terms, bias_sum = call(
        backward_kernel,
        [((XY, XCHUNK, F), BF16), ((1, F), F32)],
        [((HALF, F), BF16), ((XY, H * EDGES, F), BF16)],
        flops=4 * E_ALL * F * (HALF + TILE),
    )(picked, around, other, sub, columns)
    terms = exchange(terms, ("x", "y"))
    feature_grad, weight_grad, bias_grad = call(
        final_kernel, [((TILE, F), BF16), ((F, F), F32), ((1, F), F32)]
    )(terms, g, s, weight, bias_sum)
    return output, feature_grad, weight_grad, bias_grad.reshape(F)


def solution(mesh):
    fine = Mesh(mesh.devices.reshape(X, Y, H, L, C), ALL)
    rows, edges = P(ALL, None), P(("x", "y", "h"), ("l", "c"), None, None)
    return jax.shard_map(
        per_device,
        mesh=fine,
        in_specs=(rows, P(), P(), P(ALL), rows, edges, edges, edges, edges),
        out_specs=(rows, rows, P(), P()),
        check_vma=False,
    )
```

```python
import math

import jax
import jax.numpy as jnp
from jax import lax
from jax.experimental import pallas as pl
from jax.experimental.pallas import tpu as pltpu
from jax.sharding import Mesh, PartitionSpec as P

X, Y, H, L, C = 4, 4, 2, 4, 2
XY, ZN = X * Y, H * L
TILE, F, SLOTS, EDGES = 128, 256, 4, 96
HALF = L * TILE
ROWS = C * HALF
E_ALL = XY * EDGES
STEP = 4 * EDGES
COPIES = 4
WR, BB = F // XY, 8
ZCHUNK = TILE + WR + BB
XCHUNK = TILE + WR
F32, BF16, I32 = jnp.float32, jnp.bfloat16, jnp.int32
K0, K1 = math.sqrt(2.0 / math.pi), 0.044715
ALL = ("x", "y", "h", "l", "c")
PARAMS = pltpu.CompilerParams(vmem_limit_bytes=40 * 1024 * 1024)


def dot(a, b):
    return jnp.dot(a, b, preferred_element_type=F32)


def one_hot(index, shape, axis, base=0):
    return (index == lax.broadcasted_iota(I32, shape, axis) + base).astype(F32).astype(BF16)


def split_rows(row):
    high = row.astype(BF16).astype(F32)
    at = lax.broadcasted_iota(I32, (BB, F), 0)
    return jnp.where(at == 0, high, jnp.where(at == 1, row - high, 0.0)).astype(BF16)


def column(row):
    return jnp.transpose(jnp.broadcast_to(row, (TILE, TILE)))[:, :1]


def spread_kernel(x_ref, s_ref, out_ref, x, s, scaled, sems):
    loads = [
        pltpu.make_async_copy(x_ref, x, sems.at[0]),
        pltpu.make_async_copy(s_ref, s, sems.at[1]),
    ]
    for load in loads:
        load.start()
    for load in loads:
        load.wait()
    value = (column(s[...]) * x[...].astype(F32)).astype(BF16)
    for j in range(COPIES):
        scaled[j] = value
    stores = [
        pltpu.make_async_copy(scaled, out_ref.at[pl.ds(j * COPIES, COPIES)], sems.at[2 + j])
        for j in range(XY // COPIES)
    ]
    for store in stores:
        store.start()
    for store in stores:
        store.wait()


def spread(features, node_scale):
    return pl.pallas_call(
        spread_kernel,
        out_shape=jax.ShapeDtypeStruct((XY, TILE, F), BF16),
        in_specs=[pl.BlockSpec(memory_space=pltpu.HBM)] * 2,
        out_specs=pl.BlockSpec(memory_space=pltpu.HBM),
        scratch_shapes=[
            pltpu.VMEM((TILE, F), BF16),
            pltpu.VMEM((1, TILE), F32),
            pltpu.VMEM((COPIES, TILE, F), BF16),
            pltpu.SemaphoreType.DMA((2 + XY // COPIES,)),
        ],
        compiler_params=pltpu.CompilerParams(vmem_limit_bytes=63_480_000),
    )(features, node_scale)


def forward_send_kernel(x_ref, lane_ref, sub_ref, gathered_ref, send_ref):
    for j in range(XY):
        rows = pl.ds(j * EDGES, EDGES)
        picks = [
            one_hot(sub_ref[rows, H + b : H + b + 1], (EDGES, TILE), 1) for b in range(H)
        ]
        value = dot(jnp.concatenate(picks), x_ref[j]).astype(BF16)
        for b in range(H):
            gathered_ref[b, rows, :] = value[b * EDGES : (b + 1) * EDGES]
    for b in range(H):
        place = one_hot(lane_ref[b : b + 1, :], (HALF, E_ALL), 0, HALF)
        send_ref[b] = dot(place, gathered_ref[b]).astype(BF16)


def forward_keep_kernel(gathered_ref, lane_ref, mine_ref):
    for b in range(H):
        place = one_hot(lane_ref[b : b + 1, :], (HALF, E_ALL), 0)
        mine_ref[b] = dot(place, gathered_ref[b])


def add_kernel(mine_ref, other_ref, out_ref):
    out_ref[...] = (mine_ref[...] + other_ref[...].astype(F32)).astype(BF16)


def middle_kernel(part_ref, x_ref, s_ref, w_ref, bias_ref, ct_ref, out_ref, g_ref, wp_ref):
    s = column(s_ref[...])
    z = s * x_ref[...].astype(F32)
    for k in range(ZN):
        z += part_ref[k].astype(F32)
    z_high = z.astype(BF16)
    z_low = (z - z_high.astype(F32)).astype(BF16)
    w = w_ref[...]
    p = s * (dot(z_high, w) + dot(z_low, w)) + bias_ref[...]
    square = p * p
    th = jnp.tanh(K0 * (p + K1 * (p * square)))
    out_ref[...] = (0.5 * p * (1.0 + th)).astype(BF16)
    slope = 0.5 * (1.0 + th) + 0.5 * p * (1.0 - th * th) * (K0 * (1.0 + 3.0 * K1 * square))
    grad = ct_ref[...].astype(F32) * slope
    g = (s * grad).astype(BF16)
    g_ref[...] = g
    first = (((0,), (0,)), ((), ()))
    wg = lax.dot_general(z_high, g, first, preferred_element_type=F32)
    wg += lax.dot_general(z_low, g, first, preferred_element_type=F32)
    bias_rows = split_rows(jnp.sum(grad, axis=0, keepdims=True))
    for k in range(XY):
        wp_ref[k, pl.ds(0, WR), :] = wg[k * WR : (k + 1) * WR].astype(BF16)
        wp_ref[k, pl.ds(WR, BB), :] = bias_rows


def load_kernel(w_ref, g_ref, pay_ref):
    tail = jnp.zeros((WR + BB, F), F32)
    for k in range(XY):
        tail += w_ref[k].astype(F32)
    own = tail[:WR].astype(BF16)
    bias_rows = split_rows(jnp.sum(tail[WR:], axis=0, keepdims=True))
    g = g_ref[...]
    for k in range(ZN):
        pay_ref[k, pl.ds(0, TILE), :] = g
        pay_ref[k, pl.ds(TILE, WR), :] = own
        pay_ref[k, pl.ds(TILE + WR, BB), :] = bias_rows


def backward_mine_kernel(mine_ref, sub_ref, act_ref, picked_ref, out_ref, grads):
    out_ref[...] = act_ref[...]
    for b in range(H):
        for k in range(L):
            grads[pl.ds(k * TILE, TILE), :] = mine_ref[b * L + k, pl.ds(0, TILE), :]
        for m in range(E_ALL // STEP):
            pick = one_hot(sub_ref[pl.ds(m * STEP, STEP), b : b + 1], (STEP, HALF), 1)
            value = dot(pick, grads[...]).astype(BF16)
            for q in range(STEP // EDGES):
                picked_ref[m * (STEP // EDGES) + q, pl.ds(b * EDGES, EDGES), :] = value[
                    q * EDGES : (q + 1) * EDGES
                ]


def backward_kernel(
    picked_ref, mine_ref, other_ref, sub_ref, col_ref, pay_ref, bias_ref, grads, picked
):
    factor = 1.0 / math.sqrt(XY * ZN * C * TILE)
    tail_mine = jnp.zeros((WR + BB, F), F32)
    tail_other = jnp.zeros((WR + BB, F), F32)
    for k in range(ZN):
        rows = pl.ds(TILE, WR + BB)
        tail_mine += mine_ref[k, rows, :].astype(F32)
        tail_other += other_ref[k, rows, :].astype(F32)
    tail = (tail_mine + tail_other) * factor
    own = tail[:WR].astype(BF16)
    bias_ref[...] = jnp.sum(tail[WR:], axis=0, keepdims=True)
    for b in range(H):
        for k in range(L):
            grads[pl.ds(k * TILE, TILE), :] = other_ref[b * L + k, pl.ds(0, TILE), :]
        for m in range(E_ALL // STEP):
            pick = one_hot(sub_ref[pl.ds(m * STEP, STEP), b : b + 1], (STEP, HALF), 1, HALF)
            value = dot(pick, grads[...])
            for q in range(STEP // EDGES):
                j, rows = m * (STEP // EDGES) + q, pl.ds(b * EDGES, EDGES)
                both = value[q * EDGES : (q + 1) * EDGES] + picked_ref[j, rows, :].astype(F32)
                picked[j, rows, :] = both.astype(BF16)
    for j in range(XY):
        place = one_hot(col_ref[j : j + 1, :], (TILE, H * EDGES), 0)
        total = dot(place, picked[j])
        pay_ref[j, pl.ds(0, TILE), :] = total.astype(BF16)
        pay_ref[j, pl.ds(TILE, WR), :] = own


def final_kernel(part_ref, g_ref, s_ref, w_ref, bias_ref, fg_ref, wg_ref, out_ref):
    out_ref[...] = bias_ref[...]
    back = g_ref[...].astype(F32)
    for k in range(XY):
        back += part_ref[k, pl.ds(0, TILE), :].astype(F32)
        wg_ref[pl.ds(k * WR, WR), :] = part_ref[k, pl.ds(TILE, WR), :].astype(F32)
    grad_xw = (column(s_ref[...]) * back).astype(BF16)
    fg_ref[...] = lax.dot_general(
        grad_xw, w_ref[...], (((1,), (1,)), ((), ())), preferred_element_type=F32
    ).astype(BF16)


def call(kernel, outs, scratch=(), flops=TILE * F * F):
    return pl.pallas_call(
        kernel,
        out_shape=[jax.ShapeDtypeStruct(shape, dtype) for shape, dtype in outs],
        out_specs=[pl.BlockSpec(memory_space=pltpu.VMEM)] * len(outs),
        scratch_shapes=[pltpu.VMEM(shape, dtype) for shape, dtype in scratch],
        compiler_params=PARAMS,
        cost_estimate=pl.CostEstimate(
            flops=flops, bytes_accessed=2 * 1024 * 1024, transcendentals=0
        ),
    )


def exchange(array, axes):
    return lax.all_to_all(array, axes, 0, 0, tiled=True)


def swap(array, axis):
    return lax.ppermute(array, axis, [(0, 1), (1, 0)])


def per_device(
    features, weight, bias, node_scale, cotangent, edge_slot, edge_row, edge_col, tile_row
):
    h, c = lax.axis_index("h"), lax.axis_index("c")
    s = node_scale[None, :]
    bias = bias[None, :]

    slot = edge_slot.reshape(XY * H, EDGES)
    tiles = tile_row.reshape(XY * H, SLOTS)
    tile = sum(jnp.where(slot == k, tiles[:, k : k + 1], 0) for k in range(SLOTS))
    target = ((tile & 1) ^ c) * HALF + (tile >> 1) * TILE + edge_row.reshape(slot.shape)
    target = jnp.where(slot < SLOTS, target, -1)
    edges = jnp.stack([target, edge_col.reshape(slot.shape)]).reshape(2, XY, H, EDGES)
    kept = lax.dynamic_index_in_dim(edges, h, 2, keepdims=False)
    came = swap(lax.dynamic_index_in_dim(edges, 1 - h, 2, keepdims=False), "h")

    sources = exchange(spread(features, s), ("x", "y"))

    pairs = jnp.stack([jnp.where(h == 0, kept, came), jnp.where(h == 0, came, kept)], axis=1)
    lane = pairs.reshape(2 * H, E_ALL)
    sub = lane.T
    columns = jnp.concatenate([pairs[1, 0], pairs[1, 1]], axis=1)

    gathered, send = call(
        forward_send_kernel,
        [((H, E_ALL, F), BF16), ((H, HALF, F), BF16)],
        flops=4 * E_ALL * F * (HALF + TILE),
    )(sources, lane, sub)
    other = swap(send, "c")
    (mine,) = call(
        forward_keep_kernel, [((H, HALF, F), F32)], flops=4 * E_ALL * F * HALF
    )(gathered, lane)
    (partial,) = call(add_kernel, [((H, HALF, F), BF16)])(mine, other)
    partial = partial.reshape(ZN, TILE, F)
    partial = exchange(partial, ("h", "l"))
    act, g, w_parts = call(
        middle_kernel,
        [((TILE, F), BF16), ((TILE, F), BF16), ((XY, WR + BB, F), BF16)],
    )(partial, features, s, weight, bias, cotangent)
    w_parts = exchange(w_parts, ("x", "y"))
    (pay,) = call(load_kernel, [((ZN, ZCHUNK, F), BF16)])(w_parts, g)
    around = exchange(pay, ("h", "l"))
    other = swap(around, "c")
    picked, output = call(
        backward_mine_kernel,
        [((XY, H * EDGES, F), BF16), ((TILE, F), BF16)],
        [((HALF, F), BF16)],
        flops=4 * E_ALL * F * HALF,
    )(around, sub, act)
    terms, bias_sum = call(
        backward_kernel,
        [((XY, XCHUNK, F), BF16), ((1, F), F32)],
        [((HALF, F), BF16), ((XY, H * EDGES, F), BF16)],
        flops=4 * E_ALL * F * (HALF + TILE),
    )(picked, around, other, sub, columns)
    terms = exchange(terms, ("x", "y"))
    feature_grad, weight_grad, bias_grad = call(
        final_kernel, [((TILE, F), BF16), ((F, F), F32), ((1, F), F32)]
    )(terms, g, s, weight, bias_sum)
    return output, feature_grad, weight_grad, bias_grad.reshape(F)


def solution(mesh):
    fine = Mesh(mesh.devices.reshape(X, Y, H, L, C), ALL)
    rows, edges = P(ALL, None), P(("x", "y", "h"), ("l", "c"), None, None)
    return jax.shard_map(
        per_device,
        mesh=fine,
        in_specs=(rows, P(), P(), P(ALL), rows, edges, edges, edges, edges),
        out_specs=(rows, rows, P(), P()),
        check_vma=False,
    )
```

```python
import math

import jax
import jax.numpy as jnp
from jax import lax
from jax.experimental import pallas as pl
from jax.experimental.pallas import tpu as pltpu
from jax.sharding import Mesh, PartitionSpec as P

X, Y, H, L, C = 4, 4, 2, 4, 2
XY, ZN = X * Y, H * L
TILE, F, SLOTS, EDGES = 128, 256, 4, 96
HALF = L * TILE
ROWS = C * HALF
E_ALL = XY * EDGES
STEP = 4 * EDGES
WR, BB = F // XY, 8
ZCHUNK = TILE + WR + BB
XCHUNK = TILE + WR
F32, BF16, I32 = jnp.float32, jnp.bfloat16, jnp.int32
K0, K1 = math.sqrt(2.0 / math.pi), 0.044715
ALL = ("x", "y", "h", "l", "c")
PARAMS = pltpu.CompilerParams(vmem_limit_bytes=40 * 1024 * 1024)


def dot(a, b):
    return jnp.dot(a, b, preferred_element_type=F32)


def one_hot(index, shape, axis, base=0):
    return (index == lax.broadcasted_iota(I32, shape, axis) + base).astype(F32).astype(BF16)


def split_rows(row):
    high = row.astype(BF16).astype(F32)
    at = lax.broadcasted_iota(I32, (BB, F), 0)
    return jnp.where(at == 0, high, jnp.where(at == 1, row - high, 0.0)).astype(BF16)


def column(row):
    return jnp.transpose(jnp.broadcast_to(row, (TILE, TILE)))[:, :1]


def forward_send_kernel(x_ref, lane_ref, sub_ref, gathered_ref, send_ref):
    for j in range(XY):
        rows = pl.ds(j * EDGES, EDGES)
        picks = [
            one_hot(sub_ref[rows, H + b : H + b + 1], (EDGES, TILE), 1) for b in range(H)
        ]
        value = dot(jnp.concatenate(picks), x_ref[j]).astype(BF16)
        for b in range(H):
            gathered_ref[b, rows, :] = value[b * EDGES : (b + 1) * EDGES]
    for b in range(H):
        place = one_hot(lane_ref[b : b + 1, :], (HALF, E_ALL), 0, HALF)
        send_ref[b] = dot(place, gathered_ref[b]).astype(BF16)


def forward_keep_kernel(gathered_ref, lane_ref, mine_ref):
    for b in range(H):
        place = one_hot(lane_ref[b : b + 1, :], (HALF, E_ALL), 0)
        mine_ref[b] = dot(place, gathered_ref[b])


def add_kernel(mine_ref, other_ref, out_ref):
    out_ref[...] = (mine_ref[...] + other_ref[...].astype(F32)).astype(BF16)


def middle_kernel(part_ref, x_ref, s_ref, w_ref, bias_ref, ct_ref, out_ref, g_ref, wp_ref):
    s = column(s_ref[...])
    z = s * x_ref[...].astype(F32)
    for k in range(ZN):
        z += part_ref[k].astype(F32)
    z_high = z.astype(BF16)
    z_low = (z - z_high.astype(F32)).astype(BF16)
    w = w_ref[...]
    p = s * (dot(z_high, w) + dot(z_low, w)) + bias_ref[...]
    square = p * p
    th = jnp.tanh(K0 * (p + K1 * (p * square)))
    out_ref[...] = (0.5 * p * (1.0 + th)).astype(BF16)
    slope = 0.5 * (1.0 + th) + 0.5 * p * (1.0 - th * th) * (K0 * (1.0 + 3.0 * K1 * square))
    grad = ct_ref[...].astype(F32) * slope
    g = (s * grad).astype(BF16)
    g_ref[...] = g
    first = (((0,), (0,)), ((), ()))
    wg = lax.dot_general(z_high, g, first, preferred_element_type=F32)
    wg += lax.dot_general(z_low, g, first, preferred_element_type=F32)
    bias_rows = split_rows(jnp.sum(grad, axis=0, keepdims=True))
    for k in range(XY):
        wp_ref[k, pl.ds(0, WR), :] = wg[k * WR : (k + 1) * WR].astype(BF16)
        wp_ref[k, pl.ds(WR, BB), :] = bias_rows


def load_kernel(w_ref, g_ref, pay_ref):
    tail = jnp.zeros((WR + BB, F), F32)
    for k in range(XY):
        tail += w_ref[k].astype(F32)
    own = tail[:WR].astype(BF16)
    bias_rows = split_rows(jnp.sum(tail[WR:], axis=0, keepdims=True))
    g = g_ref[...]
    for k in range(ZN):
        pay_ref[k, pl.ds(0, TILE), :] = g
        pay_ref[k, pl.ds(TILE, WR), :] = own
        pay_ref[k, pl.ds(TILE + WR, BB), :] = bias_rows


def backward_mine_kernel(mine_ref, sub_ref, act_ref, picked_ref, out_ref, grads):
    out_ref[...] = act_ref[...]
    for b in range(H):
        for k in range(L):
            grads[pl.ds(k * TILE, TILE), :] = mine_ref[b * L + k, pl.ds(0, TILE), :]
        for m in range(E_ALL // STEP):
            pick = one_hot(sub_ref[pl.ds(m * STEP, STEP), b : b + 1], (STEP, HALF), 1)
            value = dot(pick, grads[...]).astype(BF16)
            for q in range(STEP // EDGES):
                picked_ref[m * (STEP // EDGES) + q, pl.ds(b * EDGES, EDGES), :] = value[
                    q * EDGES : (q + 1) * EDGES
                ]


def backward_kernel(
    picked_ref, mine_ref, other_ref, sub_ref, col_ref, pay_ref, bias_ref, grads, picked
):
    factor = 1.0 / math.sqrt(XY * ZN * C * TILE)
    tail_mine = jnp.zeros((WR + BB, F), F32)
    tail_other = jnp.zeros((WR + BB, F), F32)
    for k in range(ZN):
        rows = pl.ds(TILE, WR + BB)
        tail_mine += mine_ref[k, rows, :].astype(F32)
        tail_other += other_ref[k, rows, :].astype(F32)
    tail = (tail_mine + tail_other) * factor
    own = tail[:WR].astype(BF16)
    bias_ref[...] = jnp.sum(tail[WR:], axis=0, keepdims=True)
    for b in range(H):
        for k in range(L):
            grads[pl.ds(k * TILE, TILE), :] = other_ref[b * L + k, pl.ds(0, TILE), :]
        for m in range(E_ALL // STEP):
            pick = one_hot(sub_ref[pl.ds(m * STEP, STEP), b : b + 1], (STEP, HALF), 1, HALF)
            value = dot(pick, grads[...])
            for q in range(STEP // EDGES):
                j, rows = m * (STEP // EDGES) + q, pl.ds(b * EDGES, EDGES)
                both = value[q * EDGES : (q + 1) * EDGES] + picked_ref[j, rows, :].astype(F32)
                picked[j, rows, :] = both.astype(BF16)
    for j in range(XY):
        place = one_hot(col_ref[j : j + 1, :], (TILE, H * EDGES), 0)
        total = dot(place, picked[j])
        pay_ref[j, pl.ds(0, TILE), :] = total.astype(BF16)
        pay_ref[j, pl.ds(TILE, WR), :] = own


def final_kernel(part_ref, g_ref, s_ref, w_ref, bias_ref, fg_ref, wg_ref, out_ref):
    out_ref[...] = bias_ref[...]
    back = g_ref[...].astype(F32)
    for k in range(XY):
        back += part_ref[k, pl.ds(0, TILE), :].astype(F32)
        wg_ref[pl.ds(k * WR, WR), :] = part_ref[k, pl.ds(TILE, WR), :].astype(F32)
    grad_xw = (column(s_ref[...]) * back).astype(BF16)
    fg_ref[...] = lax.dot_general(
        grad_xw, w_ref[...], (((1,), (1,)), ((), ())), preferred_element_type=F32
    ).astype(BF16)


def call(kernel, outs, scratch=(), flops=TILE * F * F):
    return pl.pallas_call(
        kernel,
        out_shape=[jax.ShapeDtypeStruct(shape, dtype) for shape, dtype in outs],
        out_specs=[pl.BlockSpec(memory_space=pltpu.VMEM)] * len(outs),
        scratch_shapes=[pltpu.VMEM(shape, dtype) for shape, dtype in scratch],
        compiler_params=PARAMS,
        cost_estimate=pl.CostEstimate(
            flops=flops, bytes_accessed=2 * 1024 * 1024, transcendentals=0
        ),
    )


def exchange(array, axes):
    return lax.all_to_all(array, axes, 0, 0, tiled=True)


def swap(array, axis):
    return lax.ppermute(array, axis, [(0, 1), (1, 0)])


def per_device(
    features, weight, bias, node_scale, cotangent, edge_slot, edge_row, edge_col, tile_row
):
    h, c = lax.axis_index("h"), lax.axis_index("c")
    s = node_scale[None, :]
    bias = bias[None, :]

    slot = edge_slot.reshape(XY * H, EDGES)
    tiles = tile_row.reshape(XY * H, SLOTS)
    tile = sum(jnp.where(slot == k, tiles[:, k : k + 1], 0) for k in range(SLOTS))
    target = ((tile & 1) ^ c) * HALF + (tile >> 1) * TILE + edge_row.reshape(slot.shape)
    target = jnp.where(slot < SLOTS, target, -1)
    edges = jnp.stack([target, edge_col.reshape(slot.shape)]).reshape(2, XY, H, EDGES)
    kept = lax.dynamic_index_in_dim(edges, h, 2, keepdims=False)
    came = swap(lax.dynamic_index_in_dim(edges, 1 - h, 2, keepdims=False), "h")

    scaled = (node_scale[:, None] * features.astype(F32)).astype(BF16)
    copies = jnp.concatenate([scaled] * XY).reshape(XY, TILE, F)
    sources = exchange(copies, ("x", "y"))

    pairs = jnp.stack([jnp.where(h == 0, kept, came), jnp.where(h == 0, came, kept)], axis=1)
    lane = pairs.reshape(2 * H, E_ALL)
    sub = lane.T
    columns = jnp.concatenate([pairs[1, 0], pairs[1, 1]], axis=1)

    gathered, send = call(
        forward_send_kernel,
        [((H, E_ALL, F), BF16), ((H, HALF, F), BF16)],
        flops=4 * E_ALL * F * (HALF + TILE),
    )(sources, lane, sub)
    other = swap(send, "c")
    (mine,) = call(
        forward_keep_kernel, [((H, HALF, F), F32)], flops=4 * E_ALL * F * HALF
    )(gathered, lane)
    (partial,) = call(add_kernel, [((H, HALF, F), BF16)])(mine, other)
    partial = partial.reshape(ZN, TILE, F)
    partial = exchange(partial, ("h", "l"))
    act, g, w_parts = call(
        middle_kernel,
        [((TILE, F), BF16), ((TILE, F), BF16), ((XY, WR + BB, F), BF16)],
    )(partial, features, s, weight, bias, cotangent)
    w_parts = exchange(w_parts, ("x", "y"))
    (pay,) = call(load_kernel, [((ZN, ZCHUNK, F), BF16)])(w_parts, g)
    around = exchange(pay, ("h", "l"))
    other = swap(around, "c")
    picked, output = call(
        backward_mine_kernel,
        [((XY, H * EDGES, F), BF16), ((TILE, F), BF16)],
        [((HALF, F), BF16)],
        flops=4 * E_ALL * F * HALF,
    )(around, sub, act)
    terms, bias_sum = call(
        backward_kernel,
        [((XY, XCHUNK, F), BF16), ((1, F), F32)],
        [((HALF, F), BF16), ((XY, H * EDGES, F), BF16)],
        flops=4 * E_ALL * F * (HALF + TILE),
    )(picked, around, other, sub, columns)
    terms = exchange(terms, ("x", "y"))
    feature_grad, weight_grad, bias_grad = call(
        final_kernel, [((TILE, F), BF16), ((F, F), F32), ((1, F), F32)]
    )(terms, g, s, weight, bias_sum)
    return output, feature_grad, weight_grad, bias_grad.reshape(F)


def solution(mesh):
    fine = Mesh(mesh.devices.reshape(X, Y, H, L, C), ALL)
    rows, edges = P(ALL, None), P(("x", "y", "h"), ("l", "c"), None, None)
    return jax.shard_map(
        per_device,
        mesh=fine,
        in_specs=(rows, P(), P(), P(ALL), rows, edges, edges, edges, edges),
        out_specs=(rows, rows, P(), P()),
        check_vma=False,
    )
```

```python
import math

import jax
import jax.numpy as jnp
from jax import lax
from jax.experimental import pallas as pl
from jax.experimental.pallas import tpu as pltpu
from jax.sharding import Mesh, PartitionSpec as P

X, Y, H, L, C = 4, 4, 2, 4, 2
XY, ZN = X * Y, H * L
TILE, F, SLOTS, EDGES = 128, 256, 4, 96
HALF = L * TILE
ROWS = C * HALF
E_ALL = XY * EDGES
STEP = 4 * EDGES
COPIES = 4
WR, BB = F // XY, 8
ZCHUNK = TILE + WR + BB
XCHUNK = TILE + WR
F32, BF16, I32 = jnp.float32, jnp.bfloat16, jnp.int32
K0, K1 = math.sqrt(2.0 / math.pi), 0.044715
ALL = ("x", "y", "h", "l", "c")
PARAMS = pltpu.CompilerParams(vmem_limit_bytes=40 * 1024 * 1024)


def dot(a, b):
    return jnp.dot(a, b, preferred_element_type=F32)


def one_hot(index, shape, axis, base=0):
    return (index == lax.broadcasted_iota(I32, shape, axis) + base).astype(F32).astype(BF16)


def split_rows(row):
    high = row.astype(BF16).astype(F32)
    at = lax.broadcasted_iota(I32, (BB, F), 0)
    return jnp.where(at == 0, high, jnp.where(at == 1, row - high, 0.0)).astype(BF16)


def column(row):
    return jnp.transpose(jnp.broadcast_to(row, (TILE, TILE)))[:, :1]


def spread_kernel(x_ref, s_ref, out_ref, x, s, scaled, sems):
    loads = [
        pltpu.make_async_copy(x_ref, x, sems.at[0]),
        pltpu.make_async_copy(s_ref, s, sems.at[1]),
    ]
    for load in loads:
        load.start()
    for load in loads:
        load.wait()
    value = (column(s[...]) * x[...].astype(F32)).astype(BF16)
    for j in range(COPIES):
        scaled[j] = value
    stores = [
        pltpu.make_async_copy(scaled, out_ref.at[pl.ds(j * COPIES, COPIES)], sems.at[2 + j])
        for j in range(XY // COPIES)
    ]
    for store in stores:
        store.start()
    for store in stores:
        store.wait()


def spread(features, node_scale):
    return pl.pallas_call(
        spread_kernel,
        out_shape=jax.ShapeDtypeStruct((XY, TILE, F), BF16),
        in_specs=[pl.BlockSpec(memory_space=pltpu.HBM)] * 2,
        out_specs=pl.BlockSpec(memory_space=pltpu.HBM),
        scratch_shapes=[
            pltpu.VMEM((TILE, F), BF16),
            pltpu.VMEM((1, TILE), F32),
            pltpu.VMEM((COPIES, TILE, F), BF16),
            pltpu.SemaphoreType.DMA((2 + XY // COPIES,)),
        ],
        compiler_params=pltpu.CompilerParams(vmem_limit_bytes=63_480_000),
    )(features, node_scale)


def forward_send_kernel(x_ref, lane_ref, sub_ref, gathered_ref, send_ref):
    for j in range(XY):
        rows = pl.ds(j * EDGES, EDGES)
        picks = [
            one_hot(sub_ref[rows, H + b : H + b + 1], (EDGES, TILE), 1) for b in range(H)
        ]
        value = dot(jnp.concatenate(picks), x_ref[j]).astype(BF16)
        for b in range(H):
            gathered_ref[b, rows, :] = value[b * EDGES : (b + 1) * EDGES]
    for b in range(H):
        place = one_hot(lane_ref[b : b + 1, :], (HALF, E_ALL), 0, HALF)
        send_ref[b] = dot(place, gathered_ref[b]).astype(BF16)


def forward_keep_kernel(gathered_ref, lane_ref, mine_ref):
    for b in range(H):
        place = one_hot(lane_ref[b : b + 1, :], (HALF, E_ALL), 0)
        mine_ref[b] = dot(place, gathered_ref[b])


def add_kernel(mine_ref, other_ref, out_ref):
    out_ref[...] = (mine_ref[...] + other_ref[...].astype(F32)).astype(BF16)


def middle_kernel(part_ref, x_ref, s_ref, w_ref, bias_ref, ct_ref, out_ref, g_ref, wp_ref):
    s = column(s_ref[...])
    z = s * x_ref[...].astype(F32)
    for k in range(ZN):
        z += part_ref[k].astype(F32)
    z_high = z.astype(BF16)
    z_low = (z - z_high.astype(F32)).astype(BF16)
    w = w_ref[...]
    p = s * (dot(z_high, w) + dot(z_low, w)) + bias_ref[...]
    square = p * p
    th = jnp.tanh(K0 * (p + K1 * (p * square)))
    out_ref[...] = (0.5 * p * (1.0 + th)).astype(BF16)
    slope = 0.5 * (1.0 + th) + 0.5 * p * (1.0 - th * th) * (K0 * (1.0 + 3.0 * K1 * square))
    grad = ct_ref[...].astype(F32) * slope
    g = (s * grad).astype(BF16)
    g_ref[...] = g
    first = (((0,), (0,)), ((), ()))
    wg = lax.dot_general(z_high, g, first, preferred_element_type=F32)
    wg += lax.dot_general(z_low, g, first, preferred_element_type=F32)
    bias_rows = split_rows(jnp.sum(grad, axis=0, keepdims=True))
    for k in range(XY):
        wp_ref[k, pl.ds(0, WR), :] = wg[k * WR : (k + 1) * WR].astype(BF16)
        wp_ref[k, pl.ds(WR, BB), :] = bias_rows


def load_kernel(w_ref, g_ref, pay_ref):
    tail = jnp.zeros((WR + BB, F), F32)
    for k in range(XY):
        tail += w_ref[k].astype(F32)
    own = tail[:WR].astype(BF16)
    bias_rows = split_rows(jnp.sum(tail[WR:], axis=0, keepdims=True))
    g = g_ref[...]
    for k in range(ZN):
        pay_ref[k, pl.ds(0, TILE), :] = g
        pay_ref[k, pl.ds(TILE, WR), :] = own
        pay_ref[k, pl.ds(TILE + WR, BB), :] = bias_rows


def backward_mine_kernel(mine_ref, sub_ref, col_ref, picked_ref, place_ref, tail_ref, grads):
    tail = jnp.zeros((WR + BB, F), F32)
    for k in range(ZN):
        tail += mine_ref[k, pl.ds(TILE, WR + BB), :].astype(F32)
    tail_ref[...] = tail
    for b in range(H):
        for k in range(L):
            grads[pl.ds(k * TILE, TILE), :] = mine_ref[b * L + k, pl.ds(0, TILE), :]
        for m in range(E_ALL // STEP):
            pick = one_hot(sub_ref[pl.ds(m * STEP, STEP), b : b + 1], (STEP, HALF), 1)
            value = dot(pick, grads[...]).astype(BF16)
            for q in range(STEP // EDGES):
                picked_ref[m * (STEP // EDGES) + q, pl.ds(b * EDGES, EDGES), :] = value[
                    q * EDGES : (q + 1) * EDGES
                ]
    for j in range(XY):
        place_ref[j] = one_hot(col_ref[j : j + 1, :], (TILE, H * EDGES), 0)


def backward_kernel(
    picked_ref, tail_ref, other_ref, sub_ref, place_ref, pay_ref, bias_ref, grads, picked
):
    factor = 1.0 / math.sqrt(XY * ZN * C * TILE)
    tail_other = jnp.zeros((WR + BB, F), F32)
    for k in range(ZN):
        tail_other += other_ref[k, pl.ds(TILE, WR + BB), :].astype(F32)
    tail = (tail_ref[...] + tail_other) * factor
    own = tail[:WR].astype(BF16)
    bias_ref[...] = jnp.sum(tail[WR:], axis=0, keepdims=True)
    for b in range(H):
        for k in range(L):
            grads[pl.ds(k * TILE, TILE), :] = other_ref[b * L + k, pl.ds(0, TILE), :]
        for m in range(E_ALL // STEP):
            pick = one_hot(sub_ref[pl.ds(m * STEP, STEP), b : b + 1], (STEP, HALF), 1, HALF)
            value = dot(pick, grads[...])
            for q in range(STEP // EDGES):
                j, rows = m * (STEP // EDGES) + q, pl.ds(b * EDGES, EDGES)
                both = value[q * EDGES : (q + 1) * EDGES] + picked_ref[j, rows, :].astype(F32)
                picked[j, rows, :] = both.astype(BF16)
    for j in range(XY):
        total = dot(place_ref[j], picked[j])
        pay_ref[j, pl.ds(0, TILE), :] = total.astype(BF16)
        pay_ref[j, pl.ds(TILE, WR), :] = own


def final_kernel(
    part_ref, g_ref, s_ref, w_ref, bias_in, act_ref, fg_ref, wg_ref, bias_ref, out_ref
):
    bias_ref[...] = bias_in[...]
    out_ref[...] = act_ref[...]
    back = g_ref[...].astype(F32)
    for k in range(XY):
        back += part_ref[k, pl.ds(0, TILE), :].astype(F32)
        wg_ref[pl.ds(k * WR, WR), :] = part_ref[k, pl.ds(TILE, WR), :].astype(F32)
    grad_xw = (column(s_ref[...]) * back).astype(BF16)
    fg_ref[...] = lax.dot_general(
        grad_xw, w_ref[...], (((1,), (1,)), ((), ())), preferred_element_type=F32
    ).astype(BF16)


def call(kernel, outs, scratch=(), flops=TILE * F * F):
    return pl.pallas_call(
        kernel,
        out_shape=[jax.ShapeDtypeStruct(shape, dtype) for shape, dtype in outs],
        out_specs=[pl.BlockSpec(memory_space=pltpu.VMEM)] * len(outs),
        scratch_shapes=[pltpu.VMEM(shape, dtype) for shape, dtype in scratch],
        compiler_params=PARAMS,
        cost_estimate=pl.CostEstimate(
            flops=flops, bytes_accessed=2 * 1024 * 1024, transcendentals=0
        ),
    )


def exchange(array, axes):
    return lax.all_to_all(array, axes, 0, 0, tiled=True)


def swap(array, axis):
    return lax.ppermute(array, axis, [(0, 1), (1, 0)])


def per_device(
    features, weight, bias, node_scale, cotangent, edge_slot, edge_row, edge_col, tile_row
):
    h, c = lax.axis_index("h"), lax.axis_index("c")
    s = node_scale[None, :]
    bias = bias[None, :]

    slot = edge_slot.reshape(XY * H, EDGES)
    tiles = tile_row.reshape(XY * H, SLOTS)
    tile = sum(jnp.where(slot == k, tiles[:, k : k + 1], 0) for k in range(SLOTS))
    target = ((tile & 1) ^ c) * HALF + (tile >> 1) * TILE + edge_row.reshape(slot.shape)
    target = jnp.where(slot < SLOTS, target, -1)
    edges = jnp.stack([target, edge_col.reshape(slot.shape)]).reshape(2, XY, H, EDGES)
    kept = lax.dynamic_index_in_dim(edges, h, 2, keepdims=False)
    came = swap(lax.dynamic_index_in_dim(edges, 1 - h, 2, keepdims=False), "h")

    sources = exchange(spread(features, s), ("x", "y"))

    pairs = jnp.stack([jnp.where(h == 0, kept, came), jnp.where(h == 0, came, kept)], axis=1)
    lane = pairs.reshape(2 * H, E_ALL)
    sub = lane.T
    columns = jnp.concatenate([pairs[1, 0], pairs[1, 1]], axis=1)

    gathered, send = call(
        forward_send_kernel,
        [((H, E_ALL, F), BF16), ((H, HALF, F), BF16)],
        flops=4 * E_ALL * F * (HALF + TILE),
    )(sources, lane, sub)
    other = swap(send, "c")
    (mine,) = call(
        forward_keep_kernel, [((H, HALF, F), F32)], flops=4 * E_ALL * F * HALF
    )(gathered, lane)
    (partial,) = call(add_kernel, [((H, HALF, F), BF16)])(mine, other)
    partial = partial.reshape(ZN, TILE, F)
    partial = exchange(partial, ("h", "l"))
    act, g, w_parts = call(
        middle_kernel,
        [((TILE, F), BF16), ((TILE, F), BF16), ((XY, WR + BB, F), BF16)],
    )(partial, features, s, weight, bias, cotangent)
    w_parts = exchange(w_parts, ("x", "y"))
    (pay,) = call(load_kernel, [((ZN, ZCHUNK, F), BF16)])(w_parts, g)
    around = exchange(pay, ("h", "l"))
    other = swap(around, "c")
    picked, places, tail = call(
        backward_mine_kernel,
        [((XY, H * EDGES, F), BF16), ((XY, TILE, H * EDGES), BF16), ((WR + BB, F), F32)],
        [((HALF, F), BF16)],
        flops=4 * E_ALL * F * HALF,
    )(around, sub, columns)
    terms, bias_sum = call(
        backward_kernel,
        [((XY, XCHUNK, F), BF16), ((1, F), F32)],
        [((HALF, F), BF16), ((XY, H * EDGES, F), BF16)],
        flops=4 * E_ALL * F * (HALF + TILE),
    )(picked, tail, other, sub, places)
    terms = exchange(terms, ("x", "y"))
    feature_grad, weight_grad, bias_grad, output = call(
        final_kernel, [((TILE, F), BF16), ((F, F), F32), ((1, F), F32), ((TILE, F), BF16)]
    )(terms, g, s, weight, bias_sum, act)
    return output, feature_grad, weight_grad, bias_grad.reshape(F)


def solution(mesh):
    fine = Mesh(mesh.devices.reshape(X, Y, H, L, C), ALL)
    rows, edges = P(ALL, None), P(("x", "y", "h"), ("l", "c"), None, None)
    return jax.shard_map(
        per_device,
        mesh=fine,
        in_specs=(rows, P(), P(), P(ALL), rows, edges, edges, edges, edges),
        out_specs=(rows, rows, P(), P()),
        check_vma=False,
    )
```

```python
import math

import jax
import jax.numpy as jnp
from jax import lax
from jax.experimental import pallas as pl
from jax.experimental.pallas import tpu as pltpu
from jax.sharding import Mesh, PartitionSpec as P

X, Y, H, L, C = 4, 4, 2, 4, 2
XY, ZN = X * Y, H * L
TILE, F, SLOTS, EDGES = 128, 256, 4, 96
HALF = L * TILE
ROWS = C * HALF
E_ALL = XY * EDGES
STEP = 4 * EDGES
COPIES = 4
WR, BB = F // XY, 8
ZCHUNK = TILE + WR + BB
XCHUNK = TILE + WR
F32, BF16, I32 = jnp.float32, jnp.bfloat16, jnp.int32
K0, K1 = math.sqrt(2.0 / math.pi), 0.044715
ALL = ("x", "y", "h", "l", "c")
PARAMS = pltpu.CompilerParams(vmem_limit_bytes=40 * 1024 * 1024)


def dot(a, b):
    return jnp.dot(a, b, preferred_element_type=F32)


def one_hot(index, shape, axis, base=0):
    return (index == lax.broadcasted_iota(I32, shape, axis) + base).astype(F32).astype(BF16)


def split_rows(row):
    high = row.astype(BF16).astype(F32)
    at = lax.broadcasted_iota(I32, (BB, F), 0)
    return jnp.where(at == 0, high, jnp.where(at == 1, row - high, 0.0)).astype(BF16)


def column(row):
    return jnp.transpose(jnp.broadcast_to(row, (TILE, TILE)))[:, :1]


def spread_kernel(x_ref, s_ref, out_ref, x, s, scaled, sems):
    loads = [
        pltpu.make_async_copy(x_ref, x, sems.at[0]),
        pltpu.make_async_copy(s_ref, s, sems.at[1]),
    ]
    for load in loads:
        load.start()
    for load in loads:
        load.wait()
    value = (column(s[...]) * x[...].astype(F32)).astype(BF16)
    for j in range(COPIES):
        scaled[j] = value
    stores = [
        pltpu.make_async_copy(scaled, out_ref.at[pl.ds(j * COPIES, COPIES)], sems.at[2 + j])
        for j in range(XY // COPIES)
    ]
    for store in stores:
        store.start()
    for store in stores:
        store.wait()


def spread(features, node_scale):
    return pl.pallas_call(
        spread_kernel,
        out_shape=jax.ShapeDtypeStruct((XY, TILE, F), BF16),
        in_specs=[pl.BlockSpec(memory_space=pltpu.HBM)] * 2,
        out_specs=pl.BlockSpec(memory_space=pltpu.HBM),
        scratch_shapes=[
            pltpu.VMEM((TILE, F), BF16),
            pltpu.VMEM((1, TILE), F32),
            pltpu.VMEM((COPIES, TILE, F), BF16),
            pltpu.SemaphoreType.DMA((2 + XY // COPIES,)),
        ],
        compiler_params=pltpu.CompilerParams(vmem_limit_bytes=63_480_000),
    )(features, node_scale)


def forward_send_kernel(x_ref, lane_ref, sub_ref, gathered_ref, send_ref):
    for j in range(XY):
        rows = pl.ds(j * EDGES, EDGES)
        picks = [
            one_hot(sub_ref[rows, H + b : H + b + 1], (EDGES, TILE), 1) for b in range(H)
        ]
        value = dot(jnp.concatenate(picks), x_ref[j]).astype(BF16)
        for b in range(H):
            gathered_ref[b, rows, :] = value[b * EDGES : (b + 1) * EDGES]
    for b in range(H):
        place = one_hot(lane_ref[b : b + 1, :], (HALF, E_ALL), 0, HALF)
        send_ref[b] = dot(place, gathered_ref[b]).astype(BF16)


def forward_keep_kernel(gathered_ref, lane_ref, mine_ref):
    for b in range(H):
        place = one_hot(lane_ref[b : b + 1, :], (HALF, E_ALL), 0)
        mine_ref[b] = dot(place, gathered_ref[b])


def add_kernel(mine_ref, other_ref, out_ref):
    for b in range(H):
        for k in range(L):
            rows = pl.ds(k * TILE, TILE)
            total = mine_ref[b, rows, :] + other_ref[b, rows, :].astype(F32)
            out_ref[k * H + b] = total.astype(BF16)


def middle_kernel(part_ref, x_ref, s_ref, w_ref, bias_ref, ct_ref, out_ref, g_ref, wp_ref):
    s = column(s_ref[...])
    z = s * x_ref[...].astype(F32)
    for k in range(ZN):
        z += part_ref[k].astype(F32)
    z_high = z.astype(BF16)
    z_low = (z - z_high.astype(F32)).astype(BF16)
    w = w_ref[...]
    p = s * (dot(z_high, w) + dot(z_low, w)) + bias_ref[...]
    square = p * p
    th = jnp.tanh(K0 * (p + K1 * (p * square)))
    out_ref[...] = (0.5 * p * (1.0 + th)).astype(BF16)
    slope = 0.5 * (1.0 + th) + 0.5 * p * (1.0 - th * th) * (K0 * (1.0 + 3.0 * K1 * square))
    grad = ct_ref[...].astype(F32) * slope
    g = (s * grad).astype(BF16)
    g_ref[...] = g
    first = (((0,), (0,)), ((), ()))
    wg = lax.dot_general(z_high, g, first, preferred_element_type=F32)
    wg += lax.dot_general(z_low, g, first, preferred_element_type=F32)
    bias_rows = split_rows(jnp.sum(grad, axis=0, keepdims=True))
    for k in range(XY):
        wp_ref[k, pl.ds(0, WR), :] = wg[k * WR : (k + 1) * WR].astype(BF16)
        wp_ref[k, pl.ds(WR, BB), :] = bias_rows


def load_kernel(w_ref, g_ref, pay_ref):
    tail = jnp.zeros((WR + BB, F), F32)
    for k in range(XY):
        tail += w_ref[k].astype(F32)
    own = tail[:WR].astype(BF16)
    bias_rows = split_rows(jnp.sum(tail[WR:], axis=0, keepdims=True))
    g = g_ref[...]
    for k in range(ZN):
        pay_ref[k, pl.ds(0, TILE), :] = g
        pay_ref[k, pl.ds(TILE, WR), :] = own
        pay_ref[k, pl.ds(TILE + WR, BB), :] = bias_rows


def backward_mine_kernel(mine_ref, sub_ref, act_ref, picked_ref, out_ref, grads):
    out_ref[...] = act_ref[...]
    for b in range(H):
        for k in range(L):
            grads[pl.ds(k * TILE, TILE), :] = mine_ref[k * H + b, pl.ds(0, TILE), :]
        for m in range(E_ALL // STEP):
            pick = one_hot(sub_ref[pl.ds(m * STEP, STEP), b : b + 1], (STEP, HALF), 1)
            value = dot(pick, grads[...]).astype(BF16)
            for q in range(STEP // EDGES):
                picked_ref[m * (STEP // EDGES) + q, pl.ds(b * EDGES, EDGES), :] = value[
                    q * EDGES : (q + 1) * EDGES
                ]


def backward_kernel(
    picked_ref, mine_ref, other_ref, sub_ref, col_ref, pay_ref, bias_ref, grads, picked
):
    factor = 1.0 / math.sqrt(XY * ZN * C * TILE)
    tail_mine = jnp.zeros((WR + BB, F), F32)
    tail_other = jnp.zeros((WR + BB, F), F32)
    for k in range(ZN):
        rows = pl.ds(TILE, WR + BB)
        tail_mine += mine_ref[k, rows, :].astype(F32)
        tail_other += other_ref[k, rows, :].astype(F32)
    tail = (tail_mine + tail_other) * factor
    own = tail[:WR].astype(BF16)
    bias_ref[...] = jnp.sum(tail[WR:], axis=0, keepdims=True)
    for b in range(H):
        for k in range(L):
            grads[pl.ds(k * TILE, TILE), :] = other_ref[k * H + b, pl.ds(0, TILE), :]
        for m in range(E_ALL // STEP):
            pick = one_hot(sub_ref[pl.ds(m * STEP, STEP), b : b + 1], (STEP, HALF), 1, HALF)
            value = dot(pick, grads[...])
            for q in range(STEP // EDGES):
                j, rows = m * (STEP // EDGES) + q, pl.ds(b * EDGES, EDGES)
                both = value[q * EDGES : (q + 1) * EDGES] + picked_ref[j, rows, :].astype(F32)
                picked[j, rows, :] = both.astype(BF16)
    for j in range(XY):
        place = one_hot(col_ref[j : j + 1, :], (TILE, H * EDGES), 0)
        total = dot(place, picked[j])
        pay_ref[j, pl.ds(0, TILE), :] = total.astype(BF16)
        pay_ref[j, pl.ds(TILE, WR), :] = own


def final_kernel(part_ref, g_ref, s_ref, w_ref, bias_ref, fg_ref, wg_ref, out_ref):
    out_ref[...] = bias_ref[...]
    back = g_ref[...].astype(F32)
    for k in range(XY):
        back += part_ref[k, pl.ds(0, TILE), :].astype(F32)
        wg_ref[pl.ds(k * WR, WR), :] = part_ref[k, pl.ds(TILE, WR), :].astype(F32)
    grad_xw = (column(s_ref[...]) * back).astype(BF16)
    fg_ref[...] = lax.dot_general(
        grad_xw, w_ref[...], (((1,), (1,)), ((), ())), preferred_element_type=F32
    ).astype(BF16)


def call(kernel, outs, scratch=(), flops=TILE * F * F):
    return pl.pallas_call(
        kernel,
        out_shape=[jax.ShapeDtypeStruct(shape, dtype) for shape, dtype in outs],
        out_specs=[pl.BlockSpec(memory_space=pltpu.VMEM)] * len(outs),
        scratch_shapes=[pltpu.VMEM(shape, dtype) for shape, dtype in scratch],
        compiler_params=PARAMS,
        cost_estimate=pl.CostEstimate(
            flops=flops, bytes_accessed=2 * 1024 * 1024, transcendentals=0
        ),
    )


def exchange(array, axes):
    return lax.all_to_all(array, axes, 0, 0, tiled=True)


def swap(array, axis):
    return lax.ppermute(array, axis, [(0, 1), (1, 0)])


def per_device(
    features, weight, bias, node_scale, cotangent, edge_slot, edge_row, edge_col, tile_row
):
    h, c = lax.axis_index("h"), lax.axis_index("c")
    s = node_scale[None, :]
    bias = bias[None, :]

    slot = edge_slot.reshape(XY * H, EDGES)
    tiles = tile_row.reshape(XY * H, SLOTS)
    tile = sum(jnp.where(slot == k, tiles[:, k : k + 1], 0) for k in range(SLOTS))
    target = ((tile & 1) ^ c) * HALF + (tile >> 1) * TILE + edge_row.reshape(slot.shape)
    target = jnp.where(slot < SLOTS, target, -1)
    edges = jnp.stack([target, edge_col.reshape(slot.shape)]).reshape(2, XY, H, EDGES)
    kept = lax.dynamic_index_in_dim(edges, h, 2, keepdims=False)
    came = swap(lax.dynamic_index_in_dim(edges, 1 - h, 2, keepdims=False), "h")

    sources = exchange(spread(features, s), ("x", "y"))

    pairs = jnp.stack([jnp.where(h == 0, kept, came), jnp.where(h == 0, came, kept)], axis=1)
    lane = pairs.reshape(2 * H, E_ALL)
    sub = lane.T
    columns = jnp.concatenate([pairs[1, 0], pairs[1, 1]], axis=1)

    gathered, send = call(
        forward_send_kernel,
        [((H, E_ALL, F), BF16), ((H, HALF, F), BF16)],
        flops=4 * E_ALL * F * (HALF + TILE),
    )(sources, lane, sub)
    other = swap(send, "c")
    (mine,) = call(
        forward_keep_kernel, [((H, HALF, F), F32)], flops=4 * E_ALL * F * HALF
    )(gathered, lane)
    (partial,) = call(add_kernel, [((ZN, TILE, F), BF16)])(mine, other)
    partial = exchange(partial, ("l", "h"))
    act, g, w_parts = call(
        middle_kernel,
        [((TILE, F), BF16), ((TILE, F), BF16), ((XY, WR + BB, F), BF16)],
    )(partial, features, s, weight, bias, cotangent)
    w_parts = exchange(w_parts, ("x", "y"))
    (pay,) = call(load_kernel, [((ZN, ZCHUNK, F), BF16)])(w_parts, g)
    around = exchange(pay, ("l", "h"))
    other = swap(around, "c")
    picked, output = call(
        backward_mine_kernel,
        [((XY, H * EDGES, F), BF16), ((TILE, F), BF16)],
        [((HALF, F), BF16)],
        flops=4 * E_ALL * F * HALF,
    )(around, sub, act)
    terms, bias_sum = call(
        backward_kernel,
        [((XY, XCHUNK, F), BF16), ((1, F), F32)],
        [((HALF, F), BF16), ((XY, H * EDGES, F), BF16)],
        flops=4 * E_ALL * F * (HALF + TILE),
    )(picked, around, other, sub, columns)
    terms = exchange(terms, ("x", "y"))
    feature_grad, weight_grad, bias_grad = call(
        final_kernel, [((TILE, F), BF16), ((F, F), F32), ((1, F), F32)]
    )(terms, g, s, weight, bias_sum)
    return output, feature_grad, weight_grad, bias_grad.reshape(F)


def solution(mesh):
    fine = Mesh(mesh.devices.reshape(X, Y, H, L, C), ALL)
    rows, edges = P(ALL, None), P(("x", "y", "h"), ("l", "c"), None, None)
    return jax.shard_map(
        per_device,
        mesh=fine,
        in_specs=(rows, P(), P(), P(ALL), rows, edges, edges, edges, edges),
        out_specs=(rows, rows, P(), P()),
        check_vma=False,
    )
```

```python
import math

import jax
import jax.numpy as jnp
from jax import lax
from jax.experimental import pallas as pl
from jax.experimental.pallas import tpu as pltpu
from jax.sharding import Mesh, PartitionSpec as P

X, Y, H, L, C = 4, 4, 2, 4, 2
XY, ZN = X * Y, H * L
TILE, F, SLOTS, EDGES = 128, 256, 4, 96
HALF = L * TILE
ROWS = C * HALF
E_ALL = XY * EDGES
STEP = 4 * EDGES
COPIES = 4
WR, BB = F // XY, 8
ZCHUNK = TILE + WR + BB
XCHUNK = TILE + WR
F32, BF16, I32 = jnp.float32, jnp.bfloat16, jnp.int32
K0, K1 = math.sqrt(2.0 / math.pi), 0.044715
ALL = ("xa", "xb", "ya", "yb", "h", "l", "c")
PLANE = ("xa", "ya", "xb", "yb")
PARAMS = pltpu.CompilerParams(vmem_limit_bytes=40 * 1024 * 1024)


def dot(a, b):
    return jnp.dot(a, b, preferred_element_type=F32)


def one_hot(index, shape, axis, base=0):
    return (index == lax.broadcasted_iota(I32, shape, axis) + base).astype(F32).astype(BF16)


def split_rows(row):
    high = row.astype(BF16).astype(F32)
    at = lax.broadcasted_iota(I32, (BB, F), 0)
    return jnp.where(at == 0, high, jnp.where(at == 1, row - high, 0.0)).astype(BF16)


def column(row):
    return jnp.transpose(jnp.broadcast_to(row, (TILE, TILE)))[:, :1]


def spread_kernel(x_ref, s_ref, out_ref, x, s, scaled, sems):
    loads = [
        pltpu.make_async_copy(x_ref, x, sems.at[0]),
        pltpu.make_async_copy(s_ref, s, sems.at[1]),
    ]
    for load in loads:
        load.start()
    for load in loads:
        load.wait()
    value = (column(s[...]) * x[...].astype(F32)).astype(BF16)
    for j in range(COPIES):
        scaled[j] = value
    stores = [
        pltpu.make_async_copy(scaled, out_ref.at[pl.ds(j * COPIES, COPIES)], sems.at[2 + j])
        for j in range(XY // COPIES)
    ]
    for store in stores:
        store.start()
    for store in stores:
        store.wait()


def spread(features, node_scale):
    return pl.pallas_call(
        spread_kernel,
        out_shape=jax.ShapeDtypeStruct((XY, TILE, F), BF16),
        in_specs=[pl.BlockSpec(memory_space=pltpu.HBM)] * 2,
        out_specs=pl.BlockSpec(memory_space=pltpu.HBM),
        scratch_shapes=[
            pltpu.VMEM((TILE, F), BF16),
            pltpu.VMEM((1, TILE), F32),
            pltpu.VMEM((COPIES, TILE, F), BF16),
            pltpu.SemaphoreType.DMA((2 + XY // COPIES,)),
        ],
        compiler_params=pltpu.CompilerParams(vmem_limit_bytes=63_480_000),
    )(features, node_scale)


def forward_send_kernel(x_ref, lane_ref, sub_ref, gathered_ref, send_ref):
    for j in range(XY):
        rows = pl.ds(j * EDGES, EDGES)
        picks = [
            one_hot(sub_ref[rows, H + b : H + b + 1], (EDGES, TILE), 1) for b in range(H)
        ]
        value = dot(jnp.concatenate(picks), x_ref[j]).astype(BF16)
        for b in range(H):
            gathered_ref[b, rows, :] = value[b * EDGES : (b + 1) * EDGES]
    for b in range(H):
        place = one_hot(lane_ref[b : b + 1, :], (HALF, E_ALL), 0, HALF)
        send_ref[b] = dot(place, gathered_ref[b]).astype(BF16)


def forward_keep_kernel(gathered_ref, lane_ref, mine_ref):
    for b in range(H):
        place = one_hot(lane_ref[b : b + 1, :], (HALF, E_ALL), 0)
        mine_ref[b] = dot(place, gathered_ref[b])


def add_kernel(mine_ref, other_ref, out_ref):
    for b in range(H):
        for k in range(L):
            rows = pl.ds(k * TILE, TILE)
            total = mine_ref[b, rows, :] + other_ref[b, rows, :].astype(F32)
            out_ref[k * H + b] = total.astype(BF16)


def middle_kernel(part_ref, x_ref, s_ref, w_ref, bias_ref, ct_ref, out_ref, g_ref, wp_ref):
    s = column(s_ref[...])
    z = s * x_ref[...].astype(F32)
    for k in range(ZN):
        z += part_ref[k].astype(F32)
    z_high = z.astype(BF16)
    z_low = (z - z_high.astype(F32)).astype(BF16)
    w = w_ref[...]
    p = s * (dot(z_high, w) + dot(z_low, w)) + bias_ref[...]
    square = p * p
    th = jnp.tanh(K0 * (p + K1 * (p * square)))
    out_ref[...] = (0.5 * p * (1.0 + th)).astype(BF16)
    slope = 0.5 * (1.0 + th) + 0.5 * p * (1.0 - th * th) * (K0 * (1.0 + 3.0 * K1 * square))
    grad = ct_ref[...].astype(F32) * slope
    g = (s * grad).astype(BF16)
    g_ref[...] = g
    first = (((0,), (0,)), ((), ()))
    wg = lax.dot_general(z_high, g, first, preferred_element_type=F32)
    wg += lax.dot_general(z_low, g, first, preferred_element_type=F32)
    bias_rows = split_rows(jnp.sum(grad, axis=0, keepdims=True))
    for k in range(XY):
        wp_ref[k, pl.ds(0, WR), :] = wg[k * WR : (k + 1) * WR].astype(BF16)
        wp_ref[k, pl.ds(WR, BB), :] = bias_rows


def load_kernel(w_ref, g_ref, pay_ref):
    tail = jnp.zeros((WR + BB, F), F32)
    for k in range(XY):
        tail += w_ref[k].astype(F32)
    own = tail[:WR].astype(BF16)
    bias_rows = split_rows(jnp.sum(tail[WR:], axis=0, keepdims=True))
    g = g_ref[...]
    for k in range(ZN):
        pay_ref[k, pl.ds(0, TILE), :] = g
        pay_ref[k, pl.ds(TILE, WR), :] = own
        pay_ref[k, pl.ds(TILE + WR, BB), :] = bias_rows


def backward_mine_kernel(mine_ref, sub_ref, act_ref, picked_ref, out_ref, grads):
    out_ref[...] = act_ref[...]
    for b in range(H):
        for k in range(L):
            grads[pl.ds(k * TILE, TILE), :] = mine_ref[k * H + b, pl.ds(0, TILE), :]
        for m in range(E_ALL // STEP):
            pick = one_hot(sub_ref[pl.ds(m * STEP, STEP), b : b + 1], (STEP, HALF), 1)
            value = dot(pick, grads[...]).astype(BF16)
            for q in range(STEP // EDGES):
                picked_ref[m * (STEP // EDGES) + q, pl.ds(b * EDGES, EDGES), :] = value[
                    q * EDGES : (q + 1) * EDGES
                ]


def backward_kernel(
    picked_ref, mine_ref, other_ref, sub_ref, col_ref, pay_ref, bias_ref, grads, picked
):
    factor = 1.0 / math.sqrt(XY * ZN * C * TILE)
    tail_mine = jnp.zeros((WR + BB, F), F32)
    tail_other = jnp.zeros((WR + BB, F), F32)
    for k in range(ZN):
        rows = pl.ds(TILE, WR + BB)
        tail_mine += mine_ref[k, rows, :].astype(F32)
        tail_other += other_ref[k, rows, :].astype(F32)
    tail = (tail_mine + tail_other) * factor
    own = tail[:WR].astype(BF16)
    bias_ref[...] = jnp.sum(tail[WR:], axis=0, keepdims=True)
    for b in range(H):
        for k in range(L):
            grads[pl.ds(k * TILE, TILE), :] = other_ref[k * H + b, pl.ds(0, TILE), :]
        for m in range(E_ALL // STEP):
            pick = one_hot(sub_ref[pl.ds(m * STEP, STEP), b : b + 1], (STEP, HALF), 1, HALF)
            value = dot(pick, grads[...])
            for q in range(STEP // EDGES):
                j, rows = m * (STEP // EDGES) + q, pl.ds(b * EDGES, EDGES)
                both = value[q * EDGES : (q + 1) * EDGES] + picked_ref[j, rows, :].astype(F32)
                picked[j, rows, :] = both.astype(BF16)
    for j in range(XY):
        place = one_hot(col_ref[j : j + 1, :], (TILE, H * EDGES), 0)
        total = dot(place, picked[j])
        pay_ref[j, pl.ds(0, TILE), :] = total.astype(BF16)
        pay_ref[j, pl.ds(TILE, WR), :] = own


def final_kernel(part_ref, g_ref, s_ref, w_ref, bias_ref, fg_ref, wg_ref, out_ref):
    out_ref[...] = bias_ref[...]
    back = g_ref[...].astype(F32)
    for k in range(XY):
        back += part_ref[k, pl.ds(0, TILE), :].astype(F32)
        wg_ref[pl.ds(k * WR, WR), :] = part_ref[k, pl.ds(TILE, WR), :].astype(F32)
    grad_xw = (column(s_ref[...]) * back).astype(BF16)
    fg_ref[...] = lax.dot_general(
        grad_xw, w_ref[...], (((1,), (1,)), ((), ())), preferred_element_type=F32
    ).astype(BF16)


def call(kernel, outs, scratch=(), flops=TILE * F * F):
    return pl.pallas_call(
        kernel,
        out_shape=[jax.ShapeDtypeStruct(shape, dtype) for shape, dtype in outs],
        out_specs=[pl.BlockSpec(memory_space=pltpu.VMEM)] * len(outs),
        scratch_shapes=[pltpu.VMEM(shape, dtype) for shape, dtype in scratch],
        compiler_params=PARAMS,
        cost_estimate=pl.CostEstimate(
            flops=flops, bytes_accessed=2 * 1024 * 1024, transcendentals=0
        ),
    )


def exchange(array, axes):
    return lax.all_to_all(array, axes, 0, 0, tiled=True)


def swap(array, axis):
    return lax.ppermute(array, axis, [(0, 1), (1, 0)])


def per_device(
    features, weight, bias, node_scale, cotangent, edge_slot, edge_row, edge_col, tile_row
):
    h, c = lax.axis_index("h"), lax.axis_index("c")
    s = node_scale[None, :]
    bias = bias[None, :]

    slot = edge_slot.reshape(XY * H, EDGES)
    tiles = tile_row.reshape(XY * H, SLOTS)
    tile = sum(jnp.where(slot == k, tiles[:, k : k + 1], 0) for k in range(SLOTS))
    target = ((tile & 1) ^ c) * HALF + (tile >> 1) * TILE + edge_row.reshape(slot.shape)
    target = jnp.where(slot < SLOTS, target, -1)
    edges = jnp.stack([target, edge_col.reshape(slot.shape)]).reshape(2, 2, 2, 2, 2, H, EDGES)
    edges = edges.transpose(0, 1, 3, 2, 4, 5, 6).reshape(2, XY, H, EDGES)
    kept = lax.dynamic_index_in_dim(edges, h, 2, keepdims=False)
    came = swap(lax.dynamic_index_in_dim(edges, 1 - h, 2, keepdims=False), "h")

    sources = exchange(spread(features, s), PLANE)

    pairs = jnp.stack([jnp.where(h == 0, kept, came), jnp.where(h == 0, came, kept)], axis=1)
    lane = pairs.reshape(2 * H, E_ALL)
    sub = lane.T
    columns = jnp.concatenate([pairs[1, 0], pairs[1, 1]], axis=1)

    gathered, send = call(
        forward_send_kernel,
        [((H, E_ALL, F), BF16), ((H, HALF, F), BF16)],
        flops=4 * E_ALL * F * (HALF + TILE),
    )(sources, lane, sub)
    other = swap(send, "c")
    (mine,) = call(
        forward_keep_kernel, [((H, HALF, F), F32)], flops=4 * E_ALL * F * HALF
    )(gathered, lane)
    (partial,) = call(add_kernel, [((ZN, TILE, F), BF16)])(mine, other)
    partial = exchange(partial, ("l", "h"))
    act, g, w_parts = call(
        middle_kernel,
        [((TILE, F), BF16), ((TILE, F), BF16), ((XY, WR + BB, F), BF16)],
    )(partial, features, s, weight, bias, cotangent)
    w_parts = exchange(w_parts, PLANE)
    (pay,) = call(load_kernel, [((ZN, ZCHUNK, F), BF16)])(w_parts, g)
    around = exchange(pay, ("l", "h"))
    other = swap(around, "c")
    picked, output = call(
        backward_mine_kernel,
        [((XY, H * EDGES, F), BF16), ((TILE, F), BF16)],
        [((HALF, F), BF16)],
        flops=4 * E_ALL * F * HALF,
    )(around, sub, act)
    terms, bias_sum = call(
        backward_kernel,
        [((XY, XCHUNK, F), BF16), ((1, F), F32)],
        [((HALF, F), BF16), ((XY, H * EDGES, F), BF16)],
        flops=4 * E_ALL * F * (HALF + TILE),
    )(picked, around, other, sub, columns)
    terms = exchange(terms, PLANE)
    feature_grad, weight_grad, bias_grad = call(
        final_kernel, [((TILE, F), BF16), ((F, F), F32), ((1, F), F32)]
    )(terms, g, s, weight, bias_sum)
    return output, feature_grad, weight_grad, bias_grad.reshape(F)


def solution(mesh):
    fine = Mesh(mesh.devices.reshape(2, 2, 2, 2, H, L, C), ALL)
    rows, edges = P(ALL, None), P(ALL[:5], ALL[5:], None, None)
    return jax.shard_map(
        per_device,
        mesh=fine,
        in_specs=(rows, P(), P(), P(ALL), rows, edges, edges, edges, edges),
        out_specs=(rows, rows, P(), P()),
        check_vma=False,
    )
```

```python
import math

import jax
import jax.numpy as jnp
from jax import lax
from jax.experimental import pallas as pl
from jax.experimental.pallas import tpu as pltpu
from jax.sharding import Mesh, PartitionSpec as P

X, Y, H, L, C = 4, 4, 2, 4, 2
XY, ZN = X * Y, H * L
TILE, F, SLOTS, EDGES = 128, 256, 4, 96
HALF = L * TILE
ROWS = C * HALF
E_ALL = XY * EDGES
STEP = 4 * EDGES
COPIES = 4
WR, BB = F // XY, 8
ZCHUNK = TILE + WR + BB
XCHUNK = TILE + WR
F32, BF16, I32 = jnp.float32, jnp.bfloat16, jnp.int32
K0, K1 = math.sqrt(2.0 / math.pi), 0.044715
ALL = ("x", "y", "h", "la", "lb", "c")
LINE = ("lb", "la", "h")
PARAMS = pltpu.CompilerParams(vmem_limit_bytes=40 * 1024 * 1024)


def place_of(l, h):
    return (l % 2) * 4 + (l // 2) * 2 + h


def dot(a, b):
    return jnp.dot(a, b, preferred_element_type=F32)


def one_hot(index, shape, axis, base=0):
    return (index == lax.broadcasted_iota(I32, shape, axis) + base).astype(F32).astype(BF16)


def split_rows(row):
    high = row.astype(BF16).astype(F32)
    at = lax.broadcasted_iota(I32, (BB, F), 0)
    return jnp.where(at == 0, high, jnp.where(at == 1, row - high, 0.0)).astype(BF16)


def column(row):
    return jnp.transpose(jnp.broadcast_to(row, (TILE, TILE)))[:, :1]


def spread_kernel(x_ref, s_ref, out_ref, x, s, scaled, sems):
    loads = [
        pltpu.make_async_copy(x_ref, x, sems.at[0]),
        pltpu.make_async_copy(s_ref, s, sems.at[1]),
    ]
    for load in loads:
        load.start()
    for load in loads:
        load.wait()
    value = (column(s[...]) * x[...].astype(F32)).astype(BF16)
    for j in range(COPIES):
        scaled[j] = value
    stores = [
        pltpu.make_async_copy(scaled, out_ref.at[pl.ds(j * COPIES, COPIES)], sems.at[2 + j])
        for j in range(XY // COPIES)
    ]
    for store in stores:
        store.start()
    for store in stores:
        store.wait()


def spread(features, node_scale):
    return pl.pallas_call(
        spread_kernel,
        out_shape=jax.ShapeDtypeStruct((XY, TILE, F), BF16),
        in_specs=[pl.BlockSpec(memory_space=pltpu.HBM)] * 2,
        out_specs=pl.BlockSpec(memory_space=pltpu.HBM),
        scratch_shapes=[
            pltpu.VMEM((TILE, F), BF16),
            pltpu.VMEM((1, TILE), F32),
            pltpu.VMEM((COPIES, TILE, F), BF16),
            pltpu.SemaphoreType.DMA((2 + XY // COPIES,)),
        ],
        compiler_params=pltpu.CompilerParams(vmem_limit_bytes=63_480_000),
    )(features, node_scale)


def forward_send_kernel(x_ref, lane_ref, sub_ref, gathered_ref, send_ref):
    for j in range(XY):
        rows = pl.ds(j * EDGES, EDGES)
        picks = [
            one_hot(sub_ref[rows, H + b : H + b + 1], (EDGES, TILE), 1) for b in range(H)
        ]
        value = dot(jnp.concatenate(picks), x_ref[j]).astype(BF16)
        for b in range(H):
            gathered_ref[b, rows, :] = value[b * EDGES : (b + 1) * EDGES]
    for b in range(H):
        place = one_hot(lane_ref[b : b + 1, :], (HALF, E_ALL), 0, HALF)
        send_ref[b] = dot(place, gathered_ref[b]).astype(BF16)


def forward_keep_kernel(gathered_ref, lane_ref, mine_ref):
    for b in range(H):
        place = one_hot(lane_ref[b : b + 1, :], (HALF, E_ALL), 0)
        mine_ref[b] = dot(place, gathered_ref[b])


def add_kernel(mine_ref, other_ref, out_ref):
    for b in range(H):
        for k in range(L):
            rows = pl.ds(k * TILE, TILE)
            total = mine_ref[b, rows, :] + other_ref[b, rows, :].astype(F32)
            out_ref[place_of(k, b)] = total.astype(BF16)


def middle_kernel(part_ref, x_ref, s_ref, w_ref, bias_ref, ct_ref, out_ref, g_ref, wp_ref):
    s = column(s_ref[...])
    z = s * x_ref[...].astype(F32)
    for k in range(ZN):
        z += part_ref[k].astype(F32)
    z_high = z.astype(BF16)
    z_low = (z - z_high.astype(F32)).astype(BF16)
    w = w_ref[...]
    p = s * (dot(z_high, w) + dot(z_low, w)) + bias_ref[...]
    square = p * p
    th = jnp.tanh(K0 * (p + K1 * (p * square)))
    out_ref[...] = (0.5 * p * (1.0 + th)).astype(BF16)
    slope = 0.5 * (1.0 + th) + 0.5 * p * (1.0 - th * th) * (K0 * (1.0 + 3.0 * K1 * square))
    grad = ct_ref[...].astype(F32) * slope
    g = (s * grad).astype(BF16)
    g_ref[...] = g
    first = (((0,), (0,)), ((), ()))
    wg = lax.dot_general(z_high, g, first, preferred_element_type=F32)
    wg += lax.dot_general(z_low, g, first, preferred_element_type=F32)
    bias_rows = split_rows(jnp.sum(grad, axis=0, keepdims=True))
    for k in range(XY):
        wp_ref[k, pl.ds(0, WR), :] = wg[k * WR : (k + 1) * WR].astype(BF16)
        wp_ref[k, pl.ds(WR, BB), :] = bias_rows


def load_kernel(w_ref, g_ref, pay_ref):
    tail = jnp.zeros((WR + BB, F), F32)
    for k in range(XY):
        tail += w_ref[k].astype(F32)
    own = tail[:WR].astype(BF16)
    bias_rows = split_rows(jnp.sum(tail[WR:], axis=0, keepdims=True))
    g = g_ref[...]
    for k in range(ZN):
        pay_ref[k, pl.ds(0, TILE), :] = g
        pay_ref[k, pl.ds(TILE, WR), :] = own
        pay_ref[k, pl.ds(TILE + WR, BB), :] = bias_rows


def backward_mine_kernel(mine_ref, sub_ref, act_ref, picked_ref, out_ref, grads):
    out_ref[...] = act_ref[...]
    for b in range(H):
        for k in range(L):
            grads[pl.ds(k * TILE, TILE), :] = mine_ref[place_of(k, b), pl.ds(0, TILE), :]
        for m in range(E_ALL // STEP):
            pick = one_hot(sub_ref[pl.ds(m * STEP, STEP), b : b + 1], (STEP, HALF), 1)
            value = dot(pick, grads[...]).astype(BF16)
            for q in range(STEP // EDGES):
                picked_ref[m * (STEP // EDGES) + q, pl.ds(b * EDGES, EDGES), :] = value[
                    q * EDGES : (q + 1) * EDGES
                ]


def backward_kernel(
    picked_ref, mine_ref, other_ref, sub_ref, col_ref, pay_ref, bias_ref, grads, picked
):
    factor = 1.0 / math.sqrt(XY * ZN * C * TILE)
    tail_mine = jnp.zeros((WR + BB, F), F32)
    tail_other = jnp.zeros((WR + BB, F), F32)
    for k in range(ZN):
        rows = pl.ds(TILE, WR + BB)
        tail_mine += mine_ref[k, rows, :].astype(F32)
        tail_other += other_ref[k, rows, :].astype(F32)
    tail = (tail_mine + tail_other) * factor
    own = tail[:WR].astype(BF16)
    bias_ref[...] = jnp.sum(tail[WR:], axis=0, keepdims=True)
    for b in range(H):
        for k in range(L):
            grads[pl.ds(k * TILE, TILE), :] = other_ref[place_of(k, b), pl.ds(0, TILE), :]
        for m in range(E_ALL // STEP):
            pick = one_hot(sub_ref[pl.ds(m * STEP, STEP), b : b + 1], (STEP, HALF), 1, HALF)
            value = dot(pick, grads[...])
            for q in range(STEP // EDGES):
                j, rows = m * (STEP // EDGES) + q, pl.ds(b * EDGES, EDGES)
                both = value[q * EDGES : (q + 1) * EDGES] + picked_ref[j, rows, :].astype(F32)
                picked[j, rows, :] = both.astype(BF16)
    for j in range(XY):
        place = one_hot(col_ref[j : j + 1, :], (TILE, H * EDGES), 0)
        total = dot(place, picked[j])
        pay_ref[j, pl.ds(0, TILE), :] = total.astype(BF16)
        pay_ref[j, pl.ds(TILE, WR), :] = own


def final_kernel(part_ref, g_ref, s_ref, w_ref, bias_ref, fg_ref, wg_ref, out_ref):
    out_ref[...] = bias_ref[...]
    back = g_ref[...].astype(F32)
    for k in range(XY):
        back += part_ref[k, pl.ds(0, TILE), :].astype(F32)
        wg_ref[pl.ds(k * WR, WR), :] = part_ref[k, pl.ds(TILE, WR), :].astype(F32)
    grad_xw = (column(s_ref[...]) * back).astype(BF16)
    fg_ref[...] = lax.dot_general(
        grad_xw, w_ref[...], (((1,), (1,)), ((), ())), preferred_element_type=F32
    ).astype(BF16)


def call(kernel, outs, scratch=(), flops=TILE * F * F):
    return pl.pallas_call(
        kernel,
        out_shape=[jax.ShapeDtypeStruct(shape, dtype) for shape, dtype in outs],
        out_specs=[pl.BlockSpec(memory_space=pltpu.VMEM)] * len(outs),
        scratch_shapes=[pltpu.VMEM(shape, dtype) for shape, dtype in scratch],
        compiler_params=PARAMS,
        cost_estimate=pl.CostEstimate(
            flops=flops, bytes_accessed=2 * 1024 * 1024, transcendentals=0
        ),
    )


def exchange(array, axes):
    return lax.all_to_all(array, axes, 0, 0, tiled=True)


def swap(array, axis):
    return lax.ppermute(array, axis, [(0, 1), (1, 0)])


def per_device(
    features, weight, bias, node_scale, cotangent, edge_slot, edge_row, edge_col, tile_row
):
    h, c = lax.axis_index("h"), lax.axis_index("c")
    s = node_scale[None, :]
    bias = bias[None, :]

    slot = edge_slot.reshape(XY * H, EDGES)
    tiles = tile_row.reshape(XY * H, SLOTS)
    tile = sum(jnp.where(slot == k, tiles[:, k : k + 1], 0) for k in range(SLOTS))
    target = ((tile & 1) ^ c) * HALF + (tile >> 1) * TILE + edge_row.reshape(slot.shape)
    target = jnp.where(slot < SLOTS, target, -1)
    edges = jnp.stack([target, edge_col.reshape(slot.shape)]).reshape(2, XY, H, EDGES)
    kept = lax.dynamic_index_in_dim(edges, h, 2, keepdims=False)
    came = swap(lax.dynamic_index_in_dim(edges, 1 - h, 2, keepdims=False), "h")

    sources = exchange(spread(features, s), ("x", "y"))

    pairs = jnp.stack([jnp.where(h == 0, kept, came), jnp.where(h == 0, came, kept)], axis=1)
    lane = pairs.reshape(2 * H, E_ALL)
    sub = lane.T
    columns = jnp.concatenate([pairs[1, 0], pairs[1, 1]], axis=1)

    gathered, send = call(
        forward_send_kernel,
        [((H, E_ALL, F), BF16), ((H, HALF, F), BF16)],
        flops=4 * E_ALL * F * (HALF + TILE),
    )(sources, lane, sub)
    other = swap(send, "c")
    (mine,) = call(
        forward_keep_kernel, [((H, HALF, F), F32)], flops=4 * E_ALL * F * HALF
    )(gathered, lane)
    (partial,) = call(add_kernel, [((ZN, TILE, F), BF16)])(mine, other)
    partial = exchange(partial, LINE)
    act, g, w_parts = call(
        middle_kernel,
        [((TILE, F), BF16), ((TILE, F), BF16), ((XY, WR + BB, F), BF16)],
    )(partial, features, s, weight, bias, cotangent)
    w_parts = exchange(w_parts, ("x", "y"))
    (pay,) = call(load_kernel, [((ZN, ZCHUNK, F), BF16)])(w_parts, g)
    around = exchange(pay, LINE)
    other = swap(around, "c")
    picked, output = call(
        backward_mine_kernel,
        [((XY, H * EDGES, F), BF16), ((TILE, F), BF16)],
        [((HALF, F), BF16)],
        flops=4 * E_ALL * F * HALF,
    )(around, sub, act)
    terms, bias_sum = call(
        backward_kernel,
        [((XY, XCHUNK, F), BF16), ((1, F), F32)],
        [((HALF, F), BF16), ((XY, H * EDGES, F), BF16)],
        flops=4 * E_ALL * F * (HALF + TILE),
    )(picked, around, other, sub, columns)
    terms = exchange(terms, ("x", "y"))
    feature_grad, weight_grad, bias_grad = call(
        final_kernel, [((TILE, F), BF16), ((F, F), F32), ((1, F), F32)]
    )(terms, g, s, weight, bias_sum)
    return output, feature_grad, weight_grad, bias_grad.reshape(F)


def solution(mesh):
    fine = Mesh(mesh.devices.reshape(X, Y, H, 2, 2, C), ALL)
    rows, edges = P(ALL, None), P(ALL[:3], ALL[3:], None, None)
    return jax.shard_map(
        per_device,
        mesh=fine,
        in_specs=(rows, P(), P(), P(ALL), rows, edges, edges, edges, edges),
        out_specs=(rows, rows, P(), P()),
        check_vma=False,
    )
```

```python
import math

import jax
import jax.numpy as jnp
from jax import lax
from jax.experimental import pallas as pl
from jax.experimental.pallas import tpu as pltpu
from jax.sharding import Mesh, PartitionSpec as P

X, Y, H, L, C = 4, 4, 2, 4, 2
XY, ZN = X * Y, H * L
TILE, F, SLOTS, EDGES = 128, 256, 4, 96
HALF = L * TILE
ROWS = C * HALF
E_ALL = XY * EDGES
STEP = 4 * EDGES
COPIES = 4
WR, BB = F // XY, 8
ZCHUNK = TILE + WR + BB
XCHUNK = TILE + WR
F32, BF16, I32 = jnp.float32, jnp.bfloat16, jnp.int32
K0, K1 = math.sqrt(2.0 / math.pi), 0.044715
ALL = ("x", "y", "h", "la", "lb", "c")
LINE = ("lb", "h", "la")
PARAMS = pltpu.CompilerParams(vmem_limit_bytes=40 * 1024 * 1024)


def place_of(l, h):
    return (l % 2) * 4 + h * 2 + l // 2


def dot(a, b):
    return jnp.dot(a, b, preferred_element_type=F32)


def one_hot(index, shape, axis, base=0):
    return (index == lax.broadcasted_iota(I32, shape, axis) + base).astype(F32).astype(BF16)


def split_rows(row):
    high = row.astype(BF16).astype(F32)
    at = lax.broadcasted_iota(I32, (BB, F), 0)
    return jnp.where(at == 0, high, jnp.where(at == 1, row - high, 0.0)).astype(BF16)


def column(row):
    return jnp.transpose(jnp.broadcast_to(row, (TILE, TILE)))[:, :1]


def spread_kernel(x_ref, s_ref, out_ref, x, s, scaled, sems):
    loads = [
        pltpu.make_async_copy(x_ref, x, sems.at[0]),
        pltpu.make_async_copy(s_ref, s, sems.at[1]),
    ]
    for load in loads:
        load.start()
    for load in loads:
        load.wait()
    value = (column(s[...]) * x[...].astype(F32)).astype(BF16)
    for j in range(COPIES):
        scaled[j] = value
    stores = [
        pltpu.make_async_copy(scaled, out_ref.at[pl.ds(j * COPIES, COPIES)], sems.at[2 + j])
        for j in range(XY // COPIES)
    ]
    for store in stores:
        store.start()
    for store in stores:
        store.wait()


def spread(features, node_scale):
    return pl.pallas_call(
        spread_kernel,
        out_shape=jax.ShapeDtypeStruct((XY, TILE, F), BF16),
        in_specs=[pl.BlockSpec(memory_space=pltpu.HBM)] * 2,
        out_specs=pl.BlockSpec(memory_space=pltpu.HBM),
        scratch_shapes=[
            pltpu.VMEM((TILE, F), BF16),
            pltpu.VMEM((1, TILE), F32),
            pltpu.VMEM((COPIES, TILE, F), BF16),
            pltpu.SemaphoreType.DMA((2 + XY // COPIES,)),
        ],
        compiler_params=pltpu.CompilerParams(vmem_limit_bytes=63_480_000),
    )(features, node_scale)


def forward_send_kernel(x_ref, lane_ref, sub_ref, gathered_ref, send_ref):
    for j in range(XY):
        rows = pl.ds(j * EDGES, EDGES)
        picks = [
            one_hot(sub_ref[rows, H + b : H + b + 1], (EDGES, TILE), 1) for b in range(H)
        ]
        value = dot(jnp.concatenate(picks), x_ref[j]).astype(BF16)
        for b in range(H):
            gathered_ref[b, rows, :] = value[b * EDGES : (b + 1) * EDGES]
    for b in range(H):
        place = one_hot(lane_ref[b : b + 1, :], (HALF, E_ALL), 0, HALF)
        send_ref[b] = dot(place, gathered_ref[b]).astype(BF16)


def forward_keep_kernel(gathered_ref, lane_ref, mine_ref):
    for b in range(H):
        place = one_hot(lane_ref[b : b + 1, :], (HALF, E_ALL), 0)
        mine_ref[b] = dot(place, gathered_ref[b])


def add_kernel(mine_ref, other_ref, out_ref):
    for b in range(H):
        for k in range(L):
            rows = pl.ds(k * TILE, TILE)
            total = mine_ref[b, rows, :] + other_ref[b, rows, :].astype(F32)
            out_ref[place_of(k, b)] = total.astype(BF16)


def middle_kernel(part_ref, x_ref, s_ref, w_ref, bias_ref, ct_ref, out_ref, g_ref, wp_ref):
    s = column(s_ref[...])
    z = s * x_ref[...].astype(F32)
    for k in range(ZN):
        z += part_ref[k].astype(F32)
    z_high = z.astype(BF16)
    z_low = (z - z_high.astype(F32)).astype(BF16)
    w = w_ref[...]
    p = s * (dot(z_high, w) + dot(z_low, w)) + bias_ref[...]
    square = p * p
    th = jnp.tanh(K0 * (p + K1 * (p * square)))
    out_ref[...] = (0.5 * p * (1.0 + th)).astype(BF16)
    slope = 0.5 * (1.0 + th) + 0.5 * p * (1.0 - th * th) * (K0 * (1.0 + 3.0 * K1 * square))
    grad = ct_ref[...].astype(F32) * slope
    g = (s * grad).astype(BF16)
    g_ref[...] = g
    first = (((0,), (0,)), ((), ()))
    wg = lax.dot_general(z_high, g, first, preferred_element_type=F32)
    wg += lax.dot_general(z_low, g, first, preferred_element_type=F32)
    bias_rows = split_rows(jnp.sum(grad, axis=0, keepdims=True))
    for k in range(XY):
        wp_ref[k, pl.ds(0, WR), :] = wg[k * WR : (k + 1) * WR].astype(BF16)
        wp_ref[k, pl.ds(WR, BB), :] = bias_rows


def load_kernel(w_ref, g_ref, pay_ref):
    tail = jnp.zeros((WR + BB, F), F32)
    for k in range(XY):
        tail += w_ref[k].astype(F32)
    own = tail[:WR].astype(BF16)
    bias_rows = split_rows(jnp.sum(tail[WR:], axis=0, keepdims=True))
    g = g_ref[...]
    for k in range(ZN):
        pay_ref[k, pl.ds(0, TILE), :] = g
        pay_ref[k, pl.ds(TILE, WR), :] = own
        pay_ref[k, pl.ds(TILE + WR, BB), :] = bias_rows


def backward_mine_kernel(mine_ref, sub_ref, act_ref, picked_ref, out_ref, grads):
    out_ref[...] = act_ref[...]
    for b in range(H):
        for k in range(L):
            grads[pl.ds(k * TILE, TILE), :] = mine_ref[place_of(k, b), pl.ds(0, TILE), :]
        for m in range(E_ALL // STEP):
            pick = one_hot(sub_ref[pl.ds(m * STEP, STEP), b : b + 1], (STEP, HALF), 1)
            value = dot(pick, grads[...]).astype(BF16)
            for q in range(STEP // EDGES):
                picked_ref[m * (STEP // EDGES) + q, pl.ds(b * EDGES, EDGES), :] = value[
                    q * EDGES : (q + 1) * EDGES
                ]


def backward_kernel(
    picked_ref, mine_ref, other_ref, sub_ref, col_ref, pay_ref, bias_ref, grads, picked
):
    factor = 1.0 / math.sqrt(XY * ZN * C * TILE)
    tail_mine = jnp.zeros((WR + BB, F), F32)
    tail_other = jnp.zeros((WR + BB, F), F32)
    for k in range(ZN):
        rows = pl.ds(TILE, WR + BB)
        tail_mine += mine_ref[k, rows, :].astype(F32)
        tail_other += other_ref[k, rows, :].astype(F32)
    tail = (tail_mine + tail_other) * factor
    own = tail[:WR].astype(BF16)
    bias_ref[...] = jnp.sum(tail[WR:], axis=0, keepdims=True)
    for b in range(H):
        for k in range(L):
            grads[pl.ds(k * TILE, TILE), :] = other_ref[place_of(k, b), pl.ds(0, TILE), :]
        for m in range(E_ALL // STEP):
            pick = one_hot(sub_ref[pl.ds(m * STEP, STEP), b : b + 1], (STEP, HALF), 1, HALF)
            value = dot(pick, grads[...])
            for q in range(STEP // EDGES):
                j, rows = m * (STEP // EDGES) + q, pl.ds(b * EDGES, EDGES)
                both = value[q * EDGES : (q + 1) * EDGES] + picked_ref[j, rows, :].astype(F32)
                picked[j, rows, :] = both.astype(BF16)
    for j in range(XY):
        place = one_hot(col_ref[j : j + 1, :], (TILE, H * EDGES), 0)
        total = dot(place, picked[j])
        pay_ref[j, pl.ds(0, TILE), :] = total.astype(BF16)
        pay_ref[j, pl.ds(TILE, WR), :] = own


def final_kernel(part_ref, g_ref, s_ref, w_ref, bias_ref, fg_ref, wg_ref, out_ref):
    out_ref[...] = bias_ref[...]
    back = g_ref[...].astype(F32)
    for k in range(XY):
        back += part_ref[k, pl.ds(0, TILE), :].astype(F32)
        wg_ref[pl.ds(k * WR, WR), :] = part_ref[k, pl.ds(TILE, WR), :].astype(F32)
    grad_xw = (column(s_ref[...]) * back).astype(BF16)
    fg_ref[...] = lax.dot_general(
        grad_xw, w_ref[...], (((1,), (1,)), ((), ())), preferred_element_type=F32
    ).astype(BF16)


def call(kernel, outs, scratch=(), flops=TILE * F * F):
    return pl.pallas_call(
        kernel,
        out_shape=[jax.ShapeDtypeStruct(shape, dtype) for shape, dtype in outs],
        out_specs=[pl.BlockSpec(memory_space=pltpu.VMEM)] * len(outs),
        scratch_shapes=[pltpu.VMEM(shape, dtype) for shape, dtype in scratch],
        compiler_params=PARAMS,
        cost_estimate=pl.CostEstimate(
            flops=flops, bytes_accessed=2 * 1024 * 1024, transcendentals=0
        ),
    )


def exchange(array, axes):
    return lax.all_to_all(array, axes, 0, 0, tiled=True)


def swap(array, axis):
    return lax.ppermute(array, axis, [(0, 1), (1, 0)])


def per_device(
    features, weight, bias, node_scale, cotangent, edge_slot, edge_row, edge_col, tile_row
):
    h, c = lax.axis_index("h"), lax.axis_index("c")
    s = node_scale[None, :]
    bias = bias[None, :]

    slot = edge_slot.reshape(XY * H, EDGES)
    tiles = tile_row.reshape(XY * H, SLOTS)
    tile = sum(jnp.where(slot == k, tiles[:, k : k + 1], 0) for k in range(SLOTS))
    target = ((tile & 1) ^ c) * HALF + (tile >> 1) * TILE + edge_row.reshape(slot.shape)
    target = jnp.where(slot < SLOTS, target, -1)
    edges = jnp.stack([target, edge_col.reshape(slot.shape)]).reshape(2, XY, H, EDGES)
    kept = lax.dynamic_index_in_dim(edges, h, 2, keepdims=False)
    came = swap(lax.dynamic_index_in_dim(edges, 1 - h, 2, keepdims=False), "h")

    sources = exchange(spread(features, s), ("x", "y"))

    pairs = jnp.stack([jnp.where(h == 0, kept, came), jnp.where(h == 0, came, kept)], axis=1)
    lane = pairs.reshape(2 * H, E_ALL)
    sub = lane.T
    columns = jnp.concatenate([pairs[1, 0], pairs[1, 1]], axis=1)

    gathered, send = call(
        forward_send_kernel,
        [((H, E_ALL, F), BF16), ((H, HALF, F), BF16)],
        flops=4 * E_ALL * F * (HALF + TILE),
    )(sources, lane, sub)
    other = swap(send, "c")
    (mine,) = call(
        forward_keep_kernel, [((H, HALF, F), F32)], flops=4 * E_ALL * F * HALF
    )(gathered, lane)
    (partial,) = call(add_kernel, [((ZN, TILE, F), BF16)])(mine, other)
    partial = exchange(partial, LINE)
    act, g, w_parts = call(
        middle_kernel,
        [((TILE, F), BF16), ((TILE, F), BF16), ((XY, WR + BB, F), BF16)],
    )(partial, features, s, weight, bias, cotangent)
    w_parts = exchange(w_parts, ("x", "y"))
    (pay,) = call(load_kernel, [((ZN, ZCHUNK, F), BF16)])(w_parts, g)
    around = exchange(pay, LINE)
    other = swap(around, "c")
    picked, output = call(
        backward_mine_kernel,
        [((XY, H * EDGES, F), BF16), ((TILE, F), BF16)],
        [((HALF, F), BF16)],
        flops=4 * E_ALL * F * HALF,
    )(around, sub, act)
    terms, bias_sum = call(
        backward_kernel,
        [((XY, XCHUNK, F), BF16), ((1, F), F32)],
        [((HALF, F), BF16), ((XY, H * EDGES, F), BF16)],
        flops=4 * E_ALL * F * (HALF + TILE),
    )(picked, around, other, sub, columns)
    terms = exchange(terms, ("x", "y"))
    feature_grad, weight_grad, bias_grad = call(
        final_kernel, [((TILE, F), BF16), ((F, F), F32), ((1, F), F32)]
    )(terms, g, s, weight, bias_sum)
    return output, feature_grad, weight_grad, bias_grad.reshape(F)


def solution(mesh):
    fine = Mesh(mesh.devices.reshape(X, Y, H, 2, 2, C), ALL)
    rows, edges = P(ALL, None), P(ALL[:3], ALL[3:], None, None)
    return jax.shard_map(
        per_device,
        mesh=fine,
        in_specs=(rows, P(), P(), P(ALL), rows, edges, edges, edges, edges),
        out_specs=(rows, rows, P(), P()),
        check_vma=False,
    )
```

```python
import math

import jax
import jax.numpy as jnp
from jax import lax
from jax.experimental import pallas as pl
from jax.experimental.pallas import tpu as pltpu
from jax.sharding import Mesh, PartitionSpec as P

X, Y, H, L, C = 4, 4, 2, 4, 2
XY, ZN = X * Y, H * L
TILE, F, SLOTS, EDGES = 128, 256, 4, 96
HALF = L * TILE
ROWS = C * HALF
E_ALL = XY * EDGES
STEP = 4 * EDGES
COPIES = 4
WR, BB = F // XY, 8
ZCHUNK = TILE + WR + BB
XCHUNK = TILE + WR
F32, BF16, I32 = jnp.float32, jnp.bfloat16, jnp.int32
K0, K1 = math.sqrt(2.0 / math.pi), 0.044715
ALL = ("x", "y", "h", "l", "c")
PARAMS = pltpu.CompilerParams(vmem_limit_bytes=40 * 1024 * 1024)


def dot(a, b):
    return jnp.dot(a, b, preferred_element_type=F32)


def one_hot(index, shape, axis, base=0):
    return (index == lax.broadcasted_iota(I32, shape, axis) + base).astype(F32).astype(BF16)


def split_rows(row):
    high = row.astype(BF16).astype(F32)
    at = lax.broadcasted_iota(I32, (BB, F), 0)
    return jnp.where(at == 0, high, jnp.where(at == 1, row - high, 0.0)).astype(BF16)


def column(row):
    return jnp.transpose(jnp.broadcast_to(row, (TILE, TILE)))[:, :1]


def spread_kernel(x_ref, s_ref, out_ref, x, s, scaled, sems):
    loads = [
        pltpu.make_async_copy(x_ref, x, sems.at[0]),
        pltpu.make_async_copy(s_ref, s, sems.at[1]),
    ]
    for load in loads:
        load.start()
    for load in loads:
        load.wait()
    value = (column(s[...]) * x[...].astype(F32)).astype(BF16)
    for j in range(COPIES):
        scaled[j] = value
    stores = [
        pltpu.make_async_copy(scaled, out_ref.at[pl.ds(j * COPIES, COPIES)], sems.at[2 + j])
        for j in range(XY // COPIES)
    ]
    for store in stores:
        store.start()
    for store in stores:
        store.wait()


def spread(features, node_scale):
    return pl.pallas_call(
        spread_kernel,
        out_shape=jax.ShapeDtypeStruct((XY, TILE, F), BF16),
        in_specs=[pl.BlockSpec(memory_space=pltpu.HBM)] * 2,
        out_specs=pl.BlockSpec(memory_space=pltpu.HBM),
        scratch_shapes=[
            pltpu.VMEM((TILE, F), BF16),
            pltpu.VMEM((1, TILE), F32),
            pltpu.VMEM((COPIES, TILE, F), BF16),
            pltpu.SemaphoreType.DMA((2 + XY // COPIES,)),
        ],
        compiler_params=pltpu.CompilerParams(vmem_limit_bytes=63_480_000),
    )(features, node_scale)


def forward_send_kernel(x_ref, lane_ref, sub_ref, gathered_ref, send_ref):
    for j in range(XY):
        rows = pl.ds(j * EDGES, EDGES)
        picks = [
            one_hot(sub_ref[rows, H + b : H + b + 1], (EDGES, TILE), 1) for b in range(H)
        ]
        value = dot(jnp.concatenate(picks), x_ref[j]).astype(BF16)
        for b in range(H):
            gathered_ref[b, rows, :] = value[b * EDGES : (b + 1) * EDGES]
    for b in range(H):
        place = one_hot(lane_ref[b : b + 1, :], (HALF, E_ALL), 0, HALF)
        send_ref[b] = dot(place, gathered_ref[b]).astype(BF16)


def forward_keep_kernel(gathered_ref, lane_ref, mine_ref):
    for b in range(H):
        place = one_hot(lane_ref[b : b + 1, :], (HALF, E_ALL), 0)
        mine_ref[b] = dot(place, gathered_ref[b])


def add_kernel(mine_ref, other_ref, out_ref):
    for b in range(H):
        for k in range(L):
            rows = pl.ds(k * TILE, TILE)
            total = mine_ref[b, rows, :] + other_ref[b, rows, :].astype(F32)
            out_ref[k * H + b] = total.astype(BF16)


def middle_kernel(part_ref, x_ref, s_ref, w_ref, bias_ref, ct_ref, out_ref, g_ref, wp_ref):
    s = column(s_ref[...])
    z = s * x_ref[...].astype(F32)
    for k in range(ZN):
        z += part_ref[k].astype(F32)
    z_high = z.astype(BF16)
    z_low = (z - z_high.astype(F32)).astype(BF16)
    w = w_ref[...]
    p = s * (dot(z_high, w) + dot(z_low, w)) + bias_ref[...]
    square = p * p
    th = jnp.tanh(K0 * (p + K1 * (p * square)))
    out_ref[...] = (0.5 * p * (1.0 + th)).astype(BF16)
    slope = 0.5 * (1.0 + th) + 0.5 * p * (1.0 - th * th) * (K0 * (1.0 + 3.0 * K1 * square))
    grad = ct_ref[...].astype(F32) * slope
    g = (s * grad).astype(BF16)
    g_ref[...] = g
    first = (((0,), (0,)), ((), ()))
    wg = lax.dot_general(z_high, g, first, preferred_element_type=F32)
    wg += lax.dot_general(z_low, g, first, preferred_element_type=F32)
    bias_rows = split_rows(jnp.sum(grad, axis=0, keepdims=True))
    for k in range(XY):
        wp_ref[k, pl.ds(0, WR), :] = wg[k * WR : (k + 1) * WR].astype(BF16)
        wp_ref[k, pl.ds(WR, BB), :] = bias_rows


def load_kernel(w_ref, g_ref, pay_ref):
    tail = jnp.zeros((WR + BB, F), F32)
    for k in range(XY):
        tail += w_ref[k].astype(F32)
    own = tail[:WR].astype(BF16)
    bias_rows = split_rows(jnp.sum(tail[WR:], axis=0, keepdims=True))
    g = g_ref[...]
    for k in range(ZN):
        pay_ref[k, pl.ds(0, TILE), :] = g
        pay_ref[k, pl.ds(TILE, WR), :] = own
        pay_ref[k, pl.ds(TILE + WR, BB), :] = bias_rows


def backward_mine_kernel(mine_ref, sub_ref, act_ref, picked_ref, out_ref, grads):
    out_ref[...] = act_ref[...]
    for b in range(H):
        for k in range(L):
            grads[pl.ds(k * TILE, TILE), :] = mine_ref[k * H + b, pl.ds(0, TILE), :]
        for m in range(E_ALL // STEP):
            pick = one_hot(sub_ref[pl.ds(m * STEP, STEP), b : b + 1], (STEP, HALF), 1)
            value = dot(pick, grads[...]).astype(BF16)
            for q in range(STEP // EDGES):
                picked_ref[m * (STEP // EDGES) + q, pl.ds(b * EDGES, EDGES), :] = value[
                    q * EDGES : (q + 1) * EDGES
                ]


def backward_kernel(
    picked_ref, mine_ref, other_ref, sub_ref, col_ref, pay_ref, bias_ref, grads, picked
):
    factor = 1.0 / math.sqrt(XY * ZN * C * TILE)
    tail_mine = jnp.zeros((WR + BB, F), F32)
    tail_other = jnp.zeros((WR + BB, F), F32)
    for k in range(ZN):
        rows = pl.ds(TILE, WR + BB)
        tail_mine += mine_ref[k, rows, :].astype(F32)
        tail_other += other_ref[k, rows, :].astype(F32)
    tail = (tail_mine + tail_other) * factor
    own = tail[:WR].astype(BF16)
    bias_ref[...] = jnp.sum(tail[WR:], axis=0, keepdims=True)
    for b in range(H):
        for k in range(L):
            grads[pl.ds(k * TILE, TILE), :] = other_ref[k * H + b, pl.ds(0, TILE), :]
        for m in range(E_ALL // STEP):
            pick = one_hot(sub_ref[pl.ds(m * STEP, STEP), b : b + 1], (STEP, HALF), 1, HALF)
            value = dot(pick, grads[...])
            for q in range(STEP // EDGES):
                j, rows = m * (STEP // EDGES) + q, pl.ds(b * EDGES, EDGES)
                both = value[q * EDGES : (q + 1) * EDGES] + picked_ref[j, rows, :].astype(F32)
                picked[j, rows, :] = both.astype(BF16)
    for j in range(XY):
        place = one_hot(col_ref[j : j + 1, :], (TILE, H * EDGES), 0)
        total = dot(place, picked[j])
        pay_ref[j, pl.ds(0, TILE), :] = total.astype(BF16)
        pay_ref[j, pl.ds(TILE, WR), :] = own


def final_kernel(part_ref, g_ref, s_ref, w_ref, bias_ref, fg_ref, wg_ref, out_ref):
    out_ref[...] = bias_ref[...]
    back = g_ref[...].astype(F32)
    for k in range(XY):
        back += part_ref[k, pl.ds(0, TILE), :].astype(F32)
        wg_ref[pl.ds(k * WR, WR), :] = part_ref[k, pl.ds(TILE, WR), :].astype(F32)
    grad_xw = (column(s_ref[...]) * back).astype(BF16)
    fg_ref[...] = lax.dot_general(
        grad_xw, w_ref[...], (((1,), (1,)), ((), ())), preferred_element_type=F32
    ).astype(BF16)


def call(kernel, outs, scratch=(), flops=TILE * F * F):
    return pl.pallas_call(
        kernel,
        out_shape=[jax.ShapeDtypeStruct(shape, dtype) for shape, dtype in outs],
        out_specs=[pl.BlockSpec(memory_space=pltpu.VMEM)] * len(outs),
        scratch_shapes=[pltpu.VMEM(shape, dtype) for shape, dtype in scratch],
        compiler_params=PARAMS,
        cost_estimate=pl.CostEstimate(
            flops=flops, bytes_accessed=2 * 1024 * 1024, transcendentals=0
        ),
    )


def exchange(array, axes):
    return lax.all_to_all(array, axes, 0, 0, tiled=True)


def swap(array, axis):
    return lax.ppermute(array, axis, [(0, 1), (1, 0)])


def per_device(
    features, weight, bias, node_scale, cotangent, edge_slot, edge_row, edge_col, tile_row
):
    h, c = lax.axis_index("h"), lax.axis_index("c")
    s = node_scale[None, :]
    bias = bias[None, :]

    slot = edge_slot.reshape(XY * H, EDGES)
    tiles = tile_row.reshape(XY * H, SLOTS)
    tile = sum(jnp.where(slot == k, tiles[:, k : k + 1], 0) for k in range(SLOTS))
    target = ((tile & 1) ^ c) * HALF + (tile >> 1) * TILE + edge_row.reshape(slot.shape)
    target = jnp.where(slot < SLOTS, target, -1)
    edges = jnp.stack([target, edge_col.reshape(slot.shape)]).reshape(2, X, Y, H, EDGES)
    edges = edges.transpose(0, 2, 1, 3, 4).reshape(2, XY, H, EDGES)
    kept = lax.dynamic_index_in_dim(edges, h, 2, keepdims=False)
    came = swap(lax.dynamic_index_in_dim(edges, 1 - h, 2, keepdims=False), "h")

    sources = exchange(spread(features, s), ("y", "x"))

    pairs = jnp.stack([jnp.where(h == 0, kept, came), jnp.where(h == 0, came, kept)], axis=1)
    lane = pairs.reshape(2 * H, E_ALL)
    sub = lane.T
    columns = jnp.concatenate([pairs[1, 0], pairs[1, 1]], axis=1)

    gathered, send = call(
        forward_send_kernel,
        [((H, E_ALL, F), BF16), ((H, HALF, F), BF16)],
        flops=4 * E_ALL * F * (HALF + TILE),
    )(sources, lane, sub)
    other = swap(send, "c")
    (mine,) = call(
        forward_keep_kernel, [((H, HALF, F), F32)], flops=4 * E_ALL * F * HALF
    )(gathered, lane)
    (partial,) = call(add_kernel, [((ZN, TILE, F), BF16)])(mine, other)
    partial = exchange(partial, ("l", "h"))
    act, g, w_parts = call(
        middle_kernel,
        [((TILE, F), BF16), ((TILE, F), BF16), ((XY, WR + BB, F), BF16)],
    )(partial, features, s, weight, bias, cotangent)
    w_parts = exchange(w_parts, ("y", "x"))
    (pay,) = call(load_kernel, [((ZN, ZCHUNK, F), BF16)])(w_parts, g)
    around = exchange(pay, ("l", "h"))
    other = swap(around, "c")
    picked, output = call(
        backward_mine_kernel,
        [((XY, H * EDGES, F), BF16), ((TILE, F), BF16)],
        [((HALF, F), BF16)],
        flops=4 * E_ALL * F * HALF,
    )(around, sub, act)
    terms, bias_sum = call(
        backward_kernel,
        [((XY, XCHUNK, F), BF16), ((1, F), F32)],
        [((HALF, F), BF16), ((XY, H * EDGES, F), BF16)],
        flops=4 * E_ALL * F * (HALF + TILE),
    )(picked, around, other, sub, columns)
    terms = exchange(terms, ("y", "x"))
    feature_grad, weight_grad, bias_grad = call(
        final_kernel, [((TILE, F), BF16), ((F, F), F32), ((1, F), F32)]
    )(terms, g, s, weight, bias_sum)
    return output, feature_grad, weight_grad, bias_grad.reshape(F)


def solution(mesh):
    fine = Mesh(mesh.devices.reshape(X, Y, H, L, C), ALL)
    rows, edges = P(ALL, None), P(("x", "y", "h"), ("l", "c"), None, None)
    return jax.shard_map(
        per_device,
        mesh=fine,
        in_specs=(rows, P(), P(), P(ALL), rows, edges, edges, edges, edges),
        out_specs=(rows, rows, P(), P()),
        check_vma=False,
    )
```
